32 devices in a mesh: row: 8 (over y, x, core), col: 4 (over z).
Axes of the slice: x: 2, y: 2, z: 4, core: 2. Of those that a mesh axis runs over, the one named last changes fastest.
Arguments:
- image_in: bfloat16 [8, 1572864], P('row', 'col'), may hold values from -6 to 6
- text_in: bfloat16 [8, 236544], P('row', 'col'), may hold values from -6 to 6
- condition: bfloat16 [8, 1536], P('row'), may hold values from -6 to 6
- mod_image: bfloat16 [1536, 18432], P('row', 'col'), may hold values from -0.15625 to 0.15625
- mod_text: bfloat16 [1536, 18432], P('row', 'col'), may hold values from -0.15625 to 0.15625
- qkv_image: bfloat16 [1536, 9216], P('row', 'col'), may hold values from -0.15625 to 0.15625
- qkv_text: bfloat16 [1536, 9216], P('row', 'col'), may hold values from -0.15625 to 0.15625
- out_image: bfloat16 [1536, 3072], P('row', 'col'), may hold values from -1.75 to 1.75
- out_text: bfloat16 [1536, 3072], P('row', 'col'), may hold values from -1.75 to 1.75
- up_image: bfloat16 [2, 1536, 6144], P(None, 'row', 'col'), may hold values from -0.15625 to 0.15625
- up_text: bfloat16 [2, 1536, 6144], P(None, 'row', 'col'), may hold values from -0.15625 to 0.15625
- down_image: bfloat16 [2, 1536, 6144], P(None, 'row', 'col'), may hold values from -0.078125 to 0.078125
- down_text: bfloat16 [2, 1536, 6144], P(None, 'row', 'col'), may hold values from -0.078125 to 0.078125
- cot_image: bfloat16 [8, 1572864], P('row', 'col'), may hold values from -6 to 6
- cot_text: bfloat16 [8, 236544], P('row', 'col'), may hold values from -6 to 6
Outputs:
- image_out: bfloat16 [8, 1572864], P('row', 'col')
- text_out: bfloat16 [8, 236544], P('row', 'col')
- grad_image: float32 [8, 1572864], P('row', 'col')
- grad_text: float32 [8, 236544], P('row', 'col')
- grad_cond: float32 [8, 1536], P('row')
- grad_mod_image: float32 [1536, 18432], P('row', 'col')
- grad_mod_text: float32 [1536, 18432], P('row', 'col')
- grad_qkv_image: float32 [1536, 9216], P('row', 'col')
- grad_qkv_text: float32 [1536, 9216], P('row', 'col')
- grad_out_image: float32 [1536, 3072], P('row', 'col')
- grad_out_text: float32 [1536, 3072], P('row', 'col')
- grad_up_image: float32 [2, 1536, 6144], P(None, 'row', 'col')
- grad_up_text: float32 [2, 1536, 6144], P(None, 'row', 'col')
- grad_down_image: float32 [2, 1536, 6144], P(None, 'row', 'col')
- grad_down_text: float32 [2, 1536, 6144], P(None, 'row', 'col')
The draws below stay inside these ranges and needn't reach their ends.
All inputs are finite; a program needn't handle non-finite values.
Results may differ from the reference program's by a relative error of at most 0.022.
Values may be sent and summed in bfloat16 or wider, within the bound.
No kernel may reach another device: no remote copies, remote signals or barrier semaphores. Data moves between devices by JAX's collectives and lax.ppermute only.
A program may use at most 384 MiB of HBM per device.

```python
import jax
import jax.numpy as jnp
from jax import lax

D = 1536
HEAD = 64
FF = 6144
IMG_LEN = 1024
TXT_LEN = 154
LAYERS = 2
SEQS = 8


def draw_condition(key, part):
    key = jax.random.fold_in(key, 11)
    values = jnp.clip(jax.random.normal(key, (SEQS, D), jnp.float32), -6.0, 6.0)
    return values.astype(jnp.bfloat16)


def shard_levels(rng, dims, cuts, least, top_value):
    factor_of = 1.0
    for dim, shards_of in cuts:
        heights = jax.random.uniform(jax.random.fold_in(jax.random.fold_in(rng, 6), dim), (shards_of,), jnp.float32, least / len(cuts), top_value / len(cuts))
        factor_of = factor_of * jnp.repeat(jnp.exp(heights), dims[dim] // shards_of).reshape((-1,) + (1,) * (len(dims) - 1 - dim))
    return factor_of


def normal_values(rng, extent, scale, most, shards=(), dtype=jnp.bfloat16):
    entries = jax.random.normal(rng, extent, jnp.float32) * scale
    if len(shards) > 0:
        entries = shard_levels(rng, extent, shards, -0.22, 0.18) * entries
    return jnp.clip(entries, min=-most, max=most).astype(dtype)


def setup_inputs(seed: int = 0) -> dict:
    arg_keys = jax.random.split(jax.random.key(seed), 16)
    image_in = normal_values(arg_keys[0], (SEQS, D * IMG_LEN), 1.0, 6.0, ((0, 8), (1, 4)))
    text_in = normal_values(arg_keys[1], (SEQS, D * TXT_LEN), 1.0, 6.0, ((0, 8), (1, 4)))
    condition = draw_condition(jax.random.fold_in(arg_keys[15], 71), 0)
    mod_image = normal_values(arg_keys[3], (D, D * LAYERS * 6), D ** -0.5, 0.15625, ((0, 8), (1, 4)))
    mod_text = normal_values(arg_keys[4], (D, D * LAYERS * 6), D ** -0.5, 0.15625, ((0, 8), (1, 4)))
    qkv_image = normal_values(arg_keys[5], (D, D * LAYERS * 3), D ** -0.5, 0.15625, ((0, 8), (1, 4)))
    qkv_text = normal_values(arg_keys[6], (D, D * LAYERS * 3), D ** -0.5, 0.15625, ((0, 8), (1, 4)))
    out_image = normal_values(arg_keys[7], (D, D * LAYERS), (max(D // 128, 4)) ** -0.5, 1.75, ((0, 8), (1, 4)))
    out_text = normal_values(arg_keys[8], (D, D * LAYERS), (max(D // 128, 4)) ** -0.5, 1.75, ((0, 8), (1, 4)))
    up_image = normal_values(arg_keys[9], (LAYERS, D, FF), D ** -0.5, 0.15625, ((1, 8), (2, 4)))
    up_text = normal_values(arg_keys[10], (LAYERS, D, FF), D ** -0.5, 0.15625, ((1, 8), (2, 4)))
    down_image = normal_values(arg_keys[11], (LAYERS, D, FF), FF ** -0.5, 0.078125, ((1, 8), (2, 4)))
    down_text = normal_values(arg_keys[12], (LAYERS, D, FF), FF ** -0.5, 0.078125, ((1, 8), (2, 4)))
    cot_image = normal_values(arg_keys[13], (SEQS, D * IMG_LEN), 1.0, 6.0, ((0, 8), (1, 4)))
    cot_text = normal_values(arg_keys[14], (SEQS, D * TXT_LEN), 1.0, 6.0, ((0, 8), (1, 4)))
    return dict(image_in=image_in, text_in=text_in, condition=condition, mod_image=mod_image, mod_text=mod_text, qkv_image=qkv_image, qkv_text=qkv_text, out_image=out_image, out_text=out_text, up_image=up_image, up_text=up_text, down_image=down_image, down_text=down_text, cot_image=cot_image, cot_text=cot_text)


EPS = 1e-06
EXACT_PRECISION = lax.Precision.HIGHEST

@jax.custom_vjp
def reduced_precision(v):
    return lax.optimization_barrier(v.astype(jnp.bfloat16)).astype(jnp.float32)

@jax.custom_vjp
def reduced_precision_reverse(v):
    return v

def low_keep(v):
    return (reduced_precision(v), None)

def low_pass(kept, grad):
    return (grad,)

def back_keep(v):
    return (v, None)

def back_low(kept, grad):
    return (reduced_precision(grad),)
reduced_precision.defvjp(low_keep, low_pass)
reduced_precision_reverse.defvjp(back_keep, back_low)

def layer_norm(stream):
    average = lax.optimization_barrier(jnp.mean(stream, axis=-1, keepdims=True))
    variance = lax.optimization_barrier(jnp.mean(jnp.square(stream - average), axis=-1, keepdims=True))
    return (stream - average) * lax.rsqrt(variance + EPS)

def attend_sequence(packed):
    queries, key_rows, values = packed
    scores = reduced_precision_reverse(jnp.einsum('qhe,khe->hqk', queries, key_rows, precision=EXACT_PRECISION) * HEAD ** (-0.5))
    chances = reduced_precision(jax.nn.softmax(scores, axis=-1))
    return reduced_precision(reduced_precision_reverse(jnp.einsum('hqk,khe->qhe', chances, values, precision=EXACT_PRECISION)))

def mmdit_layer(token_streams, cond_low, layer_weight_set):
    modulation_vectors = [reduced_precision_reverse(jnp.einsum('sd,kdc->skc', cond_low, layer_weight_set[selected_stream], precision=EXACT_PRECISION)) for selected_stream in range(2)]
    first_stream_input = [reduced_precision(layer_norm(token_streams[selected_stream]) * (1.0 + modulation_vectors[selected_stream][:, 1:2]) + modulation_vectors[selected_stream][:, 0:1]) for selected_stream in range(2)]
    query_key_value = [reduced_precision(reduced_precision_reverse(jnp.einsum('uqa,aot->uqot', first_stream_input[selected_stream], layer_weight_set[2 + selected_stream], precision=EXACT_PRECISION))) for selected_stream in range(2)]
    joint = jnp.concatenate(query_key_value, axis=1)
    seqs = joint.shape[0]
    length = joint.shape[1]
    split = joint.reshape(seqs, length, 3, D // HEAD, HEAD)
    heads = lax.map(jax.checkpoint(attend_sequence), (split[:, :, 0], split[:, :, 1], split[:, :, 2]))
    heads = heads.reshape(seqs, length, D)
    image_len = token_streams[0].shape[1]
    weight_pieces = [heads[:, :image_len], heads[:, image_len:]]
    middle_results = [token_streams[selected_stream] + modulation_vectors[selected_stream][:, 2:3] * reduced_precision_reverse(jnp.einsum('qer,rz->qez', weight_pieces[selected_stream], layer_weight_set[4 + selected_stream], precision=EXACT_PRECISION)) for selected_stream in range(2)]
    second_stream_input = [reduced_precision(layer_norm(middle_results[selected_stream]) * (1.0 + modulation_vectors[selected_stream][:, 4:5]) + modulation_vectors[selected_stream][:, 3:4]) for selected_stream in range(2)]
    hidden_features = [reduced_precision(jax.nn.gelu(reduced_precision_reverse(jnp.einsum('aqz,zh->aqh', second_stream_input[selected_stream], layer_weight_set[6 + selected_stream], precision=EXACT_PRECISION)), approximate=True)) for selected_stream in range(2)]
    return [middle_results[selected_stream] + modulation_vectors[selected_stream][:, 5:6] * reduced_precision_reverse(jnp.einsum('ium,mr->iur', hidden_features[selected_stream], layer_weight_set[8 + selected_stream], precision=EXACT_PRECISION)) for selected_stream in range(2)]

def mods_order(weight):
    return jnp.transpose(weight.reshape(D, D, LAYERS, 6), (2, 3, 0, 1))

def qkv_order(weight):
    return jnp.transpose(weight.reshape(D, D, LAYERS, 3), (2, 0, 3, 1))

def out_order(weight):
    return jnp.transpose(weight.reshape(D, D, LAYERS), (2, 1, 0))

def down_order(weight):
    return jnp.transpose(weight, (0, 2, 1))

def forward(image_x, text_x, condition, layer_weight_set):
    standard = [mods_order(layer_weight_set[0]), mods_order(layer_weight_set[1]), qkv_order(layer_weight_set[2]), qkv_order(layer_weight_set[3]), out_order(layer_weight_set[4]), out_order(layer_weight_set[5]), layer_weight_set[6], layer_weight_set[7], down_order(layer_weight_set[8]), down_order(layer_weight_set[9])]
    cond_low = reduced_precision(jax.nn.silu(condition))
    seqs = condition.shape[0]
    token_streams = [jnp.transpose(image_x.reshape(seqs, D, IMG_LEN), (0, 2, 1)), jnp.transpose(text_x.reshape(seqs, D, TXT_LEN), (0, 2, 1))]
    for depth in range(LAYERS):
        token_streams = mmdit_layer(token_streams, cond_low, [weight[depth] for weight in standard])
    return (jnp.transpose(token_streams[0], (0, 2, 1)).reshape(seqs, -1), jnp.transpose(token_streams[1], (0, 2, 1)).reshape(seqs, -1))

def reference(image_in, text_in, condition, mod_image, mod_text, qkv_image, qkv_text, out_image, out_text, up_image, up_text, down_image, down_text, cot_image, cot_text):
    layer_weight_set = tuple((weight.astype(jnp.float32) for weight in (mod_image, mod_text, qkv_image, qkv_text, out_image, out_text, up_image, up_text, down_image, down_text)))
    outputs, pullback = jax.vjp(forward, image_in.astype(jnp.float32), text_in.astype(jnp.float32), condition.astype(jnp.float32), layer_weight_set)
    grad_img, grad_txt, grad_cnd, grad_weights = pullback((cot_image.astype(jnp.float32), cot_text.astype(jnp.float32)))
    return (outputs[0].astype(jnp.bfloat16), outputs[1].astype(jnp.bfloat16), grad_img, grad_txt, grad_cnd, grad_weights[0], grad_weights[1], grad_weights[2], grad_weights[3], grad_weights[4], grad_weights[5], grad_weights[6], grad_weights[7], grad_weights[8], grad_weights[9])
```

```python
import functools
import math

import jax
import jax.numpy as jnp
from jax import lax
from jax.experimental import pallas as pl
from jax.experimental.pallas import tpu as pltpu
from jax.sharding import PartitionSpec as P

D = 1536
HEAD = 64
IMG_LEN = 1024
TXT_LEN = 154
LAYERS = 2
EPS = 1e-06
CHUNKS = 1
F32 = jnp.float32
BF16 = jnp.bfloat16


def dot(a, b, ca, cb):
    return lax.dot_general(a, b, (((ca,), (cb,)), ((), ())), preferred_element_type=F32)


def nn(a, b):
    return dot(a, b, 1, 0)


def nt(a, b):
    return dot(a, b, 1, 1)


def tn(a, b):
    return dot(a, b, 0, 0)


class Plan:
    def __init__(self, rows, cols, swap):
        self.rows, self.cols, self.swap = rows, cols, swap
        half = cols // 2
        self.row, self.col = lax.axis_index("row"), lax.axis_index("col")
        self.a, self.x, self.k = self.row // 4, (self.row // 2) % 2, self.row % 2
        self.h, self.l = self.col // half, self.col % half
        self.member = self.x * half + self.l if swap else self.col

        def flat(a, x, k, h, l):
            return (a * 4 + x * 2 + k) * cols + h * half + l

        if swap:
            sides = [(a, k) for a in range(rows // 4) for k in range(2)]
            self.team = [
                [flat(a, x, k, h, l) for x in range(2) for l in range(half)] for a, k in sides for h in range(2)
            ]
            self.home = [(flat(a, x, k, 1 - x, l), flat(a, x, k, x, l)) for a, k in sides for x in range(2) for l in range(half)]
            self.across = [(r, r ^ 2) for r in range(rows)]
            self.levels = [(c, (c + half) % cols) for c in range(cols)]
            self.fetch = [[a * 4 + x * 2 + k for a, k in sides] for x in range(2)]

    def exchange(self, blocks):
        if self.swap:
            return lax.all_to_all(
                blocks, ("row", "col"), 0, 0, tiled=True, axis_index_groups=self.team
            )
        return lax.all_to_all(blocks, "col", 0, 0, tiled=True)


    def inner(self, natural):
        if not self.swap:
            return natural
        lead = natural.shape[:-1]
        cut = natural.reshape(lead + (self.rows // 4, 2, 2, D // self.rows))
        return jnp.swapaxes(cut, -3, -2).reshape(lead + (D,))

    natural = inner

    def pick(self, index, pair):
        return jnp.where(index == 0, pair[0], pair[1]), jnp.where(index == 0, pair[1], pair[0])

    def place(self, index, mine, other):
        return jnp.where(index == 0, mine, other), jnp.where(index == 0, other, mine)

    def swap_sides(self, pieces):
        mine = jnp.stack(pieces)
        if not self.swap:
            return mine
        wide = mine.shape[2] // 2
        mine, other = self.pick(self.x, [mine[:, :, :wide], mine[:, :, wide:]])
        return jnp.concatenate(self.place(self.x, mine, lax.ppermute(other, "row", self.across)), axis=1)

    def swap_levels(self, both, after=()):
        if not self.swap:
            return both
        h = tick(self.h, after) if len(after) else self.h
        return jnp.concatenate(self.place(h, both, lax.ppermute(both, "col", self.levels)), axis=2)

    def gather_weights(self, both):
        if not self.swap:
            return lax.all_gather(both, "row", axis=0)
        return lax.all_gather(both, "row", axis=0, axis_index_groups=self.fetch)

    def scatter_weights(self, whole):
        groups = self.fetch if self.swap else None
        return lax.psum_scatter(whole, "row", scatter_dimension=0, tiled=True, axis_index_groups=groups)[0]

    def sum_levels(self, both):
        if not self.swap:
            return both, both
        wide = both.shape[2] // 2
        mine, other = self.pick(self.h, [both[:, :, :wide], both[:, :, wide:]])
        return (mine.astype(F32) + lax.ppermute(other, "col", self.levels).astype(F32)).astype(BF16), other

    def join_sides(self, both):
        if not self.swap:
            return both
        rows = both.shape[1] // 2
        mine, other = self.pick(self.x, [both[:, :rows], both[:, rows:]])
        return jnp.concatenate(self.place(self.x, mine, lax.ppermute(other, "row", self.across)), axis=2)

    def rows_home(self, blocks):
        if not self.swap:
            return blocks
        moved = lax.ppermute(blocks, ("row", "col"), self.home)
        return jnp.stack(self.place(self.h, blocks, moved), axis=1)

    def rows_in(self, pair):
        got = self.exchange(pair)
        if not self.swap:
            return jnp.transpose(got, (1, 0, 2)).reshape(got.shape[1], D)
        got = got.reshape((2, self.cols // 2) + got.shape[1:])
        got = jnp.where(self.h == 0, got[0], got[1])
        return self.inner(jnp.transpose(got, (2, 1, 0, 3)).reshape(got.shape[2], D))

    def rows_out(self, own):
        tokens = own.shape[0]
        if not self.swap:
            return self.exchange(jnp.transpose(own.reshape(tokens, self.cols, -1), (1, 0, 2)))
        cut = self.natural(own).reshape(tokens, 2, self.cols // 2, D // self.cols)
        cut = jnp.transpose(cut, (2, 1, 0, 3))
        return self.exchange(jnp.concatenate([cut, cut], axis=0))

    def rows_back(self, got):
        if not self.swap:
            return got
        mine, other = self.pick(self.h, [got[:, 0], got[:, 1]])
        back = lax.ppermute(other, ("row", "col"), [(b, a) for a, b in self.home])
        return jnp.where(self.x == self.h, mine, back)

    def vectors_in(self, part):
        if not self.swap:
            mine = jnp.sum(lax.all_to_all(part, "row", 0, 0, tiled=True), axis=0, keepdims=True)
            return lax.all_to_all(jnp.broadcast_to(mine, (self.cols, mine.shape[1])), "col", 0, 0, tiled=True)
        cut = part.reshape(self.rows // 4, 1, 2, 2, -1)
        cut = jnp.broadcast_to(cut, (self.rows // 4, 2) + cut.shape[2:])
        sent = jnp.transpose(cut, (0, 1, 3, 2, 4)).reshape(self.rows, 2, -1)
        mine = jnp.sum(lax.all_to_all(sent, "row", 0, 0, tiled=True), axis=0)
        half = self.cols // 2
        sent = jnp.broadcast_to(mine[:, None], (2, half, mine.shape[1])).reshape(self.cols, -1)
        return lax.all_to_all(sent, "col", 0, 0, tiled=True)

    def vectors_out(self, part):
        got = lax.all_to_all(part, "col", 0, 0, tiled=True)
        if not self.swap:
            mine = jnp.sum(got, axis=0, keepdims=True)
            return lax.all_to_all(jnp.broadcast_to(mine, (self.rows, mine.shape[1])), "row", 0, 0, tiled=True)
        mine = jnp.sum(got.reshape(2, self.cols // 2, -1), axis=1)
        every = lax.all_to_all(jnp.broadcast_to(mine[None], (self.rows,) + mine.shape), "row", 0, 0, tiled=True)
        every = jnp.sum(every.reshape(self.rows // 4, 2, 2, 2, -1), axis=1)
        return jnp.transpose(every, (0, 2, 1, 3)).reshape(self.rows, -1)


def norm(x):
    average = jnp.mean(x, axis=1, keepdims=True)
    centred = x - average
    inverse = lax.rsqrt(jnp.mean(centred * centred, axis=1, keepdims=True) + EPS)
    return centred * inverse, inverse


def call(kernel, name, grid, ins, outs, flops=0, after=(), alias=None, scratch=(), transcendentals=0):
    args = [a for a, _, _ in ins]
    in_specs = [pl.BlockSpec(block, index) for _, block, index in ins]
    extra = list(after)
    aliases = {}
    if alias is not None:
        aliases = {len(args): 0}
        extra = [alias] + extra
    given = len(args)

    def body(*refs):
        kernel(*refs[:given], *refs[given + len(extra) :])

    moved = sum(a.size * a.dtype.itemsize for a in args)
    for shape, dtype, _, _ in outs:
        moved += math.prod(shape) * jnp.dtype(dtype).itemsize
    got = pl.pallas_call(
        body,
        grid=grid,
        in_specs=in_specs + [pl.BlockSpec(memory_space=pl.ANY)] * len(extra),
        out_specs=[pl.BlockSpec(block, index) for _, _, block, index in outs],
        out_shape=[jax.ShapeDtypeStruct(shape, dtype) for shape, dtype, _, _ in outs],
        scratch_shapes=list(scratch),
        input_output_aliases=aliases,
        compiler_params=pltpu.CompilerParams(vmem_limit_bytes=58 << 20),
        cost_estimate=pl.CostEstimate(
            flops=flops, bytes_accessed=moved, transcendentals=transcendentals
        ),
        name=name,
    )(*args, *extra)
    return got[0] if len(got) == 1 else got


def tick(index, after):
    def kernel(given, out):
        out[...] = given[...]

    one = jnp.full((8, 128), index, jnp.int32)
    whole = ((8, 128), lambda i: (0, 0))
    return call(kernel, "tick", (1,), [(one,) + whole], [((8, 128), jnp.int32) + whole], after=after)[0, 0]


def gate(array, after):
    def kernel(*refs):
        pass

    return pl.pallas_call(
        kernel,
        in_specs=[pl.BlockSpec(memory_space=pl.ANY)] * (1 + len(after)),
        out_specs=pl.BlockSpec(memory_space=pl.ANY),
        out_shape=jax.ShapeDtypeStruct(array.shape, array.dtype),
        input_output_aliases={0: 0},
        cost_estimate=pl.CostEstimate(flops=0, bytes_accessed=1024, transcendentals=0),
        name="gate",
    )(array, *after)


class Kernels:
    def __init__(self, members, ci, ct, chunks, groups, wide, hidden):
        self.q, self.ci, self.ct, self.rc, self.n = members, ci, ct, ci + ct, chunks
        self.g, self.dr = groups, D // groups
        self.wide, self.hidden = wide, hidden
        self.tokens = members * self.rc * chunks

    def sides(self, array, columns, index, lead=None):
        q, ratio = self.q, self.ci // self.ct
        if lead is None:
            return [
                (array, (q, self.ci, columns), lambda *i: (0, 0, index(*i))),
                (array, (q, self.ct, columns), lambda *i: (0, ratio, index(*i))),
            ]
        return [
            (array, (1,) * len(lead(0)) + (q, self.ci, columns), lambda *i: lead(*i) + (0, 0, index(*i))),
            (array, (1,) * len(lead(0)) + (q, self.ct, columns), lambda *i: lead(*i) + (0, ratio, index(*i))),
        ]

    def weight(self, array, columns, piece, index):
        return [
            (array, (self.g, 1, self.dr, columns), lambda *i, s=s: (0, piece(*i) + s, 0, index(*i))) for s in range(2)
        ]

    def flat(self, ref):
        value = ref[...]
        return value.reshape(-1, value.shape[-1])

    def put(self, ref, img, txt):
        cut = ref.shape[:-2]
        ref[..., : self.ci, :] = img.astype(ref.dtype).reshape(cut + (self.ci, ref.shape[-1]))
        ref[..., self.ci :, :] = txt.astype(ref.dtype).reshape(cut + (self.ct, ref.shape[-1]))

    def qkv(self, h, weights, chunk, joint, after=()):
        def kernel(hi, ht, wi, wt, out):
            self.put(out, nn(self.flat(hi), self.flat(wi)), nn(self.flat(ht), self.flat(wt)))

        return call(
            kernel,
            "qkv",
            (3,),
            self.sides(h, D, lambda j: 0) + self.weight(weights, self.wide, lambda j: 2 * j, lambda j: 0),
            [
                (
                    (self.n, self.q, self.rc, 3 * self.wide),
                    BF16,
                    (1, self.q, self.rc, self.wide),
                    lambda j: (chunk, 0, 0, j),
                )
            ],
            flops=2 * self.q * self.rc * D * 3 * self.wide,
            alias=joint,
            after=after,
        )

    def project(self, heads, weights, piece, chunk, after=()):
        def kernel(hi, ht, wi, wt, out):
            self.put(out, nt(self.flat(hi), self.flat(wi)), nt(self.flat(ht), self.flat(wt)))

        return call(
            kernel,
            "project",
            (1,),
            self.sides(heads, self.wide, lambda i: 0, lambda i: (chunk,))
            + self.weight(weights, self.wide, lambda i: piece, lambda i: 0),
            [((self.q, self.rc, D), BF16, (self.q, self.rc, D), lambda i: (0, 0, 0))],
            flops=2 * self.q * self.rc * D * self.wide,
            after=after,
        )

    def project_back(self, grad, weights, piece, chunk, joint, after=()):
        def kernel(hi, ht, wi, wt, out):
            self.put(out, nn(self.flat(hi), self.flat(wi)), nn(self.flat(ht), self.flat(wt)))

        return call(
            kernel,
            "project_back",
            (1,),
            self.sides(grad, D, lambda i: 0) + self.weight(weights, self.wide, lambda i: piece, lambda i: 0),
            [
                (
                    (self.n, self.q, self.rc, self.wide),
                    BF16,
                    (1, self.q, self.rc, self.wide),
                    lambda i: (chunk, 0, 0, 0),
                )
            ],
            flops=2 * self.q * self.rc * D * self.wide,
            alias=joint,
            after=after,
        )

    def qkv_back(self, grads, weights, chunk, after=()):
        def kernel(hi, ht, wi, wt, out, sum_i, sum_t):
            j = pl.program_id(0)
            img, txt = nt(self.flat(hi), self.flat(wi)), nt(self.flat(ht), self.flat(wt))

            @pl.when(j == 0)
            def _():
                sum_i[...] = img
                sum_t[...] = txt

            @pl.when(j == 1)
            def _():
                sum_i[...] += img
                sum_t[...] += txt

            @pl.when(j == 2)
            def _():
                self.put(out, sum_i[...] + img, sum_t[...] + txt)

        return call(
            kernel,
            "qkv_back",
            (3,),
            self.sides(grads, self.wide, lambda j: 0, lambda j: (j, chunk))
            + self.weight(weights, self.wide, lambda j: 2 * j, lambda j: 0),
            [((self.q, self.rc, D), BF16, (self.q, self.rc, D), lambda j: (0, 0, 0))],
            flops=2 * self.q * self.rc * D * 3 * self.wide,
            after=after,
            scratch=[pltpu.VMEM((self.q * self.ci, D), F32), pltpu.VMEM((self.q * self.ct, D), F32)],
        )

    def mlp(self, h, ups, downs, after=()):
        steps = 3
        block = self.hidden // steps

        def gelu(v):
            inner = 0.7978845608028654 * (v + 0.044715 * v * v * v)
            t = jnp.tanh(inner)
            half = 0.5 * (1.0 + t)
            slope = half + 0.5 * v * (1.0 - t * t) * (0.7978845608028654 * (1.0 + 3 * 0.044715 * v * v))
            return (v * half).astype(BF16), slope.astype(BF16)

        def kernel(hi, ht, ui, ut, di, dt, act, slope, out, sum_i, sum_t):
            j = pl.program_id(0)
            gi, si = gelu(nn(self.flat(hi), self.flat(ui)))
            gt, st = gelu(nn(self.flat(ht), self.flat(ut)))
            self.put(act, gi, gt)
            self.put(slope, si, st)
            img, txt = nt(gi, self.flat(di)), nt(gt, self.flat(dt))

            @pl.when(j == 0)
            def _():
                sum_i[...] = img
                sum_t[...] = txt

            @pl.when(jnp.logical_and(j > 0, j < steps - 1))
            def _():
                sum_i[...] += img
                sum_t[...] += txt

            @pl.when(j == steps - 1)
            def _():
                self.put(out, sum_i[...] + img, sum_t[...] + txt)

        return call(
            kernel,
            "mlp",
            (steps,),
            self.sides(h, D, lambda j: 0)
            + self.weight(ups, block, lambda j: 0, lambda j: j)
            + self.weight(downs, block, lambda j: 0, lambda j: j),
            [
                ((self.q, self.rc, self.hidden), BF16, (self.q, self.rc, block), lambda j: (0, 0, j)),
                ((self.q, self.rc, self.hidden), BF16, (self.q, self.rc, block), lambda j: (0, 0, j)),
                ((self.q, self.rc, D), BF16, (self.q, self.rc, D), lambda j: (0, 0, 0)),
            ],
            flops=4 * self.q * self.rc * D * self.hidden,
            transcendentals=self.q * self.rc * self.hidden,
            after=after,
            scratch=[pltpu.VMEM((self.q * self.ci, D), F32), pltpu.VMEM((self.q * self.ct, D), F32)],
        )

    def mlp_back(self, grad, slope, ups, downs, after=()):
        steps = 3
        block = self.hidden // steps

        def kernel(hi, ht, si, st, ui, ut, di, dt, pre, out, sum_i, sum_t):
            j = pl.program_id(0)
            pi = (nn(self.flat(hi), self.flat(di)) * self.flat(si).astype(F32)).astype(BF16)
            pt = (nn(self.flat(ht), self.flat(dt)) * self.flat(st).astype(F32)).astype(BF16)
            self.put(pre, pi, pt)
            img, txt = nt(pi, self.flat(ui)), nt(pt, self.flat(ut))

            @pl.when(j == 0)
            def _():
                sum_i[...] = img
                sum_t[...] = txt

            @pl.when(jnp.logical_and(j > 0, j < steps - 1))
            def _():
                sum_i[...] += img
                sum_t[...] += txt

            @pl.when(j == steps - 1)
            def _():
                self.put(out, sum_i[...] + img, sum_t[...] + txt)

        return call(
            kernel,
            "mlp_back",
            (steps,),
            self.sides(grad, D, lambda j: 0)
            + self.sides(slope, block, lambda j: j)
            + self.weight(ups, block, lambda j: 0, lambda j: j)
            + self.weight(downs, block, lambda j: 0, lambda j: j),
            [
                ((self.q, self.rc, self.hidden), BF16, (self.q, self.rc, block), lambda j: (0, 0, j)),
                ((self.q, self.rc, D), BF16, (self.q, self.rc, D), lambda j: (0, 0, 0)),
            ],
            flops=4 * self.q * self.rc * D * self.hidden,
            after=after,
            scratch=[pltpu.VMEM((self.q * self.ci, D), F32), pltpu.VMEM((self.q * self.ct, D), F32)],
        )

    def weight_grad(self, name, left, right, kinds, pieces, first, whole, after=()):
        columns = right[0][0].shape[-1]

        def rows(refs, side):
            got = [self.flat(refs[2 * c + side]) for c in range(self.n)]
            return got[0] if len(got) == 1 else jnp.concatenate(got, axis=0)

        if self.dr % 128:
            cut = []
            for kind in range(kinds):
                for side in (slice(0, self.ci), slice(self.ci, self.rc)):
                    a = jnp.concatenate([one[:, side].reshape(-1, D) for one in left], axis=0)
                    b = [one[lead(kind)] if lead else one for one, lead in right]
                    b = jnp.concatenate([one[:, side].reshape(-1, columns) for one in b], axis=0)
                    cut.append(tn(a, b).astype(BF16).reshape(self.g, self.dr, columns))
            cut = jnp.stack(cut, axis=1)
            return cut if whole is None else jnp.concatenate([whole, cut], axis=1)

        def kernel(*refs):
            ins, out = refs[:-1], refs[-1]
            for side in range(2):
                a, b = rows(ins[: 2 * self.n], side), rows(ins[2 * self.n :], side)
                out[0, side] = tn(a, b).astype(BF16)

        ins = []
        for one in left:
            ins += self.sides(one, self.dr, lambda j, g: g)
        for one, lead in right:
            ins += self.sides(one, columns, lambda j, g: 0, (lambda j, g=0, lead=lead: lead(j)) if lead else None)
        return call(
            kernel,
            name,
            (kinds, self.g),
            ins,
            [
                (
                    (self.g, pieces, self.dr, columns),
                    BF16,
                    (1, 2, self.dr, columns),
                    lambda j, g: (g, first // 2 + j, 0, 0),
                )
            ],
            flops=2 * self.tokens * D * columns * kinds,
            alias=whole,
            after=after,
        )

    def norm_in(self, mods, x, blocks=None, gate=None, after_norm=None, after=()):
        rows = self.ct

        def kernel(*refs):
            refs = list(refs)
            value = refs.pop(0)[...]
            if blocks is not None:
                added = jnp.sum(refs.pop(0)[...].astype(F32), axis=0)
                value = value + refs.pop(0)[0, gate[1] : gate[1] + 1] * added
            vectors = refs.pop(0) if after_norm is not None else None
            if blocks is not None:
                refs.pop(0)[...] = value
                refs.pop(0)[...] = added
            if after_norm is not None:
                kind = after_norm[1]
                normed = norm(value)[0]
                out = (normed * (1.0 + vectors[0, kind + 1 : kind + 2]) + vectors[0, kind : kind + 1]).astype(BF16)
                refs[0][...] = jnp.broadcast_to(out[None], refs[0].shape)

        ratio = self.ci // self.ct

        def vectors(depth):
            return (mods, (1,) + mods.shape[1:], lambda i: (depth * 2 + i // ratio, 0, 0))

        flat = ((rows, D), lambda i: (i, 0))
        many = ((self.q, rows, D), lambda i: (0, i, 0))
        ins, outs = [(x,) + flat], []
        if blocks is not None:
            ins += [(blocks,) + many, vectors(gate[0])]
            outs += [((self.rc, D), F32) + flat] * 2
        if after_norm is not None:
            ins.append(vectors(after_norm[0]))
            outs.append(((self.q, self.rc, D), BF16) + many)
        return call(kernel, "norm_in", (ratio + 1,), ins, outs, flops=20 * self.rc * D, after=after)

    def norm_back(self, mods, grad, blocks=None, x=None, scale=None, branch=None, gate=None, after=()):
        rows = self.ct
        ratio = self.ci // self.ct

        def kernel(*refs):
            refs = list(refs)
            value = refs.pop(0)[...]
            i = pl.program_id(0)
            rows_of_sums = []
            if blocks is not None:
                dh = jnp.sum(refs.pop(0)[...].astype(F32), axis=0)
                normed, inverse = norm(refs.pop(0)[...])
                dn = dh * (1.0 + refs.pop(0)[0, scale[1] : scale[1] + 1])
                value = value + inverse * (
                    dn
                    - jnp.mean(dn, axis=1, keepdims=True)
                    - normed * jnp.mean(dn * normed, axis=1, keepdims=True)
                )
                rows_of_sums += [(0, jnp.sum(dh, axis=0, keepdims=True)), (1, jnp.sum(dh * normed, axis=0, keepdims=True))]
            if branch is not None:
                rows_of_sums.append((2, jnp.sum(value * refs.pop(0)[...], axis=0, keepdims=True)))
            if gate is not None:
                factor = refs.pop(0)[0, gate[1] : gate[1] + 1]
            if blocks is not None:
                refs.pop(0)[...] = value
            if gate is not None:
                out = refs.pop(0)
                out[...] = jnp.broadcast_to((factor * value).astype(BF16)[None], out.shape)
            if not rows_of_sums:
                return
            sums = refs.pop(0)
            start = jnp.logical_or(i == 0, i == ratio)

            @pl.when(start)
            def _():
                for at, row in rows_of_sums:
                    sums[0, at : at + 1] = row

            @pl.when(jnp.logical_not(start))
            def _():
                for at, row in rows_of_sums:
                    sums[0, at : at + 1] += row

        def vectors(depth):
            return (mods, (1,) + mods.shape[1:], lambda i: (depth * 2 + i // ratio, 0, 0))

        flat = ((rows, D), lambda i: (i, 0))
        many = ((self.q, rows, D), lambda i: (0, i, 0))
        ins, outs = [(grad,) + flat], []
        if blocks is not None:
            ins += [(blocks,) + many, (x,) + flat, vectors(scale[0])]
            outs.append(((self.rc, D), F32) + flat)
        if branch is not None:
            ins.append((branch,) + flat)
        if gate is not None:
            ins.append(vectors(gate[0]))
            outs.append(((self.q, self.rc, D), BF16) + many)
        if blocks is not None or branch is not None:
            outs.append(((2, 8, D), F32, (1, 8, D), lambda i: (i // ratio, 0, 0)))
        return call(kernel, "norm_back", (ratio + 1,), ins, outs, flops=30 * self.rc * D, after=after)

    def masks(self):
        at = lax.broadcasted_iota(jnp.int32, (self.n, self.q, self.rc), 2)
        chunk = lax.broadcasted_iota(jnp.int32, (self.n, self.q, self.rc), 0)
        member = lax.broadcasted_iota(jnp.int32, (self.n, self.q, self.rc), 1)
        text = member * (self.ct * self.n) + chunk * self.ct + at - self.ci
        absent = jnp.logical_and(at >= self.ci, text >= TXT_LEN)
        return jnp.where(absent, -1e30, 0.0).astype(BF16).reshape(self.tokens, 1)

    def attend(self, joint, mask, after=()):
        t, pairs = self.tokens, self.wide // 128

        def kernel(q_ref, k_ref, v_ref, mask_ref, o_ref):
            q, k, v = q_ref[...], k_ref[...], v_ref[...]
            lane = lax.broadcasted_iota(jnp.int32, q.shape, 1)
            first = lane < HEAD
            none = jnp.zeros_like(q)
            bias = jnp.broadcast_to(mask_ref[...], k.shape)
            outs = []
            for side, spare in ((True, HEAD), (False, 0)):
                ones = jnp.where(lane == spare, jnp.ones_like(q), none)
                scaled = jnp.where(first == side, q * jnp.asarray(HEAD**-0.5, BF16), ones)
                scores = nt(scaled, jnp.where(first == side, k, bias))
                weights = jnp.exp(scores - jnp.max(scores, axis=1, keepdims=True))
                totals = jnp.sum(weights, axis=1, keepdims=True)
                outs.append(nn(weights.astype(BF16), v) * (1.0 / totals))
            o_ref[...] = jnp.where(first, outs[0], outs[1]).astype(BF16)

        flat = joint.reshape(t, 3 * self.wide)
        out = call(
            kernel,
            "attend",
            (pairs,),
            [(flat, (t, 128), lambda p, part=part: (0, part * pairs + p)) for part in range(3)]
            + [(mask, (t, 1), lambda p: (0, 0))],
            [((t, self.wide), BF16, (t, 128), lambda p: (0, p))],
            flops=pairs * 8 * t * t * 128,
            transcendentals=pairs * 2 * t * t,
            after=after,
        )
        return out.reshape(self.n, self.q, self.rc, self.wide)

    def attend_back(self, joint, mask, grad, after=()):
        t, pairs = self.tokens, self.wide // 128

        def kernel(q_ref, k_ref, v_ref, mask_ref, do_ref, out_ref):
            q, k, v, do = q_ref[...], k_ref[...], v_ref[...], do_ref[...]
            lane = lax.broadcasted_iota(jnp.int32, q.shape, 1)
            first = lane < HEAD
            none = jnp.zeros_like(q)
            bias = jnp.broadcast_to(mask_ref[...], k.shape)
            scale = jnp.asarray(HEAD**-0.5, BF16)
            dq = dk = dv = None
            for side, spare in ((True, HEAD), (False, 0)):
                mine = first == side
                ones = jnp.where(lane == spare, jnp.ones_like(q), none)
                scaled = q * scale
                grad_o = jnp.where(mine, do, none)
                scores = nt(jnp.where(mine, k, bias), jnp.where(mine, scaled, ones))
                weights = jnp.exp(scores - jnp.max(scores, axis=0, keepdims=True))
                chances = weights * (1.0 / jnp.sum(weights, axis=0, keepdims=True))
                grad_chances = nt(v, grad_o)
                centre = jnp.sum(grad_chances * chances, axis=0, keepdims=True)
                grad_scores = (chances * (grad_chances - centre)).astype(BF16)
                one_v = nn(chances.astype(BF16), grad_o)
                one_k = nn(grad_scores, jnp.where(mine, scaled, none))
                one_q = tn(grad_scores, jnp.where(mine, k * scale, none))
                dq, dk, dv = (one_q, one_k, one_v) if dq is None else (dq + one_q, dk + one_k, dv + one_v)
            out_ref[0] = dq.astype(BF16)
            out_ref[1] = dk.astype(BF16)
            out_ref[2] = dv.astype(BF16)

        flat = joint.reshape(t, 3 * self.wide)
        out = call(
            kernel,
            "attend_back",
            (pairs,),
            [(flat, (t, 128), lambda p, part=part: (0, part * pairs + p)) for part in range(3)]
            + [(mask, (t, 1), lambda p: (0, 0)), (grad.reshape(t, self.wide), (t, 128), lambda p: (0, p))],
            [((3, t, self.wide), BF16, (3, t, 128), lambda p: (0, 0, p))],
            flops=pairs * 20 * t * t * 128,
            transcendentals=pairs * 2 * t * t,
            after=after,
        )
        return out.reshape(3, self.n, self.q, self.rc, self.wide)


def order_matrix(block, kinds):
    width = block * LAYERS * kinds
    source = lax.broadcasted_iota(jnp.int32, (width, width), 0)
    target = lax.broadcasted_iota(jnp.int32, (width, width), 1)
    return (source == (target % block) * (LAYERS * kinds) + target // block).astype(BF16)


def split_columns(weight, kinds):
    rows = weight.shape[0]
    features = weight.shape[1] // (LAYERS * kinds)
    block = 128 if features % 128 == 0 else 64
    wide = block * LAYERS * kinds
    matrix = order_matrix(block, kinds)
    parts = [nn(weight[:, i * wide : (i + 1) * wide], matrix).astype(BF16) for i in range(features // block)]

    def one(at):
        return jnp.concatenate([part[:, at * block : (at + 1) * block] for part in parts], axis=1)

    return [[one(depth * kinds + kind) for kind in range(kinds)] for depth in range(LAYERS)]


def merge_columns(pieces, kinds):
    features = pieces[0][0].shape[1]
    block = 128 if features % 128 == 0 else 64
    matrix = order_matrix(block, kinds)
    parts = []
    for i in range(features // block):
        sorted_ = jnp.concatenate(
            [piece[:, i * block : (i + 1) * block] for layer in pieces for piece in layer], axis=1
        )
        parts.append(nt(sorted_, matrix))
    return jnp.concatenate(parts, axis=1)


def sort_vectors(part, kinds):
    rows = part.shape[0]
    features = part.shape[1] // (LAYERS * kinds)
    block = 128 if features % 128 == 0 else 64
    wide = block * LAYERS * kinds
    terms, rest = [], part
    for _ in range(3):
        term = lax.reduce_precision(rest, 8, 7)
        terms.append(term.astype(BF16))
        rest = rest - term
    matrix = order_matrix(block, kinds)
    cuts = jnp.concatenate(terms, axis=0)
    out = []
    for i in range(features // block):
        got = nn(cuts[:, i * wide : (i + 1) * wide], matrix).reshape(3, rows, LAYERS * kinds, block)
        out.append(got[0] + got[1] + got[2])
    return jnp.concatenate(out, axis=2)


def unsort_vectors(sorted_, kinds):
    rows, _, features = sorted_.shape
    block = 128 if features % 128 == 0 else 64
    matrix = order_matrix(block, kinds)
    out = [
        nt(sorted_[:, :, i * block : (i + 1) * block].reshape(rows, -1), matrix).astype(BF16)
        for i in range(features // block)
    ]
    return jnp.concatenate(out, axis=1)


def on_device(
    rows_count,
    cols,
    image_in,
    text_in,
    condition,
    mod_image,
    mod_text,
    qkv_image,
    qkv_text,
    out_image,
    out_text,
    up_image,
    up_text,
    down_image,
    down_text,
    cot_image,
    cot_text,
):
    features = D // cols
    swap = cols % 2 == 0 and rows_count % 4 == 0 and features % (2 * HEAD) == 0
    plan = Plan(rows_count, cols, swap)
    width_rows = mod_image.shape[0]
    img_own = IMG_LEN // cols
    txt_own = img_own // 4
    txt_pad = txt_own * cols
    wide = features + -features % 128
    k = Kernels(
        cols,
        img_own // CHUNKS,
        txt_own // CHUNKS,
        CHUNKS,
        rows_count // 2 if swap else rows_count,
        wide,
        up_image.shape[2],
    )
    chunks = range(CHUNKS)

    def filled(whole):
        return jnp.pad(whole, ((0, 0),) * 3 + ((0, wide - features),))

    qkv_shards = [split_columns(w, 3) for w in (qkv_image, qkv_text)]
    out_shards = [split_columns(w, 1) for w in (out_image, out_text)]
    w_attn, w_up, w_down = [], [], []
    sides_attn = [
        plan.swap_sides(
            [qkv_shards[s][depth][kind] for kind in range(3) for s in range(2)]
            + [out_shards[s][depth][0] for s in range(2)]
        )
        for depth in range(LAYERS)
    ]
    sides_up = [plan.swap_sides([up_image[depth], up_text[depth]]) for depth in range(LAYERS)]
    sides_down = [plan.swap_sides([down_image[depth], down_text[depth]]) for depth in range(LAYERS)]

    cond_float = condition.astype(F32)
    cond_low = jax.nn.silu(cond_float).astype(BF16)
    cond_cut = cond_low.reshape(rows_count, width_rows)
    cond_mine = lax.all_to_all(cond_cut, "row", 0, 0, tiled=True)
    mod_part = [nn(cond_mine, one) for one in (mod_image, mod_text)]
    mod_sorted = jnp.concatenate([sort_vectors(one, 6) for one in mod_part], axis=1)
    mod_cols = plan.vectors_in(mod_sorted.reshape(rows_count, -1)).reshape(cols, 2, LAYERS, 6, features)
    mods = plan.inner(jnp.transpose(mod_cols, (2, 1, 3, 0, 4)).reshape(LAYERS * 2, 6, D))

    def to_blocks(image, text):
        img = jnp.transpose(image.reshape(features, IMG_LEN)).reshape(cols, CHUNKS, k.ci, features)
        txt = jnp.pad(jnp.transpose(text.reshape(features, TXT_LEN)), ((0, txt_pad - TXT_LEN), (0, 0)))
        blocks = jnp.concatenate([img, txt.reshape(cols, CHUNKS, k.ct, features)], axis=2)
        return blocks.reshape(cols, CHUNKS * k.rc, features)

    def to_own(pair):
        own = plan.rows_in(pair).astype(F32)
        return [own[c * k.rc : (c + 1) * k.rc] for c in chunks]

    def from_blocks(got):
        got = got.reshape(cols, CHUNKS, k.rc, features)
        img = got[:, :, : k.ci].reshape(IMG_LEN, features)
        txt = got[:, :, k.ci :].reshape(txt_pad, features)[:TXT_LEN]
        return jnp.transpose(img).reshape(1, -1), jnp.transpose(txt).reshape(1, -1)

    mask = k.masks()
    pair = plan.rows_home(to_blocks(image_in, text_in))
    level = plan.swap_levels(sides_attn[0], [pair, mods, sides_up[0], sides_down[0]])
    w_qkv, w_out = [filled(plan.gather_weights(level[:6]))], [(filled(plan.gather_weights(level[6:])), 0)]
    x = to_own(pair)
    h1 = [plan.exchange(k.norm_in(mods, x[c], after_norm=(0, 0))) for c in chunks]
    kept = []
    for depth in range(LAYERS):
        last = depth + 1 == LAYERS
        side = [plan.swap_levels(gate(sides_up[depth], h1 if depth else x), h1)]
        w_up.append(plan.gather_weights(side[0]))
        if last:
            side += grads
        joint = None
        for c in chunks:
            joint = k.qkv(h1[c], w_qkv[depth], c, joint, side)
        side = []
        if last:
            side = [k.norm_back(mods, grads[c], gate=(depth, 5)) for c in chunks]
            grad_down = [plan.exchange(one) for one in side]
        heads = k.attend(joint, mask, side)
        side = grad_down if last else []
        save = dict(x=x, h1=h1, joint=joint, heads=heads, branch=[], x1=[], h2=[], act=[], slope=[], down=[])
        next_x, next_h1 = [], []
        sent = [k.project(heads, *w_out[depth], c, side) for c in chunks]
        blocks = [plan.exchange(one) for one in sent]
        side = [plan.swap_levels(gate(sides_down[depth], sent), blocks)]
        w_down.append(plan.gather_weights(side[0]))
        if not last:
            cot = to_blocks(gate(cot_image, sent), cot_text)
            side.append(cot)
        for c in chunks:
            x1, branch, h2 = k.norm_in(mods, x[c], blocks[c], (depth, 2), (depth, 3), side)
            save["x1"].append(x1)
            save["branch"].append(branch)
            save["h2"].append(plan.exchange(h2))
        side = []
        if not last:
            side = [plan.swap_levels(gate(sides_attn[depth + 1], save["x1"]), save["h2"])]
            whole = filled(plan.gather_weights(side[0]))
            w_qkv.append(whole)
            w_out.append((whole, 6))
        parts = []
        for c in chunks:
            act, slope, part = k.mlp(save["h2"][c], w_up[depth], w_down[depth], side)
            parts.append(part)
            save["act"].append(act)
            save["slope"].append(slope)
        kept.append(save)
        if last:
            break
        blocks = [plan.exchange(part) for part in parts]
        pair = plan.rows_home(gate(cot, parts))
        side = [pair, sides_up[depth + 1], sides_down[depth + 1]]
        for c in chunks:
            got = k.norm_in(mods, save["x1"][c], blocks[c], (depth, 5), (depth + 1, 0), side)
            next_x.append(got[0])
            save["down"].append(got[1])
            next_h1.append(plan.exchange(got[2]))
        grads = to_own(pair)
        x, h1 = next_x, next_h1

    start = list(grads)
    mod_grads = [None] * LAYERS
    attn_grads, up_grads, down_grads = [None] * LAYERS, [None] * LAYERS, [None] * LAYERS
    for depth in reversed(range(LAYERS)):
        first = depth + 1 == LAYERS
        save = kept[depth]
        grad_pre, blocks, grad_out, sums2, sums1, next_down = ([] for _ in range(6))
        side = []
        if not first:
            up_grads[depth + 1] = plan.join_sides(up_sum)
            side = [up_grads[depth + 1]]
        down_whole = k.weight_grad("down_grad", grad_down, [(one, None) for one in save["act"]], 1, 2, 0, None, side)
        down_both = plan.scatter_weights(down_whole)
        for c in chunks:
            pre, part = k.mlp_back(grad_down[c], save["slope"][c], w_up[depth], w_down[depth], [down_whole])
            grad_pre.append(pre)
            blocks.append(plan.exchange(part))
        up_whole = k.weight_grad("up_grad", save["h2"], [(one, None) for one in grad_pre], 1, 2, 0, None)
        side = [up_whole]
        if not first:
            attn_sum, _ = plan.sum_levels(attn_both)
            side.append(attn_sum)
        for c in chunks:
            grads[c], got, sums = k.norm_back(
                mods, grads[c], blocks[c], save["x1"][c], (depth, 4), save["branch"][c], (depth, 2), side
            )
            sums2.append(sums)
            grad_out.append(plan.exchange(got))
        up_both = plan.scatter_weights(gate(up_whole, sums2))
        down_sum, _ = plan.sum_levels(down_both)
        side = [down_sum]
        if not first:
            attn_grads[depth + 1] = plan.join_sides(attn_sum)
            side.append(attn_grads[depth + 1])
        grad_heads = None
        for c in chunks:
            grad_heads = k.project_back(grad_out[c], *w_out[depth], c, grad_heads, side)
        grad_qkv = k.attend_back(save["joint"], mask, grad_heads)
        up_sum, _ = plan.sum_levels(up_both)
        side = [up_sum]
        if first:
            last_blocks = [plan.exchange(gate(part, [grad_heads])) for part in parts]
            side += last_blocks
        else:
            image_cut = plan.rows_out(gate(image_rows, [grad_heads]))
            side += [image_cut]
        rights = [(grad_qkv, lambda kind, c=c: (kind, c)) for c in chunks]
        attn_whole = k.weight_grad("qkv_grad", save["h1"], rights, 3, 8, 0, None)
        rights = [(save["heads"], lambda kind, c=c: (c,)) for c in chunks]
        attn_whole = k.weight_grad("out_grad", grad_out, rights, 1, 8, 6, attn_whole)
        if not depth:
            side.append(attn_whole)
        for c in chunks:
            blocks[c] = plan.exchange(k.qkv_back(grad_qkv, w_qkv[depth], c, side))
        down_grads[depth] = plan.join_sides(down_sum)
        side = [attn_whole, down_grads[depth]]
        if first:
            image_rows = []
            for c in chunks:
                x2, down = k.norm_in(mods, save["x1"][c], last_blocks[c], (depth, 5))
                image_rows.append(x2.astype(BF16))
                save["down"].append(down)
            image_rows = jnp.concatenate(image_rows, axis=0)
            side.append(image_rows)
        else:
            image_out, text_out = from_blocks(plan.rows_back(image_cut))
            side.append(image_out)
        for c in chunks:
            if depth:
                grads[c], got, sums = k.norm_back(
                    mods, grads[c], blocks[c], save["x"][c], (depth, 1), kept[depth - 1]["down"][c], (depth - 1, 5), side
                )
                next_down.append(plan.exchange(got))
            else:
                grads[c], sums = k.norm_back(mods, grads[c], blocks[c], save["x"][c], (depth, 1), after=side)
            sums1.append(sums)
        if depth:
            attn_whole = gate(attn_whole, sums1)
        attn_both = plan.scatter_weights(attn_whole[..., :features])
        if first:
            gate2 = []
            for c in chunks:
                moved = start[c] * save["down"][c]
                sums = jnp.stack([jnp.sum(moved[: k.ci], axis=0), jnp.sum(moved[k.ci :], axis=0)])
                gate2.append(jnp.broadcast_to(sums[:, None], (2, 3, D)))
        first_, second, gates = sum(sums1), sum(sums2), sum(gate2)
        mod_grads[depth] = jnp.stack(
            [first_[:, 0], first_[:, 1], second[:, 2], second[:, 0], second[:, 1], gates[:, 2]], axis=1
        )
        gate2, grad_down = sums1, next_down
    up_grads[0] = plan.join_sides(up_sum)
    attn_grads[0] = plan.join_sides(plan.sum_levels(attn_both)[0])
    grad_image, grad_text = from_blocks(
        plan.rows_back(plan.rows_out(jnp.concatenate([one.astype(BF16) for one in grads], axis=0)))
    )

    mod_part = plan.natural(jnp.stack(mod_grads)).reshape(LAYERS, 2, 6, cols, features)
    mod_part = jnp.transpose(mod_part, (3, 1, 0, 2, 4)).reshape(cols, -1)
    mod_all = plan.vectors_out(mod_part).astype(BF16).reshape(rows_count, 2, LAYERS * 6, features)
    mod_cut = [unsort_vectors(mod_all[:, s], 6) for s in range(2)]
    grad_mod = [tn(cond_mine, cut) for cut in mod_cut]
    cond_part = nt(mod_cut[0], mod_image) + nt(mod_cut[1], mod_text)
    cond_sum = lax.psum(lax.all_to_all(cond_part, "row", split_axis=0, concat_axis=0, tiled=True), "col")
    _, silu_pull = jax.vjp(jax.nn.silu, cond_float)
    grad_cond = silu_pull(cond_sum.reshape(1, D))[0]

    grad_qkv_w = [
        merge_columns([[attn_grads[d][2 * kind + s] for kind in range(3)] for d in range(LAYERS)], 3)
        for s in range(2)
    ]
    grad_out_w = [merge_columns([[attn_grads[d][6 + s]] for d in range(LAYERS)], 1) for s in range(2)]
    layered = [
        jnp.stack([grads_[d][s].astype(F32) for d in range(LAYERS)]) for grads_ in (up_grads, down_grads) for s in range(2)
    ]
    return (
        image_out,
        text_out,
        grad_image.astype(F32),
        grad_text.astype(F32),
        grad_cond,
        grad_mod[0],
        grad_mod[1],
        grad_qkv_w[0],
        grad_qkv_w[1],
        grad_out_w[0],
        grad_out_w[1],
        layered[0],
        layered[1],
        layered[2],
        layered[3],
    )


def solution(mesh):
    flat = P("row", "col")
    layered = P(None, "row", "col")
    return jax.shard_map(
        functools.partial(on_device, mesh.shape["row"], mesh.shape["col"]),
        mesh=mesh,
        in_specs=(flat, flat, P("row", None)) + (flat,) * 6 + (layered,) * 4 + (flat, flat),
        out_specs=(flat,) * 4 + (P("row", None),) + (flat,) * 6 + (layered,) * 4,
        check_vma=False,
    )
```

```python
import functools
import math

import jax
import jax.numpy as jnp
from jax import lax
from jax.experimental import pallas as pl
from jax.experimental.pallas import tpu as pltpu
from jax.sharding import PartitionSpec as P

D = 1536
HEAD = 64
IMG_LEN = 1024
TXT_LEN = 154
LAYERS = 2
EPS = 1e-06
CHUNKS = 1
F32 = jnp.float32
BF16 = jnp.bfloat16


def dot(a, b, ca, cb):
    return lax.dot_general(a, b, (((ca,), (cb,)), ((), ())), preferred_element_type=F32)


def nn(a, b):
    return dot(a, b, 1, 0)


def nt(a, b):
    return dot(a, b, 1, 1)


def tn(a, b):
    return dot(a, b, 0, 0)


class Plan:
    def __init__(self, rows, cols, swap):
        self.rows, self.cols, self.swap = rows, cols, swap
        half = cols // 2
        self.row, self.col = lax.axis_index("row"), lax.axis_index("col")
        self.a, self.x, self.k = self.row // 4, (self.row // 2) % 2, self.row % 2
        self.h, self.l = self.col // half, self.col % half
        self.member = self.x * half + self.l if swap else self.col

        def flat(a, x, k, h, l):
            return (a * 4 + x * 2 + k) * cols + h * half + l

        if swap:
            sides = [(a, k) for a in range(rows // 4) for k in range(2)]
            self.team = [
                [flat(a, x, k, h, l) for x in range(2) for l in range(half)] for a, k in sides for h in range(2)
            ]
            self.plane = [
                [flat(a, x, k, h, l) for x in range(2) for h in range(2) for l in range(half)] for a, k in sides
            ]
            self.home = [(flat(a, x, k, 1 - x, l), flat(a, x, k, x, l)) for a, k in sides for x in range(2) for l in range(half)]
            self.across = [(r, r ^ 2) for r in range(rows)]
            self.levels = [(c, (c + half) % cols) for c in range(cols)]
            self.fetch = [[a * 4 + x * 2 + k for a, k in sides] for x in range(2)]

    def exchange(self, blocks):
        if self.swap:
            return lax.all_to_all(
                blocks, ("row", "col"), 0, 0, tiled=True, axis_index_groups=self.team
            )
        return lax.all_to_all(blocks, "col", 0, 0, tiled=True)


    def inner(self, natural):
        if not self.swap:
            return natural
        lead = natural.shape[:-1]
        cut = natural.reshape(lead + (self.rows // 4, 2, 2, D // self.rows))
        return jnp.swapaxes(cut, -3, -2).reshape(lead + (D,))

    natural = inner

    def pick(self, index, pair):
        return jnp.where(index == 0, pair[0], pair[1]), jnp.where(index == 0, pair[1], pair[0])

    def place(self, index, mine, other):
        return jnp.where(index == 0, mine, other), jnp.where(index == 0, other, mine)

    def swap_sides(self, pieces, after=()):
        mine = jnp.stack(pieces)
        if not self.swap:
            return mine
        wide = mine.shape[2] // 2
        mine, other = self.pick(self.x, [mine[:, :, :wide], mine[:, :, wide:]])
        if len(after):
            other = gate(other, after)
        return jnp.concatenate(self.place(self.x, mine, lax.ppermute(other, "row", self.across)), axis=1)

    def swap_levels(self, both, after=()):
        if not self.swap:
            return both
        h = tick(self.h, after) if len(after) else self.h
        return jnp.concatenate(self.place(h, both, lax.ppermute(both, "col", self.levels)), axis=2)

    def gather_weights(self, both):
        if not self.swap:
            return lax.all_gather(both, "row", axis=0)
        return lax.all_gather(both, "row", axis=0, axis_index_groups=self.fetch)

    def scatter_weights(self, whole):
        groups = self.fetch if self.swap else None
        return lax.psum_scatter(whole, "row", scatter_dimension=0, tiled=True, axis_index_groups=groups)[0]

    def sum_levels(self, both):
        if not self.swap:
            return both, both
        wide = both.shape[2] // 2
        mine, other = self.pick(self.h, [both[:, :, :wide], both[:, :, wide:]])
        return (mine.astype(F32) + lax.ppermute(other, "col", self.levels).astype(F32)).astype(BF16), other

    def join_sides(self, both):
        if not self.swap:
            return both
        rows = both.shape[1] // 2
        mine, other = self.pick(self.x, [both[:, :rows], both[:, rows:]])
        return jnp.concatenate(self.place(self.x, mine, lax.ppermute(other, "row", self.across)), axis=2)

    def rows_home(self, blocks):
        if not self.swap:
            return blocks
        moved = lax.ppermute(blocks, ("row", "col"), self.home)
        return jnp.stack(self.place(self.h, blocks, moved), axis=1)

    def rows_in(self, pair, kernels, after=()):
        got = self.exchange(pair)
        if self.swap and kernels is not None:
            return kernels.enter(self, got.reshape((2, 2) + got.shape[1:]), (1, 0), after)
        if not self.swap:
            return jnp.transpose(got, (1, 0, 2)).reshape(got.shape[1], D)
        got = got.reshape((2, self.cols // 2) + got.shape[1:])
        got = jnp.where(self.h == 0, got[0], got[1])
        return self.inner(jnp.transpose(got, (2, 1, 0, 3)).reshape(got.shape[2], D))

    def rows_over(self, blocks, kernels):
        if not self.swap or kernels is None:
            return self.rows_in(self.rows_home(blocks), kernels)
        cut = blocks.reshape((2, 1, self.cols // 2) + blocks.shape[1:])
        cut = jnp.broadcast_to(cut, (2, 2) + cut.shape[2:]).reshape((2 * self.cols,) + blocks.shape[1:])
        got = lax.all_to_all(cut, ("row", "col"), 0, 0, tiled=True, axis_index_groups=self.plane)
        return kernels.enter(self, got.reshape((2, 2, self.cols // 2) + blocks.shape[1:]), (0, 1))

    def rows_home_again(self, own, kernels, first=(), second=()):
        if not self.swap or kernels is None:
            return self.rows_back(self.rows_out(own, kernels)), own
        cut = kernels.leave(own, first)
        cut = cut.reshape((2 * self.cols,) + cut.shape[2:])
        got = lax.all_to_all(cut, ("row", "col"), 0, 0, tiled=True, axis_index_groups=self.plane)
        got = got.reshape((2, 2, self.cols // 2) + got.shape[1:])
        x = tick(self.x, second) if len(second) else self.x
        got = jnp.where(x == 0, got[:, 0], got[:, 1])
        return got.reshape((self.cols,) + got.shape[2:]), cut

    def rows_out(self, own, kernels):
        tokens, own = own.shape[0], own.astype(BF16)
        if not self.swap:
            return self.exchange(jnp.transpose(own.reshape(tokens, self.cols, -1), (1, 0, 2)))
        cut = self.natural(own).reshape(tokens, 2, self.cols // 2, D // self.cols)
        cut = jnp.transpose(cut, (2, 1, 0, 3))
        return self.exchange(jnp.concatenate([cut, cut], axis=0))

    def rows_back(self, got):
        if not self.swap:
            return got
        mine, other = self.pick(self.h, [got[:, 0], got[:, 1]])
        back = lax.ppermute(other, ("row", "col"), [(b, a) for a, b in self.home])
        return jnp.where(self.x == self.h, mine, back)

    def vectors_rows(self, part):
        if not self.swap:
            return jnp.sum(lax.all_to_all(part, "row", 0, 0, tiled=True), axis=0, keepdims=True)
        cut = part.reshape(self.rows // 4, 1, 2, 2, -1)
        cut = jnp.broadcast_to(cut, (self.rows // 4, 2) + cut.shape[2:])
        sent = jnp.transpose(cut, (0, 1, 3, 2, 4)).reshape(self.rows, 2, -1)
        return jnp.sum(lax.all_to_all(sent, "row", 0, 0, tiled=True), axis=0)

    def vectors_cols(self, mine):
        if not self.swap:
            return lax.all_to_all(jnp.broadcast_to(mine, (self.cols, mine.shape[1])), "col", 0, 0, tiled=True)
        half = self.cols // 2
        sent = jnp.broadcast_to(mine[:, None], (2, half, mine.shape[1])).reshape(self.cols, -1)
        return lax.all_to_all(sent, "col", 0, 0, tiled=True)

    def vectors_cols_back(self, part):
        got = lax.all_to_all(part, "col", 0, 0, tiled=True)
        if not self.swap:
            return jnp.sum(got, axis=0, keepdims=True)
        return jnp.sum(got.reshape(2, self.cols // 2, -1), axis=1)

    def vectors_rows_back(self, mine):
        every = lax.all_to_all(jnp.broadcast_to(mine[None], (self.rows,) + mine.shape), "row", 0, 0, tiled=True)
        if not self.swap:
            return every.reshape(self.rows, -1)
        every = jnp.sum(every.reshape(self.rows // 4, 2, 2, 2, -1), axis=1)
        return jnp.transpose(every, (0, 2, 1, 3)).reshape(self.rows, -1)

def norm(x):
    average = jnp.mean(x, axis=1, keepdims=True)
    centred = x - average
    inverse = lax.rsqrt(jnp.mean(centred * centred, axis=1, keepdims=True) + EPS)
    return centred * inverse, inverse


def call(kernel, name, grid, ins, outs, flops=0, after=(), alias=None, scratch=(), transcendentals=0, room=58):
    args = [a for a, _, _ in ins]
    in_specs = [pl.BlockSpec(block, index) for _, block, index in ins]
    extra = list(after)
    aliases = {}
    if alias is not None:
        aliases = {len(args): 0}
        extra = [alias] + extra
    given = len(args)

    def body(*refs):
        kernel(*refs[:given], *refs[given + len(extra) :])

    moved = sum(a.size * a.dtype.itemsize for a in args)
    for shape, dtype, _, _ in outs:
        moved += math.prod(shape) * jnp.dtype(dtype).itemsize
    got = pl.pallas_call(
        body,
        grid=grid,
        in_specs=in_specs + [pl.BlockSpec(memory_space=pl.ANY)] * len(extra),
        out_specs=[pl.BlockSpec(block, index) for _, _, block, index in outs],
        out_shape=[jax.ShapeDtypeStruct(shape, dtype) for shape, dtype, _, _ in outs],
        scratch_shapes=list(scratch),
        input_output_aliases=aliases,
        compiler_params=pltpu.CompilerParams(vmem_limit_bytes=room << 20),
        cost_estimate=pl.CostEstimate(
            flops=flops // 8, bytes_accessed=moved // 8, transcendentals=transcendentals // 8
        ),
        name=name,
    )(*args, *extra)
    return got[0] if len(got) == 1 else got


def tick(index, after):
    def kernel(given, out):
        out[...] = given[...]

    one = jnp.full((8, 128), index, jnp.int32)
    whole = ((8, 128), lambda i: (0, 0))
    return call(kernel, "tick", (1,), [(one,) + whole], [((8, 128), jnp.int32) + whole], after=after)[0, 0]


def gate(array, after):
    def kernel(*refs):
        pass

    return pl.pallas_call(
        kernel,
        in_specs=[pl.BlockSpec(memory_space=pl.ANY)] * (1 + len(after)),
        out_specs=pl.BlockSpec(memory_space=pl.ANY),
        out_shape=jax.ShapeDtypeStruct(array.shape, array.dtype),
        input_output_aliases={0: 0},
        cost_estimate=pl.CostEstimate(flops=0, bytes_accessed=1024, transcendentals=0),
        name="gate",
    )(array, *after)


class Kernels:
    def __init__(self, members, ci, ct, chunks, groups, wide, hidden):
        self.q, self.ci, self.ct, self.rc, self.n = members, ci, ct, ci + ct, chunks
        self.g, self.dr = groups, D // groups
        self.wide, self.hidden = wide, hidden
        self.tokens = members * self.rc * chunks

    def rows(self, array, columns, index, lead=None):
        if lead is None:
            return [(array, (self.q, self.rc, columns), lambda *i: (0, 0, index(*i)))]
        return [(array, (1,) * len(lead(0)) + (self.q, self.rc, columns), lambda *i: lead(*i) + (0, 0, index(*i)))]

    def image(self, ref):
        value = ref[..., : self.ci, :]
        return value.reshape(-1, value.shape[-1])

    def text(self, ref):
        value = ref[..., self.ci :, :]
        return value.reshape(-1, value.shape[-1])

    def weight(self, array, columns, piece, index):
        return [
            (array, (self.g, 1, self.dr, columns), lambda *i, s=s: (0, piece(*i) + s, 0, index(*i))) for s in range(2)
        ]

    def flat(self, ref):
        value = ref[...]
        return value.reshape(-1, value.shape[-1])

    def put(self, ref, img, txt):
        cut = ref.shape[:-2]
        ref[..., : self.ci, :] = img.astype(ref.dtype).reshape(cut + (self.ci, ref.shape[-1]))
        ref[..., self.ci :, :] = txt.astype(ref.dtype).reshape(cut + (self.ct, ref.shape[-1]))

    def qkv(self, h, weights, chunk, joint, after=()):
        def kernel(h, wi, wt, out):
            self.put(out, nn(self.image(h), self.flat(wi)), nn(self.text(h), self.flat(wt)))

        return call(
            kernel,
            "qkv",
            (3,),
            self.rows(h, D, lambda j: 0) + self.weight(weights, self.wide, lambda j: 2 * j, lambda j: 0),
            [
                (
                    (self.n, self.q, self.rc, 3 * self.wide),
                    BF16,
                    (1, self.q, self.rc, self.wide),
                    lambda j: (chunk, 0, 0, j),
                )
            ],
            flops=2 * self.q * self.rc * D * 3 * self.wide,
            alias=joint,
            after=after,
        )

    def project(self, heads, weights, piece, chunk, after=()):
        def kernel(h, wi, wt, out):
            self.put(out, nt(self.image(h), self.flat(wi)), nt(self.text(h), self.flat(wt)))

        return call(
            kernel,
            "project",
            (1,),
            self.rows(heads, self.wide, lambda i: 0, lambda i: (chunk,))
            + self.weight(weights, self.wide, lambda i: piece, lambda i: 0),
            [((self.q, self.rc, D), BF16, (self.q, self.rc, D), lambda i: (0, 0, 0))],
            flops=2 * self.q * self.rc * D * self.wide,
            after=after,
        )

    def project_back(self, grad, weights, piece, chunk, joint, after=()):
        def kernel(h, wi, wt, out):
            self.put(out, nn(self.image(h), self.flat(wi)), nn(self.text(h), self.flat(wt)))

        return call(
            kernel,
            "project_back",
            (1,),
            self.rows(grad, D, lambda i: 0) + self.weight(weights, self.wide, lambda i: piece, lambda i: 0),
            [
                (
                    (self.n, self.q, self.rc, self.wide),
                    BF16,
                    (1, self.q, self.rc, self.wide),
                    lambda i: (chunk, 0, 0, 0),
                )
            ],
            flops=2 * self.q * self.rc * D * self.wide,
            alias=joint,
            after=after,
        )

    def qkv_back(self, grads, weights, chunk, after=()):
        def kernel(h, wi, wt, out, sum_i, sum_t):
            j = pl.program_id(0)
            img, txt = nt(self.image(h), self.flat(wi)), nt(self.text(h), self.flat(wt))

            @pl.when(j == 0)
            def _():
                sum_i[...] = img
                sum_t[...] = txt

            @pl.when(j == 1)
            def _():
                sum_i[...] += img
                sum_t[...] += txt

            @pl.when(j == 2)
            def _():
                self.put(out, sum_i[...] + img, sum_t[...] + txt)

        return call(
            kernel,
            "qkv_back",
            (3,),
            self.rows(grads, self.wide, lambda j: 0, lambda j: (j, chunk))
            + self.weight(weights, self.wide, lambda j: 2 * j, lambda j: 0),
            [((self.q, self.rc, D), BF16, (self.q, self.rc, D), lambda j: (0, 0, 0))],
            flops=2 * self.q * self.rc * D * 3 * self.wide,
            after=after,
            scratch=[pltpu.VMEM((self.q * self.ci, D), F32), pltpu.VMEM((self.q * self.ct, D), F32)],
        )

    def mlp(self, h, ups, downs, after=()):
        steps = 3
        block = self.hidden // steps

        def gelu(v):
            inner = 0.7978845608028654 * (v + 0.044715 * v * v * v)
            t = jnp.tanh(inner)
            half = 0.5 * (1.0 + t)
            slope = half + 0.5 * v * (1.0 - t * t) * (0.7978845608028654 * (1.0 + 3 * 0.044715 * v * v))
            return (v * half).astype(BF16), slope.astype(BF16)

        def kernel(h, ui, ut, di, dt, act, slope, out, sum_i, sum_t):
            j = pl.program_id(0)
            gi, si = gelu(nn(self.image(h), self.flat(ui)))
            gt, st = gelu(nn(self.text(h), self.flat(ut)))
            self.put(act, gi, gt)
            self.put(slope, si, st)
            img, txt = nt(gi, self.flat(di)), nt(gt, self.flat(dt))

            @pl.when(j == 0)
            def _():
                sum_i[...] = img
                sum_t[...] = txt

            @pl.when(jnp.logical_and(j > 0, j < steps - 1))
            def _():
                sum_i[...] += img
                sum_t[...] += txt

            @pl.when(j == steps - 1)
            def _():
                self.put(out, sum_i[...] + img, sum_t[...] + txt)

        return call(
            kernel,
            "mlp",
            (steps,),
            self.rows(h, D, lambda j: 0)
            + self.weight(ups, block, lambda j: 0, lambda j: j)
            + self.weight(downs, block, lambda j: 0, lambda j: j),
            [
                ((self.q, self.rc, self.hidden), BF16, (self.q, self.rc, block), lambda j: (0, 0, j)),
                ((self.q, self.rc, self.hidden), BF16, (self.q, self.rc, block), lambda j: (0, 0, j)),
                ((self.q, self.rc, D), BF16, (self.q, self.rc, D), lambda j: (0, 0, 0)),
            ],
            flops=4 * self.q * self.rc * D * self.hidden,
            transcendentals=self.q * self.rc * self.hidden,
            after=after,
            scratch=[pltpu.VMEM((self.q * self.ci, D), F32), pltpu.VMEM((self.q * self.ct, D), F32)],
        )

    def mlp_back(self, grad, slope, ups, downs, after=()):
        steps = 3
        block = self.hidden // steps

        def kernel(h, s, ui, ut, di, dt, pre, out, sum_i, sum_t):
            j = pl.program_id(0)
            pi = (nn(self.image(h), self.flat(di)) * self.image(s).astype(F32)).astype(BF16)
            pt = (nn(self.text(h), self.flat(dt)) * self.text(s).astype(F32)).astype(BF16)
            self.put(pre, pi, pt)
            img, txt = nt(pi, self.flat(ui)), nt(pt, self.flat(ut))

            @pl.when(j == 0)
            def _():
                sum_i[...] = img
                sum_t[...] = txt

            @pl.when(jnp.logical_and(j > 0, j < steps - 1))
            def _():
                sum_i[...] += img
                sum_t[...] += txt

            @pl.when(j == steps - 1)
            def _():
                self.put(out, sum_i[...] + img, sum_t[...] + txt)

        return call(
            kernel,
            "mlp_back",
            (steps,),
            self.rows(grad, D, lambda j: 0)
            + self.rows(slope, block, lambda j: j)
            + self.weight(ups, block, lambda j: 0, lambda j: j)
            + self.weight(downs, block, lambda j: 0, lambda j: j),
            [
                ((self.q, self.rc, self.hidden), BF16, (self.q, self.rc, block), lambda j: (0, 0, j)),
                ((self.q, self.rc, D), BF16, (self.q, self.rc, D), lambda j: (0, 0, 0)),
            ],
            flops=4 * self.q * self.rc * D * self.hidden,
            after=after,
            scratch=[pltpu.VMEM((self.q * self.ci, D), F32), pltpu.VMEM((self.q * self.ct, D), F32)],
        )

    def weight_grad(self, name, left, right, kinds, pieces, first, whole, after=()):
        columns = right[0][0].shape[-1]

        def rows(refs, side):
            got = [self.text(ref) if side else self.image(ref) for ref in refs]
            return got[0] if len(got) == 1 else jnp.concatenate(got, axis=0)

        if self.dr % 128:
            cut = []
            for kind in range(kinds):
                for side in (slice(0, self.ci), slice(self.ci, self.rc)):
                    a = jnp.concatenate([one[:, side].reshape(-1, D) for one in left], axis=0)
                    b = [one[lead(kind)] if lead else one for one, lead in right]
                    b = jnp.concatenate([one[:, side].reshape(-1, columns) for one in b], axis=0)
                    cut.append(tn(a, b).astype(BF16).reshape(self.g, self.dr, columns))
            cut = jnp.stack(cut, axis=1)
            return cut if whole is None else jnp.concatenate([whole, cut], axis=1)

        def kernel(*refs):
            ins, out = refs[:-1], refs[-1]
            for side in range(2):
                a, b = rows(ins[: self.n], side), rows(ins[self.n :], side)
                out[0, side] = tn(a, b).astype(BF16)

        ins = []
        for one in left:
            ins += self.rows(one, self.dr, lambda j, g: g)
        for one, lead in right:
            ins += self.rows(one, columns, lambda j, g: 0, (lambda j, g=0, lead=lead: lead(j)) if lead else None)
        return call(
            kernel,
            name,
            (kinds, self.g),
            ins,
            [
                (
                    (self.g, pieces, self.dr, columns),
                    BF16,
                    (1, 2, self.dr, columns),
                    lambda j, g: (g, first // 2 + j, 0, 0),
                )
            ],
            flops=2 * self.tokens * D * columns * kinds,
            alias=whole,
            after=after,
        )

    def norm_in(self, mods, x, blocks=None, gate=None, after_norm=None, after=()):
        rows = self.ci // 4

        def kernel(*refs):
            refs = list(refs)
            value = refs.pop(0)[...]
            if blocks is not None:
                added = jnp.sum(refs.pop(0)[...].astype(F32), axis=0)
                value = value + refs.pop(0)[0, gate[1] : gate[1] + 1] * added
            vectors = refs.pop(0) if after_norm is not None else None
            if blocks is not None:
                refs.pop(0)[...] = value
                refs.pop(0)[...] = added
            if after_norm is not None:
                kind = after_norm[1]
                normed = norm(value)[0]
                out = (normed * (1.0 + vectors[0, kind + 1 : kind + 2]) + vectors[0, kind : kind + 1]).astype(BF16)
                refs[0][...] = jnp.broadcast_to(out[None], refs[0].shape)

        ratio = 4

        def vectors(depth):
            return (mods, (1,) + mods.shape[1:], lambda i: (depth * 2 + i // ratio, 0, 0))

        flat = ((rows, D), lambda i: (i, 0))
        many = ((self.q, rows, D), lambda i: (0, i, 0))
        ins, outs = [(x,) + flat], []
        if blocks is not None:
            ins += [(blocks,) + many, vectors(gate[0])]
            outs += [((self.rc, D), F32) + flat] * 2
        if after_norm is not None:
            ins.append(vectors(after_norm[0]))
            outs.append(((self.q, self.rc, D), BF16) + many)
        return call(kernel, "norm_in", (ratio + 1,), ins, outs, flops=20 * self.rc * D, after=after)

    def norm_back(self, mods, grad, blocks=None, x=None, scale=None, branch=None, gate=None, after=()):
        rows, ratio = self.ci // 4, 4

        def kernel(*refs):
            refs = list(refs)
            i = pl.program_id(0)
            held = lax.broadcasted_iota(jnp.int32, (rows, 1), 0) < self.rc - i * rows

            def take():
                return jnp.where(held, refs.pop(0)[...], 0.0)

            value = take()
            rows_of_sums = []
            if blocks is not None:
                dh = jnp.where(held, jnp.sum(refs.pop(0)[...].astype(F32), axis=0), 0.0)
                normed, inverse = norm(take())
                dn = dh * (1.0 + refs.pop(0)[0, scale[1] : scale[1] + 1])
                value = value + inverse * (
                    dn
                    - jnp.mean(dn, axis=1, keepdims=True)
                    - normed * jnp.mean(dn * normed, axis=1, keepdims=True)
                )
                rows_of_sums += [(0, jnp.sum(dh, axis=0, keepdims=True)), (1, jnp.sum(dh * normed, axis=0, keepdims=True))]
            if branch is not None:
                rows_of_sums.append((2, jnp.sum(value * take(), axis=0, keepdims=True)))
            if gate is not None:
                factor = refs.pop(0)[0, gate[1] : gate[1] + 1]
            if blocks is not None:
                refs.pop(0)[...] = value
            if gate is not None:
                out = refs.pop(0)
                out[...] = jnp.broadcast_to((factor * value).astype(BF16)[None], out.shape)
            if not rows_of_sums:
                return
            sums = refs.pop(0)
            start = jnp.logical_or(i == 0, i == ratio)

            @pl.when(start)
            def _():
                for at, row in rows_of_sums:
                    sums[0, at : at + 1] = row

            @pl.when(jnp.logical_not(start))
            def _():
                for at, row in rows_of_sums:
                    sums[0, at : at + 1] += row

        def vectors(depth):
            return (mods, (1,) + mods.shape[1:], lambda i: (depth * 2 + i // ratio, 0, 0))

        flat = ((rows, D), lambda i: (i, 0))
        many = ((self.q, rows, D), lambda i: (0, i, 0))
        ins, outs = [(grad,) + flat], []
        if blocks is not None:
            ins += [(blocks,) + many, (x,) + flat, vectors(scale[0])]
            outs.append(((self.rc, D), F32) + flat)
        if branch is not None:
            ins.append((branch,) + flat)
        if gate is not None:
            ins.append(vectors(gate[0]))
            outs.append(((self.q, self.rc, D), BF16) + many)
        if blocks is not None or branch is not None:
            outs.append(((2, 8, D), F32, (1, 8, D), lambda i: (i // ratio, 0, 0)))
        return call(kernel, "norm_back", (ratio + 1,), ins, outs, flops=30 * self.rc * D, after=after)

    def enter(self, plan, got, order, after=()):
        rows, half = self.ci // 4, D // self.g // 2
        wide = got.shape[-1]

        def kernel(index, ref, out):
            first = index[0:1, 0:1] == 0
            for a in range(2):
                for x in range(2):
                    at = (a, x) if order[0] == 0 else (x, a)
                    piece = jnp.where(first, ref[(0,) + at].astype(F32), ref[(1,) + at].astype(F32))
                    for side in range(2):
                        at = (a * 4 + side * 2 + x) * half
                        out[:, at : at + half] = piece[:, side * half : (side + 1) * half]

        return call(
            kernel,
            "enter",
            (-(-self.rc // rows),),
            [
                (jnp.full((8, 128), plan.h, jnp.int32), (8, 128), lambda i: (0, 0)),
                (got, (2, 2, 2, rows, wide), lambda i: (0, 0, 0, i, 0)),
            ],
            [((self.rc, D), F32, (rows, D), lambda i: (i, 0))],
            flops=self.rc * D,
            after=after,
        )

    def leave(self, own, after=()):
        rows, half = self.ci // 4, D // self.g // 2
        wide = D // self.q

        def kernel(ref, out):
            for a in range(2):
                for x in range(2):
                    at = [(a * 4 + side * 2 + x) * half for side in range(2)]
                    piece = jnp.concatenate([ref[:, i : i + half] for i in at], axis=1).astype(BF16)
                    for side in range(2):
                        out[side, 2 * a + x] = piece

        return call(
            kernel,
            "leave",
            (-(-self.rc // rows),),
            [(own, (rows, D), lambda i: (i, 0))],
            [((2, self.q, self.rc, wide), BF16, (2, self.q, rows, wide), lambda i: (0, 0, i, 0))],
            flops=self.rc * D,
            after=after,
        )

    def masks(self):
        at = lax.broadcasted_iota(jnp.int32, (self.n, self.q, self.rc), 2)
        chunk = lax.broadcasted_iota(jnp.int32, (self.n, self.q, self.rc), 0)
        member = lax.broadcasted_iota(jnp.int32, (self.n, self.q, self.rc), 1)
        text = member * (self.ct * self.n) + chunk * self.ct + at - self.ci
        absent = jnp.logical_and(at >= self.ci, text >= TXT_LEN)
        return jnp.where(absent, -1e30, 0.0).astype(BF16).reshape(self.tokens, 1)

    def attend(self, joint, mask, after=()):
        t, pairs = self.tokens, self.wide // 128

        def kernel(q_ref, k_ref, v_ref, mask_ref, o_ref):
            q, k, v = q_ref[...], k_ref[...], v_ref[...]
            lane = lax.broadcasted_iota(jnp.int32, q.shape, 1)
            first = lane < HEAD
            none = jnp.zeros_like(q)
            bias = jnp.broadcast_to(mask_ref[...], k.shape)
            outs = []
            for side, spare in ((True, HEAD), (False, 0)):
                ones = jnp.where(lane == spare, jnp.ones_like(q), none)
                scaled = jnp.where(first == side, q * jnp.asarray(HEAD**-0.5, BF16), ones)
                scores = nt(scaled, jnp.where(first == side, k, bias))
                weights = jnp.exp(scores - jnp.max(scores, axis=1, keepdims=True))
                totals = jnp.sum(weights, axis=1, keepdims=True)
                outs.append(nn(weights.astype(BF16), v) * (1.0 / totals))
            o_ref[...] = jnp.where(first, outs[0], outs[1]).astype(BF16)

        flat = joint.reshape(t, 3 * self.wide)
        out = call(
            kernel,
            "attend",
            (pairs,),
            [(flat, (t, 128), lambda p, part=part: (0, part * pairs + p)) for part in range(3)]
            + [(mask, (t, 1), lambda p: (0, 0))],
            [((t, self.wide), BF16, (t, 128), lambda p: (0, p))],
            flops=pairs * 8 * t * t * 128,
            transcendentals=pairs * 2 * t * t,
            after=after,
            room=48,
        )
        return out.reshape(self.n, self.q, self.rc, self.wide)

    def attend_back(self, joint, mask, grad, after=()):
        t, pairs = self.tokens, self.wide // 128

        def kernel(q_ref, k_ref, v_ref, mask_ref, do_ref, out_ref):
            q, k, v, do = q_ref[...], k_ref[...], v_ref[...], do_ref[...]
            lane = lax.broadcasted_iota(jnp.int32, q.shape, 1)
            first = lane < HEAD
            none = jnp.zeros_like(q)
            bias = jnp.broadcast_to(mask_ref[...], k.shape)
            scale = jnp.asarray(HEAD**-0.5, BF16)
            dq = dk = dv = None
            for side, spare in ((True, HEAD), (False, 0)):
                mine = first == side
                ones = jnp.where(lane == spare, jnp.ones_like(q), none)
                scaled = q * scale
                grad_o = jnp.where(mine, do, none)
                scores = nt(jnp.where(mine, k, bias), jnp.where(mine, scaled, ones))
                weights = jnp.exp(scores - jnp.max(scores, axis=0, keepdims=True))
                chances = weights * (1.0 / jnp.sum(weights, axis=0, keepdims=True))
                grad_chances = nt(v, grad_o)
                centre = jnp.sum(grad_chances * chances, axis=0, keepdims=True)
                grad_scores = (chances * (grad_chances - centre)).astype(BF16)
                one_v = nn(chances.astype(BF16), grad_o)
                one_k = nn(grad_scores, jnp.where(mine, scaled, none))
                one_q = tn(grad_scores, jnp.where(mine, k * scale, none))
                dq, dk, dv = (one_q, one_k, one_v) if dq is None else (dq + one_q, dk + one_k, dv + one_v)
            out_ref[0] = dq.astype(BF16)
            out_ref[1] = dk.astype(BF16)
            out_ref[2] = dv.astype(BF16)

        flat = joint.reshape(t, 3 * self.wide)
        out = call(
            kernel,
            "attend_back",
            (pairs,),
            [(flat, (t, 128), lambda p, part=part: (0, part * pairs + p)) for part in range(3)]
            + [(mask, (t, 1), lambda p: (0, 0)), (grad.reshape(t, self.wide), (t, 128), lambda p: (0, p))],
            [((3, t, self.wide), BF16, (3, t, 128), lambda p: (0, 0, p))],
            flops=pairs * 20 * t * t * 128,
            transcendentals=pairs * 2 * t * t,
            after=after,
            room=56,
        )
        return out.reshape(3, self.n, self.q, self.rc, self.wide)


def order_matrix(block, kinds):
    width = block * LAYERS * kinds
    source = lax.broadcasted_iota(jnp.int32, (width, width), 0)
    target = lax.broadcasted_iota(jnp.int32, (width, width), 1)
    return (source == (target % block) * (LAYERS * kinds) + target // block).astype(BF16)


def split_columns(weight, kinds):
    rows = weight.shape[0]
    features = weight.shape[1] // (LAYERS * kinds)
    block = 128 if features % 128 == 0 else 64
    wide = block * LAYERS * kinds
    matrix = order_matrix(block, kinds)
    parts = [nn(weight[:, i * wide : (i + 1) * wide], matrix).astype(BF16) for i in range(features // block)]

    def one(at):
        return jnp.concatenate([part[:, at * block : (at + 1) * block] for part in parts], axis=1)

    return [[one(depth * kinds + kind) for kind in range(kinds)] for depth in range(LAYERS)]


def merge_columns(pieces, kinds):
    features = pieces[0][0].shape[1]
    block = 128 if features % 128 == 0 else 64
    matrix = order_matrix(block, kinds)
    parts = []
    for i in range(features // block):
        sorted_ = jnp.concatenate(
            [piece[:, i * block : (i + 1) * block] for layer in pieces for piece in layer], axis=1
        )
        parts.append(nt(sorted_, matrix))
    return jnp.concatenate(parts, axis=1)


def sort_vectors(part, kinds):
    rows = part.shape[0]
    features = part.shape[1] // (LAYERS * kinds)
    block = 128 if features % 128 == 0 else 64
    wide = block * LAYERS * kinds
    terms, rest = [], part
    for _ in range(3):
        term = lax.reduce_precision(rest, 8, 7)
        terms.append(term.astype(BF16))
        rest = rest - term
    matrix = order_matrix(block, kinds)
    cuts = jnp.concatenate(terms, axis=0)
    out = []
    for i in range(features // block):
        got = nn(cuts[:, i * wide : (i + 1) * wide], matrix).reshape(3, rows, LAYERS * kinds, block)
        out.append(got[0] + got[1] + got[2])
    return jnp.concatenate(out, axis=2)


def unsort_vectors(sorted_, kinds):
    rows, _, features = sorted_.shape
    block = 128 if features % 128 == 0 else 64
    matrix = order_matrix(block, kinds)
    out = [
        nt(sorted_[:, :, i * block : (i + 1) * block].reshape(rows, -1), matrix).astype(BF16)
        for i in range(features // block)
    ]
    return jnp.concatenate(out, axis=1)


def on_device(
    rows_count,
    cols,
    image_in,
    text_in,
    condition,
    mod_image,
    mod_text,
    qkv_image,
    qkv_text,
    out_image,
    out_text,
    up_image,
    up_text,
    down_image,
    down_text,
    cot_image,
    cot_text,
):
    features = D // cols
    swap = cols % 2 == 0 and rows_count % 4 == 0 and features % (2 * HEAD) == 0
    plan = Plan(rows_count, cols, swap)
    width_rows = mod_image.shape[0]
    img_own = IMG_LEN // cols
    txt_own = -(-TXT_LEN // (16 * cols)) * 16
    txt_pad = txt_own * cols
    wide = features + -features % 128
    k = Kernels(
        cols,
        img_own // CHUNKS,
        txt_own // CHUNKS,
        CHUNKS,
        rows_count // 2 if swap else rows_count,
        wide,
        up_image.shape[2],
    )
    chunks = range(CHUNKS)
    fast = k if swap and rows_count == 8 and cols == 4 and CHUNKS == 1 else None

    def filled(whole):
        return jnp.pad(whole, ((0, 0),) * 3 + ((0, wide - features),))

    qkv_shards = [split_columns(w, 3) for w in (qkv_image, qkv_text)]
    out_shards = [split_columns(w, 1) for w in (out_image, out_text)]
    w_attn, w_up, w_down = [], [], []
    def sides_attn(depth, after=()):
        pieces = [qkv_shards[s][depth][kind] for kind in range(3) for s in range(2)]
        return plan.swap_sides(pieces + [out_shards[s][depth][0] for s in range(2)], after)

    def sides_up(depth, after=()):
        return plan.swap_sides([up_image[depth], up_text[depth]], after)

    def sides_down(depth, after=()):
        return plan.swap_sides([down_image[depth], down_text[depth]], after)

    def to_blocks(image, text):
        img = jnp.transpose(image.reshape(features, IMG_LEN)).reshape(cols, CHUNKS, k.ci, features)
        txt = jnp.pad(jnp.transpose(text.reshape(features, TXT_LEN)), ((0, txt_pad - TXT_LEN), (0, 0)))
        blocks = jnp.concatenate([img, txt.reshape(cols, CHUNKS, k.ct, features)], axis=2)
        return blocks.reshape(cols, CHUNKS * k.rc, features)

    def to_own(own):
        own = own.astype(F32)
        return [own[c * k.rc : (c + 1) * k.rc] for c in chunks]

    def from_blocks(got):
        got = got.reshape(cols, CHUNKS, k.rc, features)
        img = got[:, :, : k.ci].reshape(IMG_LEN, features)
        txt = got[:, :, k.ci :].reshape(txt_pad, features)[:TXT_LEN]
        return jnp.transpose(img).reshape(1, -1), jnp.transpose(txt).reshape(1, -1)

    cond_float = condition.astype(F32)
    cond_low = jax.nn.silu(cond_float).astype(BF16)
    cond_cut = cond_low.reshape(rows_count, width_rows)
    cond_mine = lax.all_to_all(cond_cut, "row", 0, 0, tiled=True)
    mod_part = [nn(cond_mine, one) for one in (mod_image, mod_text)]
    mod_sorted = jnp.concatenate([sort_vectors(one, 6) for one in mod_part], axis=1)
    blocks = to_blocks(image_in, text_in)
    mod_row = plan.vectors_rows(mod_sorted.reshape(rows_count, -1))
    mod_cols = plan.vectors_cols(mod_row).reshape(cols, 2, LAYERS, 6, features)
    mods = plan.inner(jnp.transpose(mod_cols, (2, 1, 3, 0, 4)).reshape(LAYERS * 2, 6, D))

    mask = k.masks()
    own = plan.rows_over(gate(blocks, [mods]), fast)
    attn = sides_attn(0)
    up = sides_up(0, [attn])
    level = plan.swap_levels(attn, [own, up])
    w_qkv, w_out = [filled(plan.gather_weights(level[:6]))], [(filled(plan.gather_weights(level[6:])), 0)]
    x = to_own(own)
    sent = [k.norm_in(mods, x[c], after_norm=(0, 0)) for c in chunks]
    h1 = [plan.exchange(one) for one in sent]
    kept = []
    for depth in range(LAYERS):
        last = depth + 1 == LAYERS
        if not depth:
            down = sides_down(depth, sent)
        side = [plan.swap_levels(gate(up, x), h1 + [down])]
        w_up.append(plan.gather_weights(side[0]))
        joint = None
        for c in chunks:
            joint = k.qkv(h1[c], w_qkv[depth], c, joint, side)
        side = []
        if last:
            side = [k.norm_back(mods, grads[c], gate=(depth, 5)) for c in chunks]
            grad_down = [plan.exchange(one) for one in side]
        heads = k.attend(joint, mask, side)
        side = grad_down if last else []
        save = dict(x=x, h1=h1, joint=joint, heads=heads, branch=[], x1=[], h2=[], act=[], slope=[], down=[])
        next_x, next_h1 = [], []
        sent = [k.project(heads, *w_out[depth], c, side) for c in chunks]
        blocks = [plan.exchange(one) for one in sent]
        other = [] if last else [to_blocks(cot_image, cot_text), sides_attn(depth + 1, sent)]
        side = [plan.swap_levels(gate(down, sent), blocks + other)]
        w_down.append(plan.gather_weights(side[0]))
        sent = []
        for c in chunks:
            x1, branch, h2 = k.norm_in(mods, x[c], blocks[c], (depth, 2), (depth, 3), side)
            sent.append(h2)
            save["x1"].append(x1)
            save["branch"].append(branch)
            save["h2"].append(plan.exchange(h2))
        side = []
        if not last:
            up = sides_up(depth + 1, sent)
            pair = plan.rows_home(gate(other[0], sent))
            side = [up, pair]
        parts = []
        for c in chunks:
            act, slope, part = k.mlp(save["h2"][c], w_up[depth], w_down[depth], side)
            parts.append(part)
            save["act"].append(act)
            save["slope"].append(slope)
        kept.append(save)
        if last:
            break
        grads = to_own(plan.rows_in(gate(pair, save["h2"] + [up]), fast, save["act"]))
        blocks = [plan.exchange(gate(part, grads)) for part in parts]
        down = sides_down(depth + 1, parts)
        side = [plan.swap_levels(gate(other[1], parts), blocks + [down])]
        whole = filled(plan.gather_weights(side[0]))
        w_qkv.append(whole)
        w_out.append((whole, 6))
        sent = []
        for c in chunks:
            got = k.norm_in(mods, save["x1"][c], blocks[c], (depth, 5), (depth + 1, 0), side)
            next_x.append(got[0])
            save["down"].append(got[1])
            sent.append(got[2])
            next_h1.append(plan.exchange(got[2]))
        x, h1 = next_x, next_h1

    start = list(grads)
    mod_grads = [None] * LAYERS
    attn_grads, up_grads, down_grads = [None] * LAYERS, [None] * LAYERS, [None] * LAYERS
    for depth in reversed(range(LAYERS)):
        first = depth + 1 == LAYERS
        save = kept[depth]
        grad_pre, blocks, grad_out, sums2, sums1, next_down = ([] for _ in range(6))
        side = []
        if not first:
            up_grads[depth + 1] = plan.join_sides(up_sum)
            side = [up_grads[depth + 1]]
        if not first:
            image_cut, _ = plan.rows_home_again(gate(image_rows, grad_down), fast)
            image_out, text_out = from_blocks(image_cut)
        down_whole = k.weight_grad("down_grad", grad_down, [(one, None) for one in save["act"]], 1, 2, 0, None, side)
        down_both = plan.scatter_weights(down_whole)
        for c in chunks:
            pre, part = k.mlp_back(grad_down[c], save["slope"][c], w_up[depth], w_down[depth], [down_whole])
            grad_pre.append(pre)
            blocks.append(plan.exchange(part if first else gate(part, [image_cut])))
        up_whole = k.weight_grad("up_grad", save["h2"], [(one, None) for one in grad_pre], 1, 2, 0, None)
        side = []
        if not first:
            attn_sum, _ = plan.sum_levels(jnp.concatenate([attn_both, last_out], axis=0))
            side.append(attn_sum)
        up_whole = gate(up_whole, blocks + side)
        side.append(up_whole)
        for c in chunks:
            grads[c], got, sums = k.norm_back(
                mods, grads[c], blocks[c], save["x1"][c], (depth, 4), save["branch"][c], (depth, 2), side
            )
            sums2.append(sums)
            grad_out.append(plan.exchange(got))
        up_both = plan.scatter_weights(up_whole)
        down_sum, _ = plan.sum_levels(down_both)
        side = [down_sum]
        if not first:
            attn_grads[depth + 1] = plan.join_sides(attn_sum)
            side.append(attn_grads[depth + 1])
        grad_heads = None
        for c in chunks:
            grad_heads = k.project_back(grad_out[c], *w_out[depth], c, grad_heads, side)
        rights = [(save["heads"], lambda kind, c=c: (c,)) for c in chunks]
        out_whole = k.weight_grad("out_grad", grad_out, rights, 1, 2, 0, None, [grad_heads])
        out_both = plan.scatter_weights(out_whole[..., :features])
        grad_qkv = k.attend_back(save["joint"], mask, grad_heads, [out_whole])
        up_sum, _ = plan.sum_levels(up_both)
        if first:
            last_blocks = [plan.exchange(gate(part, [grad_heads])) for part in parts]
            down_grads[depth] = plan.join_sides(down_sum)
            side = [up_sum, down_grads[depth]] + last_blocks
        else:
            down_grads[depth] = plan.join_sides(down_sum)
            side = [up_sum, down_grads[depth]]
        rights = [(grad_qkv, lambda kind, c=c: (kind, c)) for c in chunks]
        attn_whole = k.weight_grad("qkv_grad", save["h1"], rights, 3, 6, 0, None, [] if first else side)
        if not depth:
            side.append(attn_whole)
        for c in chunks:
            blocks[c] = plan.exchange(k.qkv_back(grad_qkv, w_qkv[depth], c, side))
        side = []
        if first:
            image_rows = []
            for c in chunks:
                x2, down = k.norm_in(mods, save["x1"][c], last_blocks[c], (depth, 5))
                image_rows.append(x2)
                save["down"].append(down)
            image_rows = jnp.concatenate(image_rows, axis=0)
            side.append(image_rows)
        if depth:
            attn_whole = gate(attn_whole, blocks + side)
            side.append(attn_whole)
        else:
            out_sum, _ = plan.sum_levels(out_both)
            side.append(out_sum)
        attn_both = plan.scatter_weights(attn_whole[..., :features])
        for c in chunks:
            if depth:
                grads[c], got, sums = k.norm_back(
                    mods, grads[c], blocks[c], save["x"][c], (depth, 1), kept[depth - 1]["down"][c], (depth - 1, 5), side
                )
                next_down.append(plan.exchange(got))
            else:
                grads[c], sums = k.norm_back(mods, grads[c], blocks[c], save["x"][c], (depth, 1), after=side)
            sums1.append(sums)
        last_out = out_both
        if first:
            gate2 = []
            for c in chunks:
                moved = start[c] * save["down"][c]
                sums = jnp.stack([jnp.sum(moved[: k.ci], axis=0), jnp.sum(moved[k.ci :], axis=0)])
                gate2.append(jnp.broadcast_to(sums[:, None], (2, 3, D)))
        first_, second, gates = sum(sums1), sum(sums2), sum(gate2)
        mod_grads[depth] = jnp.stack(
            [first_[:, 0], first_[:, 1], second[:, 2], second[:, 0], second[:, 1], gates[:, 2]], axis=1
        )
        gate2, grad_down = sums1, next_down
    up_grads[0] = plan.join_sides(up_sum)
    attn_sum, _ = plan.sum_levels(attn_both)
    attn_grads[0] = plan.join_sides(jnp.concatenate([attn_sum, out_sum], axis=0))
    mod_part = plan.natural(jnp.stack(mod_grads)).reshape(LAYERS, 2, 6, cols, features)
    mod_part = jnp.transpose(mod_part, (3, 1, 0, 2, 4)).reshape(cols, -1)
    mod_col = plan.vectors_cols_back(mod_part)
    cut, _ = plan.rows_home_again(jnp.concatenate(grads, axis=0), fast, [mod_col])
    grad_image, grad_text = from_blocks(cut)
    mod_all = plan.vectors_rows_back(gate(mod_col, [cut, attn_sum])).astype(BF16)
    mod_all = mod_all.reshape(rows_count, 2, LAYERS * 6, features)
    mod_cut = [unsort_vectors(mod_all[:, s], 6) for s in range(2)]
    grad_mod = [tn(cond_mine, cut) for cut in mod_cut]
    cond_part = nt(mod_cut[0], mod_image) + nt(mod_cut[1], mod_text)
    cond_part = jnp.broadcast_to(cond_part[:, None], (rows_count, cols, width_rows)).reshape(-1, width_rows)
    cond_sum = lax.all_to_all(cond_part, ("row", "col"), 0, 0, tiled=True)
    cond_sum = jnp.sum(cond_sum.reshape(rows_count, cols, width_rows), axis=1)
    _, silu_pull = jax.vjp(jax.nn.silu, cond_float)
    grad_cond = silu_pull(cond_sum.reshape(1, D))[0]

    grad_qkv_w = [
        merge_columns([[attn_grads[d][2 * kind + s] for kind in range(3)] for d in range(LAYERS)], 3)
        for s in range(2)
    ]
    grad_out_w = [merge_columns([[attn_grads[d][6 + s]] for d in range(LAYERS)], 1) for s in range(2)]
    layered = [
        jnp.stack([grads_[d][s].astype(F32) for d in range(LAYERS)]) for grads_ in (up_grads, down_grads) for s in range(2)
    ]
    return (
        image_out,
        text_out,
        grad_image.astype(F32),
        grad_text.astype(F32),
        grad_cond,
        grad_mod[0],
        grad_mod[1],
        grad_qkv_w[0],
        grad_qkv_w[1],
        grad_out_w[0],
        grad_out_w[1],
        layered[0],
        layered[1],
        layered[2],
        layered[3],
    )


def solution(mesh):
    flat = P("row", "col")
    layered = P(None, "row", "col")
    return jax.shard_map(
        functools.partial(on_device, mesh.shape["row"], mesh.shape["col"]),
        mesh=mesh,
        in_specs=(flat, flat, P("row", None)) + (flat,) * 6 + (layered,) * 4 + (flat, flat),
        out_specs=(flat,) * 4 + (P("row", None),) + (flat,) * 6 + (layered,) * 4,
        check_vma=False,
    )
```

```python
import functools
import math

import jax
import jax.numpy as jnp
from jax import lax
from jax.experimental import pallas as pl
from jax.experimental.pallas import tpu as pltpu
from jax.sharding import PartitionSpec as P

D = 1536
HEAD = 64
IMG_LEN = 1024
TXT_LEN = 154
LAYERS = 2
EPS = 1e-06
CHUNKS = 1
F32 = jnp.float32
BF16 = jnp.bfloat16


def dot(a, b, ca, cb):
    return lax.dot_general(a, b, (((ca,), (cb,)), ((), ())), preferred_element_type=F32)


def nn(a, b):
    return dot(a, b, 1, 0)


def nt(a, b):
    return dot(a, b, 1, 1)


def tn(a, b):
    return dot(a, b, 0, 0)


class Plan:
    def __init__(self, rows, cols, swap):
        self.rows, self.cols, self.swap = rows, cols, swap
        half = cols // 2
        self.row, self.col = lax.axis_index("row"), lax.axis_index("col")
        self.a, self.x, self.k = self.row // 4, (self.row // 2) % 2, self.row % 2
        self.h, self.l = self.col // half, self.col % half
        self.member = self.x * half + self.l if swap else self.col

        def flat(a, x, k, h, l):
            return (a * 4 + x * 2 + k) * cols + h * half + l

        if swap:
            sides = [(a, k) for a in range(rows // 4) for k in range(2)]
            self.team = [
                [flat(a, x, k, h, l) for x in range(2) for l in range(half)] for a, k in sides for h in range(2)
            ]
            self.plane = [
                [flat(a, x, k, h, l) for x in range(2) for h in range(2) for l in range(half)] for a, k in sides
            ]
            self.home = [(flat(a, x, k, 1 - x, l), flat(a, x, k, x, l)) for a, k in sides for x in range(2) for l in range(half)]
            self.across = [(r, r ^ 2) for r in range(rows)]
            self.levels = [(c, (c + half) % cols) for c in range(cols)]
            self.fetch = [[a * 4 + x * 2 + k for a, k in sides] for x in range(2)]

    def exchange(self, blocks):
        if self.swap:
            return lax.all_to_all(
                blocks, ("row", "col"), 0, 0, tiled=True, axis_index_groups=self.team
            )
        return lax.all_to_all(blocks, "col", 0, 0, tiled=True)


    def inner(self, natural):
        if not self.swap:
            return natural
        lead = natural.shape[:-1]
        cut = natural.reshape(lead + (self.rows // 4, 2, 2, D // self.rows))
        return jnp.swapaxes(cut, -3, -2).reshape(lead + (D,))

    natural = inner

    def pick(self, index, pair):
        return jnp.where(index == 0, pair[0], pair[1]), jnp.where(index == 0, pair[1], pair[0])

    def place(self, index, mine, other):
        return jnp.where(index == 0, mine, other), jnp.where(index == 0, other, mine)

    def swap_sides(self, pieces, after=()):
        mine = jnp.stack(pieces)
        if not self.swap:
            return mine
        wide = mine.shape[2] // 2
        mine, other = self.pick(self.x, [mine[:, :, :wide], mine[:, :, wide:]])
        if len(after):
            other = gate(other, after)
        return jnp.concatenate(self.place(self.x, mine, lax.ppermute(other, "row", self.across)), axis=1)

    def swap_levels(self, both, after=()):
        if not self.swap:
            return both
        h = tick(self.h, after) if len(after) else self.h
        return jnp.concatenate(self.place(h, both, lax.ppermute(both, "col", self.levels)), axis=2)

    def gather_weights(self, both):
        if not self.swap:
            return lax.all_gather(both, "row", axis=0)
        return lax.all_gather(both, "row", axis=0, axis_index_groups=self.fetch)

    def scatter_weights(self, whole):
        groups = self.fetch if self.swap else None
        return lax.psum_scatter(whole, "row", scatter_dimension=0, tiled=True, axis_index_groups=groups)[0]

    def sum_levels(self, both):
        if not self.swap:
            return both, both
        wide = both.shape[2] // 2
        mine, other = self.pick(self.h, [both[:, :, :wide], both[:, :, wide:]])
        return (mine.astype(F32) + lax.ppermute(other, "col", self.levels).astype(F32)).astype(BF16), other

    def join_sides(self, both):
        if not self.swap:
            return both
        rows = both.shape[1] // 2
        mine, other = self.pick(self.x, [both[:, :rows], both[:, rows:]])
        return jnp.concatenate(self.place(self.x, mine, lax.ppermute(other, "row", self.across)), axis=2)

    def rows_home(self, blocks):
        if not self.swap:
            return blocks
        moved = lax.ppermute(blocks, ("row", "col"), self.home)
        return jnp.stack(self.place(self.h, blocks, moved), axis=1)

    def rows_in(self, pair, kernels, after=()):
        got = self.exchange(pair)
        if self.swap and kernels is not None:
            return got, kernels.enter(self, got.reshape((2, 2) + got.shape[1:]), (1, 0), after)
        if not self.swap:
            return got, jnp.transpose(got, (1, 0, 2)).reshape(got.shape[1], D)
        got = got.reshape((2, self.cols // 2) + got.shape[1:])
        got = jnp.where(self.h == 0, got[0], got[1])
        return got, self.inner(jnp.transpose(got, (2, 1, 0, 3)).reshape(got.shape[2], D))

    def rows_over(self, blocks, kernels):
        if not self.swap or kernels is None:
            return self.rows_in(self.rows_home(blocks), kernels)[1]
        cut = blocks.reshape((2, 1, self.cols // 2) + blocks.shape[1:])
        cut = jnp.broadcast_to(cut, (2, 2) + cut.shape[2:]).reshape((2 * self.cols,) + blocks.shape[1:])
        got = lax.all_to_all(cut, ("row", "col"), 0, 0, tiled=True, axis_index_groups=self.plane)
        return kernels.enter(self, got.reshape((2, 2, self.cols // 2) + blocks.shape[1:]), (0, 1))

    def rows_home_again(self, own, kernels, extra=None, second=()):
        if not self.swap or kernels is None:
            return self.rows_back(self.rows_out(own, kernels))
        cut = kernels.leave(own)
        tokens = cut.shape[2]
        if extra is not None:
            more = jnp.broadcast_to(extra.astype(BF16)[None], (2,) + extra.shape)
            cut = jnp.concatenate([cut, more], axis=2)
        cut = cut.reshape((2 * self.cols,) + cut.shape[2:])
        got = lax.all_to_all(cut, ("row", "col"), 0, 0, tiled=True, axis_index_groups=self.plane)
        got = got.reshape((2, 2, self.cols // 2) + got.shape[1:])
        x = tick(self.x, second) if len(second) else self.x
        rows = jnp.where(x == 0, got[:, 0, :, :tokens], got[:, 1, :, :tokens])
        rows = rows.reshape((self.cols,) + rows.shape[2:])
        if extra is None:
            return rows
        return rows, jnp.sum(got[:, :, :, tokens:].astype(F32), axis=(0, 2))

    def vectors_near(self, mine):
        every = jnp.broadcast_to(mine[None], (self.rows // 2,) + mine.shape)
        every = lax.all_to_all(every, "row", 0, 0, tiled=True, axis_index_groups=self.fetch)
        every = every.reshape((self.rows // 4, 2) + mine.shape)
        return jnp.swapaxes(every, 1, 2).reshape(self.rows, -1)

    def rows_out(self, own, kernels):
        tokens, own = own.shape[0], own.astype(BF16)
        if not self.swap:
            return self.exchange(jnp.transpose(own.reshape(tokens, self.cols, -1), (1, 0, 2)))
        cut = self.natural(own).reshape(tokens, 2, self.cols // 2, D // self.cols)
        cut = jnp.transpose(cut, (2, 1, 0, 3))
        return self.exchange(jnp.concatenate([cut, cut], axis=0))

    def rows_back(self, got):
        if not self.swap:
            return got
        mine, other = self.pick(self.h, [got[:, 0], got[:, 1]])
        back = lax.ppermute(other, ("row", "col"), [(b, a) for a, b in self.home])
        return jnp.where(self.x == self.h, mine, back)

    def vectors_rows(self, part):
        if not self.swap:
            return jnp.sum(lax.all_to_all(part, "row", 0, 0, tiled=True), axis=0, keepdims=True)
        cut = part.reshape(self.rows // 4, 1, 2, 2, -1)
        cut = jnp.broadcast_to(cut, (self.rows // 4, 2) + cut.shape[2:])
        sent = jnp.transpose(cut, (0, 1, 3, 2, 4)).reshape(self.rows, 2, -1)
        return jnp.sum(lax.all_to_all(sent, "row", 0, 0, tiled=True), axis=0)

    def vectors_cols(self, mine):
        if not self.swap:
            return lax.all_to_all(jnp.broadcast_to(mine, (self.cols, mine.shape[1])), "col", 0, 0, tiled=True)
        half = self.cols // 2
        sent = jnp.broadcast_to(mine[:, None], (2, half, mine.shape[1])).reshape(self.cols, -1)
        return lax.all_to_all(sent, "col", 0, 0, tiled=True)

    def vectors_cols_back(self, part):
        got = lax.all_to_all(part, "col", 0, 0, tiled=True)
        if not self.swap:
            return jnp.sum(got, axis=0, keepdims=True)
        return jnp.sum(got.reshape(2, self.cols // 2, -1), axis=1)

    def vectors_rows_back(self, mine):
        every = lax.all_to_all(jnp.broadcast_to(mine[None], (self.rows,) + mine.shape), "row", 0, 0, tiled=True)
        if not self.swap:
            return every.reshape(self.rows, -1)
        every = jnp.sum(every.reshape(self.rows // 4, 2, 2, 2, -1), axis=1)
        return jnp.transpose(every, (0, 2, 1, 3)).reshape(self.rows, -1)

def norm(x):
    average = jnp.mean(x, axis=1, keepdims=True)
    centred = x - average
    inverse = lax.rsqrt(jnp.mean(centred * centred, axis=1, keepdims=True) + EPS)
    return centred * inverse, inverse


def call(kernel, name, grid, ins, outs, flops=0, after=(), alias=None, scratch=(), transcendentals=0, room=58):
    args = [a for a, _, _ in ins]
    in_specs = [pl.BlockSpec(block, index) for _, block, index in ins]
    extra = list(after)
    aliases = {}
    if alias is not None:
        aliases = {len(args): 0}
        extra = [alias] + extra
    given = len(args)

    def body(*refs):
        kernel(*refs[:given], *refs[given + len(extra) :])

    moved = sum(a.size * a.dtype.itemsize for a in args)
    for shape, dtype, _, _ in outs:
        moved += math.prod(shape) * jnp.dtype(dtype).itemsize
    got = pl.pallas_call(
        body,
        grid=grid,
        in_specs=in_specs + [pl.BlockSpec(memory_space=pl.ANY)] * len(extra),
        out_specs=[pl.BlockSpec(block, index) for _, _, block, index in outs],
        out_shape=[jax.ShapeDtypeStruct(shape, dtype) for shape, dtype, _, _ in outs],
        scratch_shapes=list(scratch),
        input_output_aliases=aliases,
        compiler_params=pltpu.CompilerParams(vmem_limit_bytes=room << 20),
        cost_estimate=pl.CostEstimate(
            flops=flops // 8, bytes_accessed=moved // 8, transcendentals=transcendentals // 8
        ),
        name=name,
    )(*args, *extra)
    return got[0] if len(got) == 1 else got


def tick(index, after):
    def kernel(given, out):
        out[...] = given[...]

    one = jnp.full((8, 128), index, jnp.int32)
    whole = ((8, 128), lambda i: (0, 0))
    return call(kernel, "tick", (1,), [(one,) + whole], [((8, 128), jnp.int32) + whole], after=after)[0, 0]


def gate(array, after):
    def kernel(*refs):
        pass

    return pl.pallas_call(
        kernel,
        in_specs=[pl.BlockSpec(memory_space=pl.ANY)] * (1 + len(after)),
        out_specs=pl.BlockSpec(memory_space=pl.ANY),
        out_shape=jax.ShapeDtypeStruct(array.shape, array.dtype),
        input_output_aliases={0: 0},
        cost_estimate=pl.CostEstimate(flops=0, bytes_accessed=1024, transcendentals=0),
        name="gate",
    )(array, *after)


class Kernels:
    def __init__(self, members, ci, ct, chunks, groups, wide, hidden):
        self.q, self.ci, self.ct, self.rc, self.n = members, ci, ct, ci + ct, chunks
        self.g, self.dr = groups, D // groups
        self.wide, self.hidden = wide, hidden
        self.tokens = members * self.rc * chunks

    def rows(self, array, columns, index, lead=None):
        if lead is None:
            return [(array, (self.q, self.rc, columns), lambda *i: (0, 0, index(*i)))]
        return [(array, (1,) * len(lead(0)) + (self.q, self.rc, columns), lambda *i: lead(*i) + (0, 0, index(*i)))]

    def image(self, ref):
        value = ref[..., : self.ci, :]
        return value.reshape(-1, value.shape[-1])

    def text(self, ref):
        value = ref[..., self.ci :, :]
        return value.reshape(-1, value.shape[-1])

    def weight(self, array, columns, piece, index):
        return [
            (array, (self.g, 1, self.dr, columns), lambda *i, s=s: (0, piece(*i) + s, 0, index(*i))) for s in range(2)
        ]

    def flat(self, ref):
        value = ref[...]
        return value.reshape(-1, value.shape[-1])

    def put(self, ref, img, txt):
        cut = ref.shape[:-2]
        ref[..., : self.ci, :] = img.astype(ref.dtype).reshape(cut + (self.ci, ref.shape[-1]))
        ref[..., self.ci :, :] = txt.astype(ref.dtype).reshape(cut + (self.ct, ref.shape[-1]))

    def qkv(self, h, weights, chunk, joint, after=()):
        def kernel(h, wi, wt, out):
            self.put(out, nn(self.image(h), self.flat(wi)), nn(self.text(h), self.flat(wt)))

        return call(
            kernel,
            "qkv",
            (3,),
            self.rows(h, D, lambda j: 0) + self.weight(weights, self.wide, lambda j: 2 * j, lambda j: 0),
            [
                (
                    (self.n, self.q, self.rc, 3 * self.wide),
                    BF16,
                    (1, self.q, self.rc, self.wide),
                    lambda j: (chunk, 0, 0, j),
                )
            ],
            flops=2 * self.q * self.rc * D * 3 * self.wide,
            alias=joint,
            after=after,
        )

    def project(self, heads, weights, piece, chunk, after=()):
        def kernel(h, wi, wt, out):
            self.put(out, nt(self.image(h), self.flat(wi)), nt(self.text(h), self.flat(wt)))

        return call(
            kernel,
            "project",
            (1,),
            self.rows(heads, self.wide, lambda i: 0, lambda i: (chunk,))
            + self.weight(weights, self.wide, lambda i: piece, lambda i: 0),
            [((self.q, self.rc, D), BF16, (self.q, self.rc, D), lambda i: (0, 0, 0))],
            flops=2 * self.q * self.rc * D * self.wide,
            after=after,
        )

    def project_back(self, grad, weights, piece, chunk, joint, after=()):
        def kernel(h, wi, wt, out):
            self.put(out, nn(self.image(h), self.flat(wi)), nn(self.text(h), self.flat(wt)))

        return call(
            kernel,
            "project_back",
            (1,),
            self.rows(grad, D, lambda i: 0) + self.weight(weights, self.wide, lambda i: piece, lambda i: 0),
            [
                (
                    (self.n, self.q, self.rc, self.wide),
                    BF16,
                    (1, self.q, self.rc, self.wide),
                    lambda i: (chunk, 0, 0, 0),
                )
            ],
            flops=2 * self.q * self.rc * D * self.wide,
            alias=joint,
            after=after,
        )

    def qkv_back(self, grads, weights, chunk, after=()):
        def kernel(h, wi, wt, out, sum_i, sum_t):
            j = pl.program_id(0)
            img, txt = nt(self.image(h), self.flat(wi)), nt(self.text(h), self.flat(wt))

            @pl.when(j == 0)
            def _():
                sum_i[...] = img
                sum_t[...] = txt

            @pl.when(j == 1)
            def _():
                sum_i[...] += img
                sum_t[...] += txt

            @pl.when(j == 2)
            def _():
                self.put(out, sum_i[...] + img, sum_t[...] + txt)

        return call(
            kernel,
            "qkv_back",
            (3,),
            self.rows(grads, self.wide, lambda j: 0, lambda j: (j, chunk))
            + self.weight(weights, self.wide, lambda j: 2 * j, lambda j: 0),
            [((self.q, self.rc, D), BF16, (self.q, self.rc, D), lambda j: (0, 0, 0))],
            flops=2 * self.q * self.rc * D * 3 * self.wide,
            after=after,
            scratch=[pltpu.VMEM((self.q * self.ci, D), F32), pltpu.VMEM((self.q * self.ct, D), F32)],
        )

    def mlp(self, h, ups, downs, after=()):
        steps = 3
        block = self.hidden // steps

        def gelu(v):
            inner = 0.7978845608028654 * (v + 0.044715 * v * v * v)
            t = jnp.tanh(inner)
            half = 0.5 * (1.0 + t)
            slope = half + 0.5 * v * (1.0 - t * t) * (0.7978845608028654 * (1.0 + 3 * 0.044715 * v * v))
            return (v * half).astype(BF16), slope.astype(BF16)

        def kernel(h, ui, ut, di, dt, act, slope, out, sum_i, sum_t):
            j = pl.program_id(0)
            gi, si = gelu(nn(self.image(h), self.flat(ui)))
            gt, st = gelu(nn(self.text(h), self.flat(ut)))
            self.put(act, gi, gt)
            self.put(slope, si, st)
            img, txt = nt(gi, self.flat(di)), nt(gt, self.flat(dt))

            @pl.when(j == 0)
            def _():
                sum_i[...] = img
                sum_t[...] = txt

            @pl.when(jnp.logical_and(j > 0, j < steps - 1))
            def _():
                sum_i[...] += img
                sum_t[...] += txt

            @pl.when(j == steps - 1)
            def _():
                self.put(out, sum_i[...] + img, sum_t[...] + txt)

        return call(
            kernel,
            "mlp",
            (steps,),
            self.rows(h, D, lambda j: 0)
            + self.weight(ups, block, lambda j: 0, lambda j: j)
            + self.weight(downs, block, lambda j: 0, lambda j: j),
            [
                ((self.q, self.rc, self.hidden), BF16, (self.q, self.rc, block), lambda j: (0, 0, j)),
                ((self.q, self.rc, self.hidden), BF16, (self.q, self.rc, block), lambda j: (0, 0, j)),
                ((self.q, self.rc, D), BF16, (self.q, self.rc, D), lambda j: (0, 0, 0)),
            ],
            flops=4 * self.q * self.rc * D * self.hidden,
            transcendentals=self.q * self.rc * self.hidden,
            after=after,
            scratch=[pltpu.VMEM((self.q * self.ci, D), F32), pltpu.VMEM((self.q * self.ct, D), F32)],
        )

    def mlp_back(self, grad, slope, ups, downs, after=()):
        steps = 3
        block = self.hidden // steps

        def kernel(h, s, ui, ut, di, dt, pre, out, sum_i, sum_t):
            j = pl.program_id(0)
            pi = (nn(self.image(h), self.flat(di)) * self.image(s).astype(F32)).astype(BF16)
            pt = (nn(self.text(h), self.flat(dt)) * self.text(s).astype(F32)).astype(BF16)
            self.put(pre, pi, pt)
            img, txt = nt(pi, self.flat(ui)), nt(pt, self.flat(ut))

            @pl.when(j == 0)
            def _():
                sum_i[...] = img
                sum_t[...] = txt

            @pl.when(jnp.logical_and(j > 0, j < steps - 1))
            def _():
                sum_i[...] += img
                sum_t[...] += txt

            @pl.when(j == steps - 1)
            def _():
                self.put(out, sum_i[...] + img, sum_t[...] + txt)

        return call(
            kernel,
            "mlp_back",
            (steps,),
            self.rows(grad, D, lambda j: 0)
            + self.rows(slope, block, lambda j: j)
            + self.weight(ups, block, lambda j: 0, lambda j: j)
            + self.weight(downs, block, lambda j: 0, lambda j: j),
            [
                ((self.q, self.rc, self.hidden), BF16, (self.q, self.rc, block), lambda j: (0, 0, j)),
                ((self.q, self.rc, D), BF16, (self.q, self.rc, D), lambda j: (0, 0, 0)),
            ],
            flops=4 * self.q * self.rc * D * self.hidden,
            after=after,
            scratch=[pltpu.VMEM((self.q * self.ci, D), F32), pltpu.VMEM((self.q * self.ct, D), F32)],
        )

    def weight_grad(self, name, left, right, kinds, pieces, first, whole, after=()):
        columns = right[0][0].shape[-1]

        def rows(refs, side):
            got = [self.text(ref) if side else self.image(ref) for ref in refs]
            return got[0] if len(got) == 1 else jnp.concatenate(got, axis=0)

        if self.dr % 128:
            cut = []
            for kind in range(kinds):
                for side in (slice(0, self.ci), slice(self.ci, self.rc)):
                    a = jnp.concatenate([one[:, side].reshape(-1, D) for one in left], axis=0)
                    b = [one[lead(kind)] if lead else one for one, lead in right]
                    b = jnp.concatenate([one[:, side].reshape(-1, columns) for one in b], axis=0)
                    cut.append(tn(a, b).astype(BF16).reshape(self.g, self.dr, columns))
            cut = jnp.stack(cut, axis=1)
            return cut if whole is None else jnp.concatenate([whole, cut], axis=1)

        def kernel(*refs):
            ins, out = refs[:-1], refs[-1]
            for side in range(2):
                a, b = rows(ins[: self.n], side), rows(ins[self.n :], side)
                out[0, side] = tn(a, b).astype(BF16)

        ins = []
        for one in left:
            ins += self.rows(one, self.dr, lambda j, g: g)
        for one, lead in right:
            ins += self.rows(one, columns, lambda j, g: 0, (lambda j, g=0, lead=lead: lead(j)) if lead else None)
        return call(
            kernel,
            name,
            (kinds, self.g),
            ins,
            [
                (
                    (self.g, pieces, self.dr, columns),
                    BF16,
                    (1, 2, self.dr, columns),
                    lambda j, g: (g, first // 2 + j, 0, 0),
                )
            ],
            flops=2 * self.tokens * D * columns * kinds,
            alias=whole,
            after=after,
        )

    def norm_in(self, mods, x, blocks=None, gate=None, after_norm=None, after=()):
        rows = self.ci // 4

        def kernel(*refs):
            refs = list(refs)
            value = refs.pop(0)[...]
            if blocks is not None:
                added = jnp.sum(refs.pop(0)[...].astype(F32), axis=0)
                value = value + refs.pop(0)[0, gate[1] : gate[1] + 1] * added
            vectors = refs.pop(0) if after_norm is not None else None
            if blocks is not None:
                refs.pop(0)[...] = value
                refs.pop(0)[...] = added
            if after_norm is not None:
                kind = after_norm[1]
                normed = norm(value)[0]
                out = (normed * (1.0 + vectors[0, kind + 1 : kind + 2]) + vectors[0, kind : kind + 1]).astype(BF16)
                refs[0][...] = jnp.broadcast_to(out[None], refs[0].shape)

        ratio = 4

        def vectors(depth):
            return (mods, (1,) + mods.shape[1:], lambda i: (depth * 2 + i // ratio, 0, 0))

        flat = ((rows, D), lambda i: (i, 0))
        many = ((self.q, rows, D), lambda i: (0, i, 0))
        ins, outs = [(x,) + flat], []
        if blocks is not None:
            ins += [(blocks,) + many, vectors(gate[0])]
            outs += [((self.rc, D), F32) + flat] * 2
        if after_norm is not None:
            ins.append(vectors(after_norm[0]))
            outs.append(((self.q, self.rc, D), BF16) + many)
        return call(kernel, "norm_in", (ratio + 1,), ins, outs, flops=20 * self.rc * D, after=after)

    def norm_back(self, mods, grad, blocks=None, x=None, scale=None, branch=None, gate=None, after=()):
        rows, ratio = self.ci // 4, 4

        def kernel(*refs):
            refs = list(refs)
            i = pl.program_id(0)
            held = lax.broadcasted_iota(jnp.int32, (rows, 1), 0) < self.rc - i * rows

            def take():
                return jnp.where(held, refs.pop(0)[...], 0.0)

            value = take()
            rows_of_sums = []
            if blocks is not None:
                dh = jnp.where(held, jnp.sum(refs.pop(0)[...].astype(F32), axis=0), 0.0)
                normed, inverse = norm(take())
                dn = dh * (1.0 + refs.pop(0)[0, scale[1] : scale[1] + 1])
                value = value + inverse * (
                    dn
                    - jnp.mean(dn, axis=1, keepdims=True)
                    - normed * jnp.mean(dn * normed, axis=1, keepdims=True)
                )
                rows_of_sums += [(0, jnp.sum(dh, axis=0, keepdims=True)), (1, jnp.sum(dh * normed, axis=0, keepdims=True))]
            if branch is not None:
                rows_of_sums.append((2, jnp.sum(value * take(), axis=0, keepdims=True)))
            if gate is not None:
                factor = refs.pop(0)[0, gate[1] : gate[1] + 1]
            if blocks is not None:
                refs.pop(0)[...] = value
            if gate is not None:
                out = refs.pop(0)
                out[...] = jnp.broadcast_to((factor * value).astype(BF16)[None], out.shape)
            if not rows_of_sums:
                return
            sums = refs.pop(0)
            start = jnp.logical_or(i == 0, i == ratio)

            @pl.when(start)
            def _():
                for at, row in rows_of_sums:
                    sums[0, at : at + 1] = row

            @pl.when(jnp.logical_not(start))
            def _():
                for at, row in rows_of_sums:
                    sums[0, at : at + 1] += row

        def vectors(depth):
            return (mods, (1,) + mods.shape[1:], lambda i: (depth * 2 + i // ratio, 0, 0))

        flat = ((rows, D), lambda i: (i, 0))
        many = ((self.q, rows, D), lambda i: (0, i, 0))
        ins, outs = [(grad,) + flat], []
        if blocks is not None:
            ins += [(blocks,) + many, (x,) + flat, vectors(scale[0])]
            outs.append(((self.rc, D), F32) + flat)
        if branch is not None:
            ins.append((branch,) + flat)
        if gate is not None:
            ins.append(vectors(gate[0]))
            outs.append(((self.q, self.rc, D), BF16) + many)
        if blocks is not None or branch is not None:
            outs.append(((2, 8, D), F32, (1, 8, D), lambda i: (i // ratio, 0, 0)))
        return call(kernel, "norm_back", (ratio + 1,), ins, outs, flops=30 * self.rc * D, after=after)

    def enter(self, plan, got, order, after=()):
        rows, half = self.ci // 4, D // self.g // 2
        wide = got.shape[-1]

        def kernel(index, ref, out):
            first = index[0:1, 0:1] == 0
            for a in range(2):
                for x in range(2):
                    at = (a, x) if order[0] == 0 else (x, a)
                    piece = jnp.where(first, ref[(0,) + at].astype(F32), ref[(1,) + at].astype(F32))
                    for side in range(2):
                        at = (a * 4 + side * 2 + x) * half
                        out[:, at : at + half] = piece[:, side * half : (side + 1) * half]

        return call(
            kernel,
            "enter",
            (-(-self.rc // rows),),
            [
                (jnp.full((8, 128), plan.h, jnp.int32), (8, 128), lambda i: (0, 0)),
                (got, (2, 2, 2, rows, wide), lambda i: (0, 0, 0, i, 0)),
            ],
            [((self.rc, D), F32, (rows, D), lambda i: (i, 0))],
            flops=self.rc * D,
            after=after,
        )

    def leave(self, own, after=()):
        rows, half = self.ci // 4, D // self.g // 2
        wide = D // self.q

        def kernel(ref, out):
            for a in range(2):
                for x in range(2):
                    at = [(a * 4 + side * 2 + x) * half for side in range(2)]
                    piece = jnp.concatenate([ref[:, i : i + half] for i in at], axis=1).astype(BF16)
                    for side in range(2):
                        out[side, 2 * a + x] = piece

        return call(
            kernel,
            "leave",
            (-(-self.rc // rows),),
            [(own, (rows, D), lambda i: (i, 0))],
            [((2, self.q, self.rc, wide), BF16, (2, self.q, rows, wide), lambda i: (0, 0, i, 0))],
            flops=self.rc * D,
            after=after,
        )

    def masks(self):
        at = lax.broadcasted_iota(jnp.int32, (self.n, self.q, self.rc), 2)
        chunk = lax.broadcasted_iota(jnp.int32, (self.n, self.q, self.rc), 0)
        member = lax.broadcasted_iota(jnp.int32, (self.n, self.q, self.rc), 1)
        text = member * (self.ct * self.n) + chunk * self.ct + at - self.ci
        absent = jnp.logical_and(at >= self.ci, text >= TXT_LEN)
        return jnp.where(absent, -1e30, 0.0).astype(BF16).reshape(self.tokens, 1)

    def attend(self, joint, mask, after=()):
        t, pairs = self.tokens, self.wide // 128

        def kernel(q_ref, k_ref, v_ref, mask_ref, o_ref):
            q, k, v = q_ref[...], k_ref[...], v_ref[...]
            lane = lax.broadcasted_iota(jnp.int32, q.shape, 1)
            first = lane < HEAD
            none = jnp.zeros_like(q)
            bias = jnp.broadcast_to(mask_ref[...], k.shape)
            outs = []
            for side, spare in ((True, HEAD), (False, 0)):
                ones = jnp.where(lane == spare, jnp.ones_like(q), none)
                scaled = jnp.where(first == side, q * jnp.asarray(HEAD**-0.5, BF16), ones)
                scores = nt(scaled, jnp.where(first == side, k, bias))
                weights = jnp.exp(scores - jnp.max(scores, axis=1, keepdims=True))
                totals = jnp.sum(weights, axis=1, keepdims=True)
                outs.append(nn(weights.astype(BF16), v) * (1.0 / totals))
            o_ref[...] = jnp.where(first, outs[0], outs[1]).astype(BF16)

        flat = joint.reshape(t, 3 * self.wide)
        out = call(
            kernel,
            "attend",
            (pairs,),
            [(flat, (t, 128), lambda p, part=part: (0, part * pairs + p)) for part in range(3)]
            + [(mask, (t, 1), lambda p: (0, 0))],
            [((t, self.wide), BF16, (t, 128), lambda p: (0, p))],
            flops=pairs * 8 * t * t * 128,
            transcendentals=pairs * 2 * t * t,
            after=after,
            room=48,
        )
        return out.reshape(self.n, self.q, self.rc, self.wide)

    def attend_back(self, joint, mask, grad, after=()):
        t, pairs = self.tokens, self.wide // 128

        def kernel(q_ref, k_ref, v_ref, mask_ref, do_ref, out_ref):
            q, k, v, do = q_ref[...], k_ref[...], v_ref[...], do_ref[...]
            lane = lax.broadcasted_iota(jnp.int32, q.shape, 1)
            first = lane < HEAD
            none = jnp.zeros_like(q)
            bias = jnp.broadcast_to(mask_ref[...], k.shape)
            scale = jnp.asarray(HEAD**-0.5, BF16)
            dq = dk = dv = None
            for side, spare in ((True, HEAD), (False, 0)):
                mine = first == side
                ones = jnp.where(lane == spare, jnp.ones_like(q), none)
                scaled = q * scale
                grad_o = jnp.where(mine, do, none)
                scores = nt(jnp.where(mine, k, bias), jnp.where(mine, scaled, ones))
                weights = jnp.exp(scores - jnp.max(scores, axis=0, keepdims=True))
                chances = weights * (1.0 / jnp.sum(weights, axis=0, keepdims=True))
                grad_chances = nt(v, grad_o)
                centre = jnp.sum(grad_chances * chances, axis=0, keepdims=True)
                grad_scores = (chances * (grad_chances - centre)).astype(BF16)
                one_v = nn(chances.astype(BF16), grad_o)
                one_k = nn(grad_scores, jnp.where(mine, scaled, none))
                one_q = tn(jnp.where(mine, k * scale, none), grad_scores)
                dq, dk, dv = (one_q, one_k, one_v) if dq is None else (dq + one_q, dk + one_k, dv + one_v)
            out_ref[0] = jnp.transpose(dq).astype(BF16)
            out_ref[1] = dk.astype(BF16)
            out_ref[2] = dv.astype(BF16)

        flat = joint.reshape(t, 3 * self.wide)
        out = call(
            kernel,
            "attend_back",
            (pairs,),
            [(flat, (t, 128), lambda p, part=part: (0, part * pairs + p)) for part in range(3)]
            + [(mask, (t, 1), lambda p: (0, 0)), (grad.reshape(t, self.wide), (t, 128), lambda p: (0, p))],
            [((3, t, self.wide), BF16, (3, t, 128), lambda p: (0, 0, p))],
            flops=pairs * 20 * t * t * 128,
            transcendentals=pairs * 2 * t * t,
            after=after,
            room=56,
        )
        return out.reshape(3, self.n, self.q, self.rc, self.wide)


def order_matrix(block, kinds):
    width = block * LAYERS * kinds
    source = lax.broadcasted_iota(jnp.int32, (width, width), 0)
    target = lax.broadcasted_iota(jnp.int32, (width, width), 1)
    return (source == (target % block) * (LAYERS * kinds) + target // block).astype(BF16)


def split_columns(weight, kinds):
    rows = weight.shape[0]
    features = weight.shape[1] // (LAYERS * kinds)
    block = 128 if features % 128 == 0 else 64
    wide = block * LAYERS * kinds
    matrix = order_matrix(block, kinds)
    parts = [nn(weight[:, i * wide : (i + 1) * wide], matrix).astype(BF16) for i in range(features // block)]

    def one(at):
        return jnp.concatenate([part[:, at * block : (at + 1) * block] for part in parts], axis=1)

    return [[one(depth * kinds + kind) for kind in range(kinds)] for depth in range(LAYERS)]


def merge_columns(pieces, kinds):
    features = pieces[0][0].shape[1]
    block = 128 if features % 128 == 0 else 64
    matrix = order_matrix(block, kinds)
    parts = []
    for i in range(features // block):
        sorted_ = jnp.concatenate(
            [piece[:, i * block : (i + 1) * block] for layer in pieces for piece in layer], axis=1
        )
        parts.append(nt(sorted_, matrix))
    return jnp.concatenate(parts, axis=1)


def sort_vectors(part, kinds):
    rows = part.shape[0]
    features = part.shape[1] // (LAYERS * kinds)
    block = 128 if features % 128 == 0 else 64
    wide = block * LAYERS * kinds
    terms, rest = [], part
    for _ in range(3):
        term = lax.reduce_precision(rest, 8, 7)
        terms.append(term.astype(BF16))
        rest = rest - term
    matrix = order_matrix(block, kinds)
    cuts = jnp.concatenate(terms, axis=0)
    out = []
    for i in range(features // block):
        got = nn(cuts[:, i * wide : (i + 1) * wide], matrix).reshape(3, rows, LAYERS * kinds, block)
        out.append(got[0] + got[1] + got[2])
    return jnp.concatenate(out, axis=2)


def unsort_vectors(sorted_, kinds):
    rows, _, features = sorted_.shape
    block = 128 if features % 128 == 0 else 64
    matrix = order_matrix(block, kinds)
    out = [
        nt(sorted_[:, :, i * block : (i + 1) * block].reshape(rows, -1), matrix).astype(BF16)
        for i in range(features // block)
    ]
    return jnp.concatenate(out, axis=1)


def on_device(
    rows_count,
    cols,
    image_in,
    text_in,
    condition,
    mod_image,
    mod_text,
    qkv_image,
    qkv_text,
    out_image,
    out_text,
    up_image,
    up_text,
    down_image,
    down_text,
    cot_image,
    cot_text,
):
    features = D // cols
    swap = cols % 2 == 0 and rows_count % 4 == 0 and features % (2 * HEAD) == 0
    plan = Plan(rows_count, cols, swap)
    width_rows = mod_image.shape[0]
    img_own = IMG_LEN // cols
    txt_own = -(-TXT_LEN // (16 * cols)) * 16
    txt_pad = txt_own * cols
    wide = features + -features % 128
    k = Kernels(
        cols,
        img_own // CHUNKS,
        txt_own // CHUNKS,
        CHUNKS,
        rows_count // 2 if swap else rows_count,
        wide,
        up_image.shape[2],
    )
    chunks = range(CHUNKS)
    fast = k if swap and rows_count == 8 and cols == 4 and CHUNKS == 1 else None

    def filled(whole):
        return jnp.pad(whole, ((0, 0),) * 3 + ((0, wide - features),))

    qkv_shards = [split_columns(w, 3) for w in (qkv_image, qkv_text)]
    out_shards = [split_columns(w, 1) for w in (out_image, out_text)]
    w_attn, w_up, w_down = [], [], []
    def sides_attn(depth, after=()):
        pieces = [qkv_shards[s][depth][kind] for kind in range(3) for s in range(2)]
        return plan.swap_sides(pieces + [out_shards[s][depth][0] for s in range(2)], after)

    def sides_up(depth, after=()):
        return plan.swap_sides([up_image[depth], up_text[depth]], after)

    def sides_down(depth, after=()):
        return plan.swap_sides([down_image[depth], down_text[depth]], after)

    def to_blocks(image, text):
        img = jnp.transpose(image.reshape(features, IMG_LEN)).reshape(cols, CHUNKS, k.ci, features)
        txt = jnp.pad(jnp.transpose(text.reshape(features, TXT_LEN)), ((0, txt_pad - TXT_LEN), (0, 0)))
        blocks = jnp.concatenate([img, txt.reshape(cols, CHUNKS, k.ct, features)], axis=2)
        return blocks.reshape(cols, CHUNKS * k.rc, features)

    def to_own(own):
        own = own.astype(F32)
        return [own[c * k.rc : (c + 1) * k.rc] for c in chunks]

    def from_blocks(got):
        got = got.reshape(cols, CHUNKS, k.rc, features)
        img = got[:, :, : k.ci].reshape(IMG_LEN, features)
        txt = got[:, :, k.ci :].reshape(txt_pad, features)[:TXT_LEN]
        return jnp.transpose(img).reshape(1, -1), jnp.transpose(txt).reshape(1, -1)

    cond_float = condition.astype(F32)
    cond_low = jax.nn.silu(cond_float).astype(BF16)
    cond_cut = cond_low.reshape(rows_count, width_rows)
    cond_mine = lax.all_to_all(cond_cut, "row", 0, 0, tiled=True)
    mod_part = [nn(cond_mine, one) for one in (mod_image, mod_text)]
    mod_sorted = jnp.concatenate([sort_vectors(one, 6) for one in mod_part], axis=1)
    blocks = to_blocks(image_in, text_in)
    mod_row = plan.vectors_rows(mod_sorted.reshape(rows_count, -1))
    mod_cols = plan.vectors_cols(mod_row).reshape(cols, 2, LAYERS, 6, features)
    mods = plan.inner(jnp.transpose(mod_cols, (2, 1, 3, 0, 4)).reshape(LAYERS * 2, 6, D))

    mask = k.masks()
    own = plan.rows_over(gate(blocks, [mods]), fast)
    attn = sides_attn(0)
    up = sides_up(0, [attn])
    level = plan.swap_levels(attn, [own, up])
    w_qkv, w_out = [filled(plan.gather_weights(level[:6]))], [(filled(plan.gather_weights(level[6:])), 0)]
    x = to_own(own)
    sent = [k.norm_in(mods, x[c], after_norm=(0, 0)) for c in chunks]
    h1 = [plan.exchange(one) for one in sent]
    kept = []
    for depth in range(LAYERS):
        last = depth + 1 == LAYERS
        if not depth:
            down = sides_down(depth, sent)
        side = [plan.swap_levels(gate(up, x), h1 + [down])]
        w_up.append(plan.gather_weights(side[0]))
        joint = None
        for c in chunks:
            joint = k.qkv(h1[c], w_qkv[depth], c, joint, side)
        side = []
        if last:
            side = [k.norm_back(mods, grads[c], gate=(depth, 5)) for c in chunks]
            grad_down = [plan.exchange(one) for one in side]
        heads = k.attend(joint, mask, side)
        side = grad_down if last else []
        save = dict(x=x, h1=h1, joint=joint, heads=heads, branch=[], x1=[], h2=[], act=[], slope=[], down=[])
        next_x, next_h1 = [], []
        sent = [k.project(heads, *w_out[depth], c, side) for c in chunks]
        blocks = [plan.exchange(one) for one in sent]
        other = [] if last else [to_blocks(cot_image, cot_text), sides_attn(depth + 1, sent)]
        side = [plan.swap_levels(gate(down, sent), blocks + other)]
        w_down.append(plan.gather_weights(side[0]))
        sent = []
        for c in chunks:
            x1, branch, h2 = k.norm_in(mods, x[c], blocks[c], (depth, 2), (depth, 3), side)
            sent.append(h2)
            save["x1"].append(x1)
            save["branch"].append(branch)
            save["h2"].append(plan.exchange(h2))
        side = []
        if not last:
            up = sides_up(depth + 1, sent)
            pair = plan.rows_home(gate(other[0], sent))
            side = [up, pair]
        parts = []
        for c in chunks:
            act, slope, part = k.mlp(save["h2"][c], w_up[depth], w_down[depth], side)
            parts.append(part)
            save["act"].append(act)
            save["slope"].append(slope)
        kept.append(save)
        if last:
            break
        got, grads = plan.rows_in(gate(pair, save["h2"] + [up]), fast, save["act"])
        grads = to_own(grads)
        blocks = [plan.exchange(gate(part, [got])) for part in parts]
        down = sides_down(depth + 1, save["act"])
        side = [plan.swap_levels(gate(other[1], save["act"]), blocks + [down, *grads])]
        whole = filled(plan.gather_weights(side[0]))
        w_qkv.append(whole)
        w_out.append((whole, 6))
        sent = []
        for c in chunks:
            got = k.norm_in(mods, save["x1"][c], blocks[c], (depth, 5), (depth + 1, 0), side)
            next_x.append(got[0])
            save["down"].append(got[1])
            sent.append(got[2])
            next_h1.append(plan.exchange(got[2]))
        x, h1 = next_x, next_h1

    start = list(grads)
    mod_grads = [None] * LAYERS
    attn_grads, up_grads, down_grads = [None] * LAYERS, [None] * LAYERS, [None] * LAYERS
    for depth in reversed(range(LAYERS)):
        first = depth + 1 == LAYERS
        save = kept[depth]
        grad_pre, blocks, grad_out, sums2, sums1, next_down = ([] for _ in range(6))
        side = []
        if not first:
            up_grads[depth + 1] = plan.join_sides(up_sum)
            side = [up_grads[depth + 1]]
        if not first:
            image_cut = plan.rows_home_again(gate(image_rows, grad_down), fast)
            image_out, text_out = from_blocks(image_cut)
        down_whole = k.weight_grad("down_grad", grad_down, [(one, None) for one in save["act"]], 1, 2, 0, None, side)
        down_both = plan.scatter_weights(down_whole)
        for c in chunks:
            pre, part = k.mlp_back(grad_down[c], save["slope"][c], w_up[depth], w_down[depth], [down_whole])
            grad_pre.append(pre)
            blocks.append(plan.exchange(part if first else gate(part, [image_cut])))
        up_whole = k.weight_grad("up_grad", save["h2"], [(one, None) for one in grad_pre], 1, 2, 0, None)
        side = []
        if not first:
            attn_sum, _ = plan.sum_levels(jnp.concatenate([attn_both, last_out], axis=0))
            side.append(attn_sum)
        up_whole = gate(up_whole, blocks + side)
        side.append(up_whole)
        for c in chunks:
            grads[c], got, sums = k.norm_back(
                mods, grads[c], blocks[c], save["x1"][c], (depth, 4), save["branch"][c], (depth, 2), side
            )
            sums2.append(sums)
            grad_out.append(plan.exchange(got))
        up_both = plan.scatter_weights(up_whole)
        down_sum, _ = plan.sum_levels(down_both)
        side = [down_sum]
        if not first:
            attn_grads[depth + 1] = plan.join_sides(attn_sum)
            side.append(attn_grads[depth + 1])
        grad_heads = None
        for c in chunks:
            grad_heads = k.project_back(grad_out[c], *w_out[depth], c, grad_heads, side)
        side = []
        if not depth:
            rights = [(save["heads"], lambda kind, c=c: (c,)) for c in chunks]
            out_whole = k.weight_grad("out_grad", grad_out, rights, 1, 2, 0, None, [grad_heads])
            out_both = plan.scatter_weights(out_whole[..., :features])
            side = [out_whole]
        grad_qkv = k.attend_back(save["joint"], mask, grad_heads, side)
        up_sum, _ = plan.sum_levels(up_both)
        if first:
            last_blocks = [plan.exchange(gate(part, [grad_heads])) for part in parts]
            down_grads[depth] = plan.join_sides(down_sum)
            side = [up_sum, down_grads[depth]] + last_blocks
        else:
            down_grads[depth] = plan.join_sides(down_sum)
            side = [up_sum, down_grads[depth]]
        rights = [(grad_qkv, lambda kind, c=c: (kind, c)) for c in chunks]
        attn_whole = k.weight_grad("qkv_grad", save["h1"], rights, 3, 6, 0, None, [] if first else side)
        if not depth:
            side.append(attn_whole)
        for c in chunks:
            blocks[c] = plan.exchange(k.qkv_back(grad_qkv, w_qkv[depth], c, side))
        side = []
        if first:
            image_rows = []
            for c in chunks:
                x2, down = k.norm_in(mods, save["x1"][c], last_blocks[c], (depth, 5))
                image_rows.append(x2)
                save["down"].append(down)
            image_rows = jnp.concatenate(image_rows, axis=0)
            side.append(image_rows)
        if depth:
            rights = [(save["heads"], lambda kind, c=c: (c,)) for c in chunks]
            out_whole = k.weight_grad("out_grad", grad_out, rights, 1, 2, 0, None)
            attn_whole = gate(attn_whole, blocks + side + [out_whole])
            side.append(attn_whole)
            out_both = plan.scatter_weights(gate(out_whole, [attn_whole])[..., :features])
        else:
            out_sum, _ = plan.sum_levels(out_both)
            side.append(out_sum)
        attn_both = plan.scatter_weights(attn_whole[..., :features])
        for c in chunks:
            if depth:
                grads[c], got, sums = k.norm_back(
                    mods, grads[c], blocks[c], save["x"][c], (depth, 1), kept[depth - 1]["down"][c], (depth - 1, 5), side
                )
                next_down.append(plan.exchange(got))
            else:
                grads[c], sums = k.norm_back(mods, grads[c], blocks[c], save["x"][c], (depth, 1), after=side)
            sums1.append(sums)
        last_out = out_both
        if first:
            gate2 = []
            for c in chunks:
                moved = start[c] * save["down"][c]
                sums = jnp.stack([jnp.sum(moved[: k.ci], axis=0), jnp.sum(moved[k.ci :], axis=0)])
                gate2.append(jnp.broadcast_to(sums[:, None], (2, 3, D)))
        first_, second, gates = sum(sums1), sum(sums2), sum(gate2)
        mod_grads[depth] = jnp.stack(
            [first_[:, 0], first_[:, 1], second[:, 2], second[:, 0], second[:, 1], gates[:, 2]], axis=1
        )
        gate2, grad_down = sums1, next_down
    up_grads[0] = plan.join_sides(up_sum)
    attn_sum, _ = plan.sum_levels(attn_both)
    attn_grads[0] = plan.join_sides(jnp.concatenate([attn_sum, out_sum], axis=0))
    mod_part = plan.natural(jnp.stack(mod_grads)).reshape(LAYERS, 2, 6, cols, features)
    mod_part = jnp.transpose(mod_part, (3, 1, 0, 2, 4)).reshape(cols, -1)
    grads = jnp.concatenate(grads, axis=0)
    if fast is None:
        mod_all = plan.vectors_rows_back(plan.vectors_cols_back(mod_part)).astype(BF16)
        cut = plan.rows_home_again(grads, fast)
    else:
        cut, more = plan.rows_home_again(grads, fast, mod_part.reshape(cols, -1, features))
        mod_all = plan.vectors_near(gate(more.reshape(2, -1).astype(BF16), [attn_sum]))
    grad_image, grad_text = from_blocks(cut)
    mod_all = mod_all.reshape(rows_count, 2, LAYERS * 6, features)
    mod_cut = [unsort_vectors(mod_all[:, s], 6) for s in range(2)]
    grad_mod = [tn(cond_mine, cut) for cut in mod_cut]
    cond_part = nt(mod_cut[0], mod_image) + nt(mod_cut[1], mod_text)
    cond_part = jnp.broadcast_to(cond_part[:, None], (rows_count, cols, width_rows)).reshape(-1, width_rows)
    cond_sum = lax.all_to_all(cond_part, ("row", "col"), 0, 0, tiled=True)
    cond_sum = jnp.sum(cond_sum.reshape(rows_count, cols, width_rows), axis=1)
    _, silu_pull = jax.vjp(jax.nn.silu, cond_float)
    grad_cond = silu_pull(cond_sum.reshape(1, D))[0]

    grad_qkv_w = [
        merge_columns([[attn_grads[d][2 * kind + s] for kind in range(3)] for d in range(LAYERS)], 3)
        for s in range(2)
    ]
    grad_out_w = [merge_columns([[attn_grads[d][6 + s]] for d in range(LAYERS)], 1) for s in range(2)]
    layered = [
        jnp.stack([grads_[d][s].astype(F32) for d in range(LAYERS)]) for grads_ in (up_grads, down_grads) for s in range(2)
    ]
    return (
        image_out,
        text_out,
        grad_image.astype(F32),
        grad_text.astype(F32),
        grad_cond,
        grad_mod[0],
        grad_mod[1],
        grad_qkv_w[0],
        grad_qkv_w[1],
        grad_out_w[0],
        grad_out_w[1],
        layered[0],
        layered[1],
        layered[2],
        layered[3],
    )


def solution(mesh):
    flat = P("row", "col")
    layered = P(None, "row", "col")
    return jax.shard_map(
        functools.partial(on_device, mesh.shape["row"], mesh.shape["col"]),
        mesh=mesh,
        in_specs=(flat, flat, P("row", None)) + (flat,) * 6 + (layered,) * 4 + (flat, flat),
        out_specs=(flat,) * 4 + (P("row", None),) + (flat,) * 6 + (layered,) * 4,
        check_vma=False,
    )
```

```python
import functools
import math

import jax
import jax.numpy as jnp
from jax import lax
from jax.experimental import pallas as pl
from jax.experimental.pallas import tpu as pltpu
from jax.sharding import PartitionSpec as P

D = 1536
HEAD = 64
IMG_LEN = 1024
TXT_LEN = 154
LAYERS = 2
EPS = 1e-06
CHUNKS = 1
F32 = jnp.float32
BF16 = jnp.bfloat16


def dot(a, b, ca, cb):
    return lax.dot_general(a, b, (((ca,), (cb,)), ((), ())), preferred_element_type=F32)


def nn(a, b):
    return dot(a, b, 1, 0)


def nt(a, b):
    return dot(a, b, 1, 1)


def tn(a, b):
    return dot(a, b, 0, 0)


class Plan:
    def __init__(self, rows, cols, swap):
        self.rows, self.cols, self.swap = rows, cols, swap
        half = cols // 2
        self.row, self.col = lax.axis_index("row"), lax.axis_index("col")
        self.a, self.x, self.k = self.row // 4, (self.row // 2) % 2, self.row % 2
        self.h, self.l = self.col // half, self.col % half
        self.member = self.x * half + self.l if swap else self.col

        def flat(a, x, k, h, l):
            return (a * 4 + x * 2 + k) * cols + h * half + l

        if swap:
            sides = [(a, k) for a in range(rows // 4) for k in range(2)]
            self.team = [
                [flat(a, x, k, h, l) for x in range(2) for l in range(half)] for a, k in sides for h in range(2)
            ]
            self.plane = [
                [flat(a, x, k, h, l) for x in range(2) for h in range(2) for l in range(half)] for a, k in sides
            ]
            self.home = [(flat(a, x, k, 1 - x, l), flat(a, x, k, x, l)) for a, k in sides for x in range(2) for l in range(half)]
            self.across = [(r, r ^ 2) for r in range(rows)]
            self.levels = [(c, (c + half) % cols) for c in range(cols)]
            self.fetch = [[a * 4 + x * 2 + k for a, k in sides] for x in range(2)]

    def exchange(self, blocks):
        if self.swap:
            return lax.all_to_all(
                blocks, ("row", "col"), 0, 0, tiled=True, axis_index_groups=self.team
            )
        return lax.all_to_all(blocks, "col", 0, 0, tiled=True)


    def inner(self, natural):
        if not self.swap:
            return natural
        lead = natural.shape[:-1]
        cut = natural.reshape(lead + (self.rows // 4, 2, 2, D // self.rows))
        return jnp.swapaxes(cut, -3, -2).reshape(lead + (D,))

    natural = inner

    def pick(self, index, pair):
        return jnp.where(index == 0, pair[0], pair[1]), jnp.where(index == 0, pair[1], pair[0])

    def place(self, index, mine, other):
        return jnp.where(index == 0, mine, other), jnp.where(index == 0, other, mine)

    def swap_sides(self, pieces, after=()):
        mine = jnp.stack(pieces)
        if not self.swap:
            return mine
        wide = mine.shape[2] // 2
        mine, other = self.pick(self.x, [mine[:, :, :wide], mine[:, :, wide:]])
        if len(after):
            other = gate(other, after)
        return jnp.concatenate(self.place(self.x, mine, lax.ppermute(other, "row", self.across)), axis=1)

    def swap_levels(self, both, after=()):
        if not self.swap:
            return both
        h = tick(self.h, after) if len(after) else self.h
        return jnp.concatenate(self.place(h, both, lax.ppermute(both, "col", self.levels)), axis=2)

    def gather_weights(self, both):
        if not self.swap:
            return lax.all_gather(both, "row", axis=0)
        return lax.all_gather(both, "row", axis=0, axis_index_groups=self.fetch)

    def scatter_weights(self, whole):
        groups = self.fetch if self.swap else None
        return lax.psum_scatter(whole, "row", scatter_dimension=0, tiled=True, axis_index_groups=groups)[0]

    def sum_levels(self, both):
        if not self.swap:
            return both, both
        wide = both.shape[2] // 2
        mine, other = self.pick(self.h, [both[:, :, :wide], both[:, :, wide:]])
        return (mine.astype(F32) + lax.ppermute(other, "col", self.levels).astype(F32)).astype(BF16), other

    def join_sides(self, both):
        if not self.swap:
            return both
        rows = both.shape[1] // 2
        mine, other = self.pick(self.x, [both[:, :rows], both[:, rows:]])
        return jnp.concatenate(self.place(self.x, mine, lax.ppermute(other, "row", self.across)), axis=2)

    def rows_home(self, blocks):
        if not self.swap:
            return blocks
        moved = lax.ppermute(blocks, ("row", "col"), self.home)
        return jnp.stack(self.place(self.h, blocks, moved), axis=1)

    def rows_in(self, pair, kernels, after=()):
        got = self.exchange(pair)
        if self.swap and kernels is not None:
            return got, kernels.enter(self, got.reshape((2, 2) + got.shape[1:]), (1, 0), after)
        if not self.swap:
            return got, jnp.transpose(got, (1, 0, 2)).reshape(got.shape[1], D)
        got = got.reshape((2, self.cols // 2) + got.shape[1:])
        got = jnp.where(self.h == 0, got[0], got[1])
        return got, self.inner(jnp.transpose(got, (2, 1, 0, 3)).reshape(got.shape[2], D))

    def rows_over(self, blocks, kernels):
        if not self.swap or kernels is None:
            return self.rows_in(self.rows_home(blocks), kernels)[1]
        cut = blocks.reshape((2, 1, self.cols // 2) + blocks.shape[1:])
        cut = jnp.broadcast_to(cut, (2, 2) + cut.shape[2:]).reshape((2 * self.cols,) + blocks.shape[1:])
        got = lax.all_to_all(cut, ("row", "col"), 0, 0, tiled=True, axis_index_groups=self.plane)
        return kernels.enter(self, got.reshape((2, 2, self.cols // 2) + blocks.shape[1:]), (0, 1))

    def rows_home_again(self, own, kernels, extra=None, second=()):
        if not self.swap or kernels is None:
            return self.rows_back(self.rows_out(own, kernels))
        cut = kernels.leave(own)
        tokens = cut.shape[2]
        if extra is not None:
            more = jnp.broadcast_to(extra.astype(BF16)[None], (2,) + extra.shape)
            cut = jnp.concatenate([cut, more], axis=2)
        cut = cut.reshape((2 * self.cols,) + cut.shape[2:])
        got = lax.all_to_all(cut, ("row", "col"), 0, 0, tiled=True, axis_index_groups=self.plane)
        got = got.reshape((2, 2, self.cols // 2) + got.shape[1:])
        x = tick(self.x, second) if len(second) else self.x
        rows = jnp.where(x == 0, got[:, 0, :, :tokens], got[:, 1, :, :tokens])
        rows = rows.reshape((self.cols,) + rows.shape[2:])
        if extra is None:
            return rows
        return rows, jnp.sum(got[:, :, :, tokens:].astype(F32), axis=(0, 2))

    def vectors_near(self, mine):
        every = jnp.broadcast_to(mine[None], (self.rows // 2,) + mine.shape)
        every = lax.all_to_all(every, "row", 0, 0, tiled=True, axis_index_groups=self.fetch)
        every = every.reshape((self.rows // 4, 2) + mine.shape)
        return jnp.swapaxes(every, 1, 2).reshape(self.rows, -1)

    def rows_out(self, own, kernels):
        tokens, own = own.shape[0], own.astype(BF16)
        if not self.swap:
            return self.exchange(jnp.transpose(own.reshape(tokens, self.cols, -1), (1, 0, 2)))
        cut = self.natural(own).reshape(tokens, 2, self.cols // 2, D // self.cols)
        cut = jnp.transpose(cut, (2, 1, 0, 3))
        return self.exchange(jnp.concatenate([cut, cut], axis=0))

    def rows_back(self, got):
        if not self.swap:
            return got
        mine, other = self.pick(self.h, [got[:, 0], got[:, 1]])
        back = lax.ppermute(other, ("row", "col"), [(b, a) for a, b in self.home])
        return jnp.where(self.x == self.h, mine, back)

    def vectors_rows(self, part):
        if not self.swap:
            return jnp.sum(lax.all_to_all(part, "row", 0, 0, tiled=True), axis=0, keepdims=True)
        cut = part.reshape(self.rows // 4, 1, 2, 2, -1)
        cut = jnp.broadcast_to(cut, (self.rows // 4, 2) + cut.shape[2:])
        sent = jnp.transpose(cut, (0, 1, 3, 2, 4)).reshape(self.rows, 2, -1)
        return jnp.sum(lax.all_to_all(sent, "row", 0, 0, tiled=True), axis=0)

    def vectors_cols(self, mine):
        if not self.swap:
            return lax.all_to_all(jnp.broadcast_to(mine, (self.cols, mine.shape[1])), "col", 0, 0, tiled=True)
        half = self.cols // 2
        sent = jnp.broadcast_to(mine[:, None], (2, half, mine.shape[1])).reshape(self.cols, -1)
        return lax.all_to_all(sent, "col", 0, 0, tiled=True)

    def vectors_cols_back(self, part):
        got = lax.all_to_all(part, "col", 0, 0, tiled=True)
        if not self.swap:
            return jnp.sum(got, axis=0, keepdims=True)
        return jnp.sum(got.reshape(2, self.cols // 2, -1), axis=1)

    def vectors_rows_back(self, mine):
        every = lax.all_to_all(jnp.broadcast_to(mine[None], (self.rows,) + mine.shape), "row", 0, 0, tiled=True)
        if not self.swap:
            return every.reshape(self.rows, -1)
        every = jnp.sum(every.reshape(self.rows // 4, 2, 2, 2, -1), axis=1)
        return jnp.transpose(every, (0, 2, 1, 3)).reshape(self.rows, -1)

def norm(x):
    average = jnp.mean(x, axis=1, keepdims=True)
    centred = x - average
    inverse = lax.rsqrt(jnp.mean(centred * centred, axis=1, keepdims=True) + EPS)
    return centred * inverse, inverse


def call(kernel, name, grid, ins, outs, flops=0, after=(), alias=None, scratch=(), transcendentals=0, room=58):
    args = [a for a, _, _ in ins]
    in_specs = [pl.BlockSpec(block, index) for _, block, index in ins]
    extra = list(after)
    aliases = {}
    if alias is not None:
        aliases = {len(args): 0}
        extra = [alias] + extra
    given = len(args)

    def body(*refs):
        kernel(*refs[:given], *refs[given + len(extra) :])

    moved = sum(a.size * a.dtype.itemsize for a in args)
    for shape, dtype, _, _ in outs:
        moved += math.prod(shape) * jnp.dtype(dtype).itemsize
    got = pl.pallas_call(
        body,
        grid=grid,
        in_specs=in_specs + [pl.BlockSpec(memory_space=pl.ANY)] * len(extra),
        out_specs=[pl.BlockSpec(block, index) for _, _, block, index in outs],
        out_shape=[jax.ShapeDtypeStruct(shape, dtype) for shape, dtype, _, _ in outs],
        scratch_shapes=list(scratch),
        input_output_aliases=aliases,
        compiler_params=pltpu.CompilerParams(vmem_limit_bytes=room << 20),
        cost_estimate=pl.CostEstimate(
            flops=flops // 8, bytes_accessed=moved // 8, transcendentals=transcendentals // 8
        ),
        name=name,
    )(*args, *extra)
    return got[0] if len(got) == 1 else got


def tick(index, after):
    def kernel(given, out):
        out[...] = given[...]

    one = jnp.full((8, 128), index, jnp.int32)
    whole = ((8, 128), lambda i: (0, 0))
    return call(kernel, "tick", (1,), [(one,) + whole], [((8, 128), jnp.int32) + whole], after=after)[0, 0]


def gate(array, after):
    def kernel(*refs):
        pass

    return pl.pallas_call(
        kernel,
        in_specs=[pl.BlockSpec(memory_space=pl.ANY)] * (1 + len(after)),
        out_specs=pl.BlockSpec(memory_space=pl.ANY),
        out_shape=jax.ShapeDtypeStruct(array.shape, array.dtype),
        input_output_aliases={0: 0},
        cost_estimate=pl.CostEstimate(flops=0, bytes_accessed=1024, transcendentals=0),
        name="gate",
    )(array, *after)


class Kernels:
    def __init__(self, members, ci, ct, chunks, groups, wide, hidden):
        self.q, self.ci, self.ct, self.rc, self.n = members, ci, ct, ci + ct, chunks
        self.g, self.dr = groups, D // groups
        self.wide, self.hidden = wide, hidden
        self.tokens = members * self.rc * chunks

    def rows(self, array, columns, index, lead=None):
        if lead is None:
            return [(array, (self.q, self.rc, columns), lambda *i: (0, 0, index(*i)))]
        return [(array, (1,) * len(lead(0)) + (self.q, self.rc, columns), lambda *i: lead(*i) + (0, 0, index(*i)))]

    def image(self, ref):
        value = ref[..., : self.ci, :]
        return value.reshape(-1, value.shape[-1])

    def text(self, ref):
        value = ref[..., self.ci :, :]
        return value.reshape(-1, value.shape[-1])

    def weight(self, array, columns, piece, index):
        return [
            (array, (self.g, 1, self.dr, columns), lambda *i, s=s: (0, piece(*i) + s, 0, index(*i))) for s in range(2)
        ]

    def flat(self, ref):
        value = ref[...]
        return value.reshape(-1, value.shape[-1])

    def put(self, ref, img, txt):
        cut = ref.shape[:-2]
        ref[..., : self.ci, :] = img.astype(ref.dtype).reshape(cut + (self.ci, ref.shape[-1]))
        ref[..., self.ci :, :] = txt.astype(ref.dtype).reshape(cut + (self.ct, ref.shape[-1]))

    def qkv(self, h, weights, chunk, joint, after=()):
        def kernel(h, wi, wt, out):
            self.put(out, nn(self.image(h), self.flat(wi)), nn(self.text(h), self.flat(wt)))

        return call(
            kernel,
            "qkv",
            (3,),
            self.rows(h, D, lambda j: 0) + self.weight(weights, self.wide, lambda j: 2 * j, lambda j: 0),
            [
                (
                    (self.n, self.q, self.rc, 3 * self.wide),
                    BF16,
                    (1, self.q, self.rc, self.wide),
                    lambda j: (chunk, 0, 0, j),
                )
            ],
            flops=2 * self.q * self.rc * D * 3 * self.wide,
            alias=joint,
            after=after,
        )

    def project(self, heads, weights, piece, chunk, after=()):
        def kernel(h, wi, wt, out):
            self.put(out, nt(self.image(h), self.flat(wi)), nt(self.text(h), self.flat(wt)))

        return call(
            kernel,
            "project",
            (1,),
            self.rows(heads, self.wide, lambda i: 0, lambda i: (chunk,))
            + self.weight(weights, self.wide, lambda i: piece, lambda i: 0),
            [((self.q, self.rc, D), BF16, (self.q, self.rc, D), lambda i: (0, 0, 0))],
            flops=2 * self.q * self.rc * D * self.wide,
            after=after,
        )

    def project_back(self, grad, weights, piece, chunk, joint, after=()):
        def kernel(h, wi, wt, out):
            self.put(out, nn(self.image(h), self.flat(wi)), nn(self.text(h), self.flat(wt)))

        return call(
            kernel,
            "project_back",
            (1,),
            self.rows(grad, D, lambda i: 0) + self.weight(weights, self.wide, lambda i: piece, lambda i: 0),
            [
                (
                    (self.n, self.q, self.rc, self.wide),
                    BF16,
                    (1, self.q, self.rc, self.wide),
                    lambda i: (chunk, 0, 0, 0),
                )
            ],
            flops=2 * self.q * self.rc * D * self.wide,
            alias=joint,
            after=after,
        )

    def qkv_back(self, grads, weights, chunk, after=()):
        def kernel(h, wi, wt, out, sum_i, sum_t):
            j = pl.program_id(0)
            img, txt = nt(self.image(h), self.flat(wi)), nt(self.text(h), self.flat(wt))

            @pl.when(j == 0)
            def _():
                sum_i[...] = img
                sum_t[...] = txt

            @pl.when(j == 1)
            def _():
                sum_i[...] += img
                sum_t[...] += txt

            @pl.when(j == 2)
            def _():
                self.put(out, sum_i[...] + img, sum_t[...] + txt)

        return call(
            kernel,
            "qkv_back",
            (3,),
            self.rows(grads, self.wide, lambda j: 0, lambda j: (j, chunk))
            + self.weight(weights, self.wide, lambda j: 2 * j, lambda j: 0),
            [((self.q, self.rc, D), BF16, (self.q, self.rc, D), lambda j: (0, 0, 0))],
            flops=2 * self.q * self.rc * D * 3 * self.wide,
            after=after,
            scratch=[pltpu.VMEM((self.q * self.ci, D), F32), pltpu.VMEM((self.q * self.ct, D), F32)],
        )

    def mlp(self, h, ups, downs, after=()):
        steps = 3
        block = self.hidden // steps

        def gelu(v):
            inner = 0.7978845608028654 * (v + 0.044715 * v * v * v)
            t = jnp.tanh(inner)
            half = 0.5 * (1.0 + t)
            slope = half + 0.5 * v * (1.0 - t * t) * (0.7978845608028654 * (1.0 + 3 * 0.044715 * v * v))
            return (v * half).astype(BF16), slope.astype(BF16)

        def kernel(h, ui, ut, di, dt, act, slope, out, sum_i, sum_t):
            j = pl.program_id(0)
            gi, si = gelu(nn(self.image(h), self.flat(ui)))
            gt, st = gelu(nn(self.text(h), self.flat(ut)))
            self.put(act, gi, gt)
            self.put(slope, si, st)
            img, txt = nt(gi, self.flat(di)), nt(gt, self.flat(dt))

            @pl.when(j == 0)
            def _():
                sum_i[...] = img
                sum_t[...] = txt

            @pl.when(jnp.logical_and(j > 0, j < steps - 1))
            def _():
                sum_i[...] += img
                sum_t[...] += txt

            @pl.when(j == steps - 1)
            def _():
                self.put(out, sum_i[...] + img, sum_t[...] + txt)

        return call(
            kernel,
            "mlp",
            (steps,),
            self.rows(h, D, lambda j: 0)
            + self.weight(ups, block, lambda j: 0, lambda j: j)
            + self.weight(downs, block, lambda j: 0, lambda j: j),
            [
                ((self.q, self.rc, self.hidden), BF16, (self.q, self.rc, block), lambda j: (0, 0, j)),
                ((self.q, self.rc, self.hidden), BF16, (self.q, self.rc, block), lambda j: (0, 0, j)),
                ((self.q, self.rc, D), BF16, (self.q, self.rc, D), lambda j: (0, 0, 0)),
            ],
            flops=4 * self.q * self.rc * D * self.hidden,
            transcendentals=self.q * self.rc * self.hidden,
            after=after,
            scratch=[pltpu.VMEM((self.q * self.ci, D), F32), pltpu.VMEM((self.q * self.ct, D), F32)],
        )

    def mlp_back(self, grad, slope, ups, downs, after=()):
        steps = 3
        block = self.hidden // steps

        def kernel(h, s, ui, ut, di, dt, pre, out, sum_i, sum_t):
            j = pl.program_id(0)
            pi = (nn(self.image(h), self.flat(di)) * self.image(s).astype(F32)).astype(BF16)
            pt = (nn(self.text(h), self.flat(dt)) * self.text(s).astype(F32)).astype(BF16)
            self.put(pre, pi, pt)
            img, txt = nt(pi, self.flat(ui)), nt(pt, self.flat(ut))

            @pl.when(j == 0)
            def _():
                sum_i[...] = img
                sum_t[...] = txt

            @pl.when(jnp.logical_and(j > 0, j < steps - 1))
            def _():
                sum_i[...] += img
                sum_t[...] += txt

            @pl.when(j == steps - 1)
            def _():
                self.put(out, sum_i[...] + img, sum_t[...] + txt)

        return call(
            kernel,
            "mlp_back",
            (steps,),
            self.rows(grad, D, lambda j: 0)
            + self.rows(slope, block, lambda j: j)
            + self.weight(ups, block, lambda j: 0, lambda j: j)
            + self.weight(downs, block, lambda j: 0, lambda j: j),
            [
                ((self.q, self.rc, self.hidden), BF16, (self.q, self.rc, block), lambda j: (0, 0, j)),
                ((self.q, self.rc, D), BF16, (self.q, self.rc, D), lambda j: (0, 0, 0)),
            ],
            flops=4 * self.q * self.rc * D * self.hidden,
            after=after,
            scratch=[pltpu.VMEM((self.q * self.ci, D), F32), pltpu.VMEM((self.q * self.ct, D), F32)],
        )

    def weight_grad(self, name, left, right, kinds, pieces, first, whole, after=()):
        columns = right[0][0].shape[-1]

        def rows(refs, side):
            got = [self.text(ref) if side else self.image(ref) for ref in refs]
            return got[0] if len(got) == 1 else jnp.concatenate(got, axis=0)

        if self.dr % 128:
            cut = []
            for kind in range(kinds):
                for side in (slice(0, self.ci), slice(self.ci, self.rc)):
                    a = jnp.concatenate([one[:, side].reshape(-1, D) for one in left], axis=0)
                    b = [one[lead(kind)] if lead else one for one, lead in right]
                    b = jnp.concatenate([one[:, side].reshape(-1, columns) for one in b], axis=0)
                    cut.append(tn(a, b).astype(BF16).reshape(self.g, self.dr, columns))
            cut = jnp.stack(cut, axis=1)
            return cut if whole is None else jnp.concatenate([whole, cut], axis=1)

        def kernel(*refs):
            ins, out = refs[:-1], refs[-1]
            for side in range(2):
                a, b = rows(ins[: self.n], side), rows(ins[self.n :], side)
                out[0, side] = tn(a, b).astype(BF16)

        ins = []
        for one in left:
            ins += self.rows(one, self.dr, lambda j, g: g)
        for one, lead in right:
            ins += self.rows(one, columns, lambda j, g: 0, (lambda j, g=0, lead=lead: lead(j)) if lead else None)
        return call(
            kernel,
            name,
            (kinds, self.g),
            ins,
            [
                (
                    (self.g, pieces, self.dr, columns),
                    BF16,
                    (1, 2, self.dr, columns),
                    lambda j, g: (g, first // 2 + j, 0, 0),
                )
            ],
            flops=2 * self.tokens * D * columns * kinds,
            alias=whole,
            after=after,
        )

    def norm_in(self, mods, x, blocks=None, gate=None, after_norm=None, after=()):
        rows = self.ci // 2

        def kernel(*refs):
            refs = list(refs)
            value = refs.pop(0)[...]
            if blocks is not None:
                added = jnp.sum(refs.pop(0)[...].astype(F32), axis=0)
                value = value + refs.pop(0)[0, gate[1] : gate[1] + 1] * added
            vectors = refs.pop(0) if after_norm is not None else None
            if blocks is not None:
                refs.pop(0)[...] = value
                refs.pop(0)[...] = added
            if after_norm is not None:
                kind = after_norm[1]
                normed = norm(value)[0]
                out = (normed * (1.0 + vectors[0, kind + 1 : kind + 2]) + vectors[0, kind : kind + 1]).astype(BF16)
                refs[0][...] = jnp.broadcast_to(out[None], refs[0].shape)

        ratio = 2

        def vectors(depth):
            return (mods, (1,) + mods.shape[1:], lambda i: (depth * 2 + i // ratio, 0, 0))

        flat = ((rows, D), lambda i: (i, 0))
        many = ((self.q, rows, D), lambda i: (0, i, 0))
        ins, outs = [(x,) + flat], []
        if blocks is not None:
            ins += [(blocks,) + many, vectors(gate[0])]
            outs += [((self.rc, D), F32) + flat] * 2
        if after_norm is not None:
            ins.append(vectors(after_norm[0]))
            outs.append(((self.q, self.rc, D), BF16) + many)
        return call(kernel, "norm_in", (ratio + 1,), ins, outs, flops=20 * self.rc * D, after=after)

    def norm_back(self, mods, grad, blocks=None, x=None, scale=None, branch=None, gate=None, after=()):
        rows, ratio = self.ci // 2, 2

        def kernel(*refs):
            refs = list(refs)
            i = pl.program_id(0)
            held = lax.broadcasted_iota(jnp.int32, (rows, 1), 0) < self.rc - i * rows

            def take():
                return jnp.where(held, refs.pop(0)[...], 0.0)

            value = take()
            rows_of_sums = []
            if blocks is not None:
                dh = jnp.where(held, jnp.sum(refs.pop(0)[...].astype(F32), axis=0), 0.0)
                normed, inverse = norm(take())
                dn = dh * (1.0 + refs.pop(0)[0, scale[1] : scale[1] + 1])
                value = value + inverse * (
                    dn
                    - jnp.mean(dn, axis=1, keepdims=True)
                    - normed * jnp.mean(dn * normed, axis=1, keepdims=True)
                )
                rows_of_sums += [(0, jnp.sum(dh, axis=0, keepdims=True)), (1, jnp.sum(dh * normed, axis=0, keepdims=True))]
            if branch is not None:
                rows_of_sums.append((2, jnp.sum(value * take(), axis=0, keepdims=True)))
            if gate is not None:
                factor = refs.pop(0)[0, gate[1] : gate[1] + 1]
            if blocks is not None:
                refs.pop(0)[...] = value
            if gate is not None:
                out = refs.pop(0)
                out[...] = jnp.broadcast_to((factor * value).astype(BF16)[None], out.shape)
            if not rows_of_sums:
                return
            sums = refs.pop(0)
            start = jnp.logical_or(i == 0, i == ratio)

            @pl.when(start)
            def _():
                for at, row in rows_of_sums:
                    sums[0, at : at + 1] = row

            @pl.when(jnp.logical_not(start))
            def _():
                for at, row in rows_of_sums:
                    sums[0, at : at + 1] += row

        def vectors(depth):
            return (mods, (1,) + mods.shape[1:], lambda i: (depth * 2 + i // ratio, 0, 0))

        flat = ((rows, D), lambda i: (i, 0))
        many = ((self.q, rows, D), lambda i: (0, i, 0))
        ins, outs = [(grad,) + flat], []
        if blocks is not None:
            ins += [(blocks,) + many, (x,) + flat, vectors(scale[0])]
            outs.append(((self.rc, D), F32) + flat)
        if branch is not None:
            ins.append((branch,) + flat)
        if gate is not None:
            ins.append(vectors(gate[0]))
            outs.append(((self.q, self.rc, D), BF16) + many)
        if blocks is not None or branch is not None:
            outs.append(((2, 8, D), F32, (1, 8, D), lambda i: (i // ratio, 0, 0)))
        return call(kernel, "norm_back", (ratio + 1,), ins, outs, flops=30 * self.rc * D, after=after)

    def enter(self, plan, got, order, after=()):
        rows, half = self.ci // 4, D // self.g // 2
        wide = got.shape[-1]

        def kernel(index, ref, out):
            first = index[0:1, 0:1] == 0
            for a in range(2):
                for x in range(2):
                    at = (a, x) if order[0] == 0 else (x, a)
                    piece = jnp.where(first, ref[(0,) + at].astype(F32), ref[(1,) + at].astype(F32))
                    for side in range(2):
                        at = (a * 4 + side * 2 + x) * half
                        out[:, at : at + half] = piece[:, side * half : (side + 1) * half]

        return call(
            kernel,
            "enter",
            (-(-self.rc // rows),),
            [
                (jnp.full((8, 128), plan.h, jnp.int32), (8, 128), lambda i: (0, 0)),
                (got, (2, 2, 2, rows, wide), lambda i: (0, 0, 0, i, 0)),
            ],
            [((self.rc, D), F32, (rows, D), lambda i: (i, 0))],
            flops=self.rc * D,
            after=after,
        )

    def leave(self, own, after=()):
        rows, half = self.ci // 4, D // self.g // 2
        wide = D // self.q

        def kernel(ref, out):
            for a in range(2):
                for x in range(2):
                    at = [(a * 4 + side * 2 + x) * half for side in range(2)]
                    piece = jnp.concatenate([ref[:, i : i + half] for i in at], axis=1).astype(BF16)
                    for side in range(2):
                        out[side, 2 * a + x] = piece

        return call(
            kernel,
            "leave",
            (-(-self.rc // rows),),
            [(own, (rows, D), lambda i: (i, 0))],
            [((2, self.q, self.rc, wide), BF16, (2, self.q, rows, wide), lambda i: (0, 0, i, 0))],
            flops=self.rc * D,
            after=after,
        )

    def masks(self):
        at = lax.broadcasted_iota(jnp.int32, (self.n, self.q, self.rc), 2)
        chunk = lax.broadcasted_iota(jnp.int32, (self.n, self.q, self.rc), 0)
        member = lax.broadcasted_iota(jnp.int32, (self.n, self.q, self.rc), 1)
        text = member * (self.ct * self.n) + chunk * self.ct + at - self.ci
        absent = jnp.logical_and(at >= self.ci, text >= TXT_LEN)
        return jnp.where(absent, -1e30, 0.0).astype(BF16).reshape(self.tokens, 1)

    def attend(self, joint, mask, after=()):
        t, pairs = self.tokens, self.wide // 128

        def kernel(q_ref, k_ref, v_ref, mask_ref, o_ref):
            q, k, v = q_ref[...], k_ref[...], v_ref[...]
            lane = lax.broadcasted_iota(jnp.int32, q.shape, 1)
            first = lane < HEAD
            none = jnp.zeros_like(q)
            bias = jnp.broadcast_to(mask_ref[...], k.shape)
            outs = []
            for side, spare in ((True, HEAD), (False, 0)):
                ones = jnp.where(lane == spare, jnp.ones_like(q), none)
                scaled = jnp.where(first == side, q * jnp.asarray(HEAD**-0.5, BF16), ones)
                scores = nt(scaled, jnp.where(first == side, k, bias))
                weights = jnp.exp(scores - jnp.max(scores, axis=1, keepdims=True))
                totals = jnp.sum(weights, axis=1, keepdims=True)
                outs.append(nn(weights.astype(BF16), v) * (1.0 / totals))
            o_ref[...] = jnp.where(first, outs[0], outs[1]).astype(BF16)

        flat = joint.reshape(t, 3 * self.wide)
        out = call(
            kernel,
            "attend",
            (pairs,),
            [(flat, (t, 128), lambda p, part=part: (0, part * pairs + p)) for part in range(3)]
            + [(mask, (t, 1), lambda p: (0, 0))],
            [((t, self.wide), BF16, (t, 128), lambda p: (0, p))],
            flops=pairs * 8 * t * t * 128,
            transcendentals=pairs * 2 * t * t,
            after=after,
            room=48,
        )
        return out.reshape(self.n, self.q, self.rc, self.wide)

    def attend_back(self, joint, mask, grad, after=()):
        t, pairs = self.tokens, self.wide // 128

        def kernel(q_ref, k_ref, v_ref, mask_ref, do_ref, out_ref):
            q, k, v, do = q_ref[...], k_ref[...], v_ref[...], do_ref[...]
            lane = lax.broadcasted_iota(jnp.int32, q.shape, 1)
            first = lane < HEAD
            none = jnp.zeros_like(q)
            bias = jnp.broadcast_to(mask_ref[...], k.shape)
            scale = jnp.asarray(HEAD**-0.5, BF16)
            dq = dk = dv = None
            for side, spare in ((True, HEAD), (False, 0)):
                mine = first == side
                ones = jnp.where(lane == spare, jnp.ones_like(q), none)
                scaled = q * scale
                grad_o = jnp.where(mine, do, none)
                scores = nt(jnp.where(mine, k, bias), jnp.where(mine, scaled, ones))
                weights = jnp.exp(scores - jnp.max(scores, axis=0, keepdims=True))
                chances = weights * (1.0 / jnp.sum(weights, axis=0, keepdims=True))
                grad_chances = nt(v, grad_o)
                centre = jnp.sum(grad_chances * chances, axis=0, keepdims=True)
                grad_scores = (chances * (grad_chances - centre)).astype(BF16)
                one_v = nn(chances.astype(BF16), grad_o)
                one_k = nn(grad_scores, jnp.where(mine, scaled, none))
                one_q = tn(jnp.where(mine, k * scale, none), grad_scores)
                dq, dk, dv = (one_q, one_k, one_v) if dq is None else (dq + one_q, dk + one_k, dv + one_v)
            out_ref[0] = jnp.transpose(dq).astype(BF16)
            out_ref[1] = dk.astype(BF16)
            out_ref[2] = dv.astype(BF16)

        flat = joint.reshape(t, 3 * self.wide)
        out = call(
            kernel,
            "attend_back",
            (pairs,),
            [(flat, (t, 128), lambda p, part=part: (0, part * pairs + p)) for part in range(3)]
            + [(mask, (t, 1), lambda p: (0, 0)), (grad.reshape(t, self.wide), (t, 128), lambda p: (0, p))],
            [((3, t, self.wide), BF16, (3, t, 128), lambda p: (0, 0, p))],
            flops=pairs * 20 * t * t * 128,
            transcendentals=pairs * 2 * t * t,
            after=after,
            room=56,
        )
        return out.reshape(3, self.n, self.q, self.rc, self.wide)


def order_matrix(block, kinds):
    width = block * LAYERS * kinds
    source = lax.broadcasted_iota(jnp.int32, (width, width), 0)
    target = lax.broadcasted_iota(jnp.int32, (width, width), 1)
    return (source == (target % block) * (LAYERS * kinds) + target // block).astype(BF16)


def split_columns(weight, kinds):
    rows = weight.shape[0]
    features = weight.shape[1] // (LAYERS * kinds)
    block = 128 if features % 128 == 0 else 64
    wide = block * LAYERS * kinds
    matrix = order_matrix(block, kinds)
    parts = [nn(weight[:, i * wide : (i + 1) * wide], matrix).astype(BF16) for i in range(features // block)]

    def one(at):
        return jnp.concatenate([part[:, at * block : (at + 1) * block] for part in parts], axis=1)

    return [[one(depth * kinds + kind) for kind in range(kinds)] for depth in range(LAYERS)]


def merge_columns(pieces, kinds):
    features = pieces[0][0].shape[1]
    block = 128 if features % 128 == 0 else 64
    matrix = order_matrix(block, kinds)
    parts = []
    for i in range(features // block):
        sorted_ = jnp.concatenate(
            [piece[:, i * block : (i + 1) * block] for layer in pieces for piece in layer], axis=1
        )
        parts.append(nt(sorted_, matrix))
    return jnp.concatenate(parts, axis=1)


def sort_vectors(part, kinds):
    rows = part.shape[0]
    features = part.shape[1] // (LAYERS * kinds)
    block = 128 if features % 128 == 0 else 64
    wide = block * LAYERS * kinds
    terms, rest = [], part
    for _ in range(3):
        term = lax.reduce_precision(rest, 8, 7)
        terms.append(term.astype(BF16))
        rest = rest - term
    matrix = order_matrix(block, kinds)
    cuts = jnp.concatenate(terms, axis=0)
    out = []
    for i in range(features // block):
        got = nn(cuts[:, i * wide : (i + 1) * wide], matrix).reshape(3, rows, LAYERS * kinds, block)
        out.append(got[0] + got[1] + got[2])
    return jnp.concatenate(out, axis=2)


def unsort_vectors(sorted_, kinds):
    rows, _, features = sorted_.shape
    block = 128 if features % 128 == 0 else 64
    matrix = order_matrix(block, kinds)
    out = [
        nt(sorted_[:, :, i * block : (i + 1) * block].reshape(rows, -1), matrix).astype(BF16)
        for i in range(features // block)
    ]
    return jnp.concatenate(out, axis=1)


def on_device(
    rows_count,
    cols,
    image_in,
    text_in,
    condition,
    mod_image,
    mod_text,
    qkv_image,
    qkv_text,
    out_image,
    out_text,
    up_image,
    up_text,
    down_image,
    down_text,
    cot_image,
    cot_text,
):
    features = D // cols
    swap = cols % 2 == 0 and rows_count % 4 == 0 and features % (2 * HEAD) == 0
    plan = Plan(rows_count, cols, swap)
    width_rows = mod_image.shape[0]
    img_own = IMG_LEN // cols
    txt_own = -(-TXT_LEN // (16 * cols)) * 16
    txt_pad = txt_own * cols
    wide = features + -features % 128
    k = Kernels(
        cols,
        img_own // CHUNKS,
        txt_own // CHUNKS,
        CHUNKS,
        rows_count // 2 if swap else rows_count,
        wide,
        up_image.shape[2],
    )
    chunks = range(CHUNKS)
    fast = k if swap and rows_count == 8 and cols == 4 and CHUNKS == 1 else None

    def filled(whole):
        return jnp.pad(whole, ((0, 0),) * 3 + ((0, wide - features),))

    qkv_shards = [split_columns(w, 3) for w in (qkv_image, qkv_text)]
    out_shards = [split_columns(w, 1) for w in (out_image, out_text)]
    w_attn, w_up, w_down = [], [], []
    def sides_attn(depth, after=()):
        pieces = [qkv_shards[s][depth][kind] for kind in range(3) for s in range(2)]
        return plan.swap_sides(pieces + [out_shards[s][depth][0] for s in range(2)], after)

    def sides_up(depth, after=()):
        return plan.swap_sides([up_image[depth], up_text[depth]], after)

    def sides_down(depth, after=()):
        return plan.swap_sides([down_image[depth], down_text[depth]], after)

    def to_blocks(image, text):
        img = jnp.transpose(image.reshape(features, IMG_LEN)).reshape(cols, CHUNKS, k.ci, features)
        txt = jnp.pad(jnp.transpose(text.reshape(features, TXT_LEN)), ((0, txt_pad - TXT_LEN), (0, 0)))
        blocks = jnp.concatenate([img, txt.reshape(cols, CHUNKS, k.ct, features)], axis=2)
        return blocks.reshape(cols, CHUNKS * k.rc, features)

    def to_own(own):
        own = own.astype(F32)
        return [own[c * k.rc : (c + 1) * k.rc] for c in chunks]

    def from_blocks(got):
        got = got.reshape(cols, CHUNKS, k.rc, features)
        img = got[:, :, : k.ci].reshape(IMG_LEN, features)
        txt = got[:, :, k.ci :].reshape(txt_pad, features)[:TXT_LEN]
        return jnp.transpose(img).reshape(1, -1), jnp.transpose(txt).reshape(1, -1)

    cond_float = condition.astype(F32)
    cond_low = jax.nn.silu(cond_float).astype(BF16)
    cond_cut = cond_low.reshape(rows_count, width_rows)
    cond_mine = lax.all_to_all(cond_cut, "row", 0, 0, tiled=True)
    mod_part = [nn(cond_mine, one) for one in (mod_image, mod_text)]
    mod_sorted = jnp.concatenate([sort_vectors(one, 6) for one in mod_part], axis=1)
    blocks = to_blocks(image_in, text_in)
    mod_row = plan.vectors_rows(mod_sorted.reshape(rows_count, -1))
    mod_cols = plan.vectors_cols(mod_row).reshape(cols, 2, LAYERS, 6, features)
    mods = plan.inner(jnp.transpose(mod_cols, (2, 1, 3, 0, 4)).reshape(LAYERS * 2, 6, D))

    mask = k.masks()
    own = plan.rows_over(gate(blocks, [mods]), fast)
    attn = sides_attn(0)
    up = sides_up(0, [attn])
    level = plan.swap_levels(attn, [own, up])
    w_qkv, w_out = [filled(plan.gather_weights(level[:6]))], [(filled(plan.gather_weights(level[6:])), 0)]
    x = to_own(own)
    sent = [k.norm_in(mods, x[c], after_norm=(0, 0)) for c in chunks]
    h1 = [plan.exchange(one) for one in sent]
    kept = []
    for depth in range(LAYERS):
        last = depth + 1 == LAYERS
        if not depth:
            down = sides_down(depth, sent)
        side = [plan.swap_levels(gate(up, x), h1 + [down])]
        w_up.append(plan.gather_weights(side[0]))
        joint = None
        for c in chunks:
            joint = k.qkv(h1[c], w_qkv[depth], c, joint, side)
        side = []
        if last:
            side = [k.norm_back(mods, grads[c], gate=(depth, 5)) for c in chunks]
            grad_down = [plan.exchange(one) for one in side]
        heads = k.attend(joint, mask, side)
        side = grad_down if last else []
        save = dict(x=x, h1=h1, joint=joint, heads=heads, branch=[], x1=[], h2=[], act=[], slope=[], down=[])
        next_x, next_h1 = [], []
        sent = [k.project(heads, *w_out[depth], c, side) for c in chunks]
        blocks = [plan.exchange(one) for one in sent]
        other = [] if last else [to_blocks(cot_image, cot_text), sides_attn(depth + 1, sent)]
        side = [plan.swap_levels(gate(down, sent), blocks + other)]
        w_down.append(plan.gather_weights(side[0]))
        sent = []
        for c in chunks:
            x1, branch, h2 = k.norm_in(mods, x[c], blocks[c], (depth, 2), (depth, 3), side)
            sent.append(h2)
            save["x1"].append(x1)
            save["branch"].append(branch)
            save["h2"].append(plan.exchange(h2))
        side = []
        if not last:
            up = sides_up(depth + 1, sent)
            pair = plan.rows_home(gate(other[0], sent))
            side = [up, pair]
        parts = []
        for c in chunks:
            act, slope, part = k.mlp(save["h2"][c], w_up[depth], w_down[depth], side)
            parts.append(part)
            save["act"].append(act)
            save["slope"].append(slope)
        kept.append(save)
        if last:
            break
        got, grads = plan.rows_in(gate(pair, save["h2"] + [up]), fast, save["act"])
        grads = to_own(grads)
        blocks = [plan.exchange(gate(part, [got])) for part in parts]
        down = sides_down(depth + 1, save["act"])
        side = [plan.swap_levels(gate(other[1], save["act"]), blocks + [down, *grads])]
        whole = filled(plan.gather_weights(side[0]))
        w_qkv.append(whole)
        w_out.append((whole, 6))
        sent = []
        for c in chunks:
            got = k.norm_in(mods, save["x1"][c], blocks[c], (depth, 5), (depth + 1, 0), side)
            next_x.append(got[0])
            save["down"].append(got[1])
            sent.append(got[2])
            next_h1.append(plan.exchange(got[2]))
        x, h1 = next_x, next_h1

    start = list(grads)
    mod_grads = [None] * LAYERS
    attn_grads, up_grads, down_grads = [None] * LAYERS, [None] * LAYERS, [None] * LAYERS
    for depth in reversed(range(LAYERS)):
        first = depth + 1 == LAYERS
        save = kept[depth]
        grad_pre, blocks, grad_out, sums2, sums1, next_down = ([] for _ in range(6))
        side = []
        if not first:
            up_grads[depth + 1] = plan.join_sides(up_sum)
            side = [up_grads[depth + 1]]
        if not first:
            image_cut = plan.rows_home_again(gate(image_rows, grad_down), fast)
            image_out, text_out = from_blocks(image_cut)
        down_whole = k.weight_grad("down_grad", grad_down, [(one, None) for one in save["act"]], 1, 2, 0, None, side)
        down_both = plan.scatter_weights(down_whole)
        for c in chunks:
            pre, part = k.mlp_back(grad_down[c], save["slope"][c], w_up[depth], w_down[depth], [down_whole])
            grad_pre.append(pre)
            blocks.append(plan.exchange(part if first else gate(part, [image_cut])))
        up_whole = k.weight_grad("up_grad", save["h2"], [(one, None) for one in grad_pre], 1, 2, 0, None)
        side = []
        if not first:
            attn_sum, _ = plan.sum_levels(jnp.concatenate([attn_both, last_out], axis=0))
            side.append(attn_sum)
        up_whole = gate(up_whole, blocks + side)
        side.append(up_whole)
        for c in chunks:
            grads[c], got, sums = k.norm_back(
                mods, grads[c], blocks[c], save["x1"][c], (depth, 4), save["branch"][c], (depth, 2), side
            )
            sums2.append(sums)
            grad_out.append(plan.exchange(got))
        up_both = plan.scatter_weights(up_whole)
        down_sum, _ = plan.sum_levels(down_both)
        side = [down_sum]
        if not first:
            attn_grads[depth + 1] = plan.join_sides(attn_sum)
            side.append(attn_grads[depth + 1])
        grad_heads = None
        for c in chunks:
            grad_heads = k.project_back(grad_out[c], *w_out[depth], c, grad_heads, side)
        side = []
        if not depth:
            rights = [(save["heads"], lambda kind, c=c: (c,)) for c in chunks]
            out_whole = k.weight_grad("out_grad", grad_out, rights, 1, 2, 0, None, [grad_heads])
            out_both = plan.scatter_weights(out_whole[..., :features])
            side = [out_whole]
        grad_qkv = k.attend_back(save["joint"], mask, grad_heads, side)
        up_sum, _ = plan.sum_levels(up_both)
        if first:
            last_blocks = [plan.exchange(gate(part, [grad_heads])) for part in parts]
            down_grads[depth] = plan.join_sides(down_sum)
            side = [up_sum, down_grads[depth]] + last_blocks
        else:
            down_grads[depth] = plan.join_sides(down_sum)
            side = [up_sum, down_grads[depth]]
        rights = [(grad_qkv, lambda kind, c=c: (kind, c)) for c in chunks]
        attn_whole = k.weight_grad("qkv_grad", save["h1"], rights, 3, 6, 0, None, [] if first else side)
        if not depth:
            side.append(attn_whole)
        for c in chunks:
            blocks[c] = plan.exchange(k.qkv_back(grad_qkv, w_qkv[depth], c, side))
        side = []
        if first:
            image_rows = []
            for c in chunks:
                x2, down = k.norm_in(mods, save["x1"][c], last_blocks[c], (depth, 5))
                image_rows.append(x2)
                save["down"].append(down)
            image_rows = jnp.concatenate(image_rows, axis=0)
            side.append(image_rows)
        if depth:
            rights = [(save["heads"], lambda kind, c=c: (c,)) for c in chunks]
            out_whole = k.weight_grad("out_grad", grad_out, rights, 1, 2, 0, None)
            attn_whole = gate(attn_whole, blocks + side + [out_whole])
            side.append(attn_whole)
            out_both = plan.scatter_weights(gate(out_whole, [attn_whole])[..., :features])
        else:
            out_sum, _ = plan.sum_levels(out_both)
            side.append(out_sum)
        attn_both = plan.scatter_weights(attn_whole[..., :features])
        for c in chunks:
            if depth:
                grads[c], got, sums = k.norm_back(
                    mods, grads[c], blocks[c], save["x"][c], (depth, 1), kept[depth - 1]["down"][c], (depth - 1, 5), side
                )
                next_down.append(plan.exchange(got))
            else:
                grads[c], sums = k.norm_back(mods, grads[c], blocks[c], save["x"][c], (depth, 1), after=side)
            sums1.append(sums)
        last_out = out_both
        if first:
            gate2 = []
            for c in chunks:
                moved = start[c] * save["down"][c]
                sums = jnp.stack([jnp.sum(moved[: k.ci], axis=0), jnp.sum(moved[k.ci :], axis=0)])
                gate2.append(jnp.broadcast_to(sums[:, None], (2, 3, D)))
        first_, second, gates = sum(sums1), sum(sums2), sum(gate2)
        mod_grads[depth] = jnp.stack(
            [first_[:, 0], first_[:, 1], second[:, 2], second[:, 0], second[:, 1], gates[:, 2]], axis=1
        )
        gate2, grad_down = sums1, next_down
    up_grads[0] = plan.join_sides(up_sum)
    attn_sum, _ = plan.sum_levels(attn_both)
    attn_grads[0] = plan.join_sides(jnp.concatenate([attn_sum, out_sum], axis=0))
    mod_part = plan.natural(jnp.stack(mod_grads)).reshape(LAYERS, 2, 6, cols, features)
    mod_part = jnp.transpose(mod_part, (3, 1, 0, 2, 4)).reshape(cols, -1)
    grads = jnp.concatenate(grads, axis=0)
    if fast is None:
        mod_all = plan.vectors_rows_back(plan.vectors_cols_back(mod_part)).astype(BF16)
        cut = plan.rows_home_again(grads, fast)
    else:
        cut, more = plan.rows_home_again(grads, fast, mod_part.reshape(cols, -1, features))
        mod_all = plan.vectors_near(gate(more.reshape(2, -1).astype(BF16), [attn_sum]))
    grad_image, grad_text = from_blocks(cut)
    mod_all = mod_all.reshape(rows_count, 2, LAYERS * 6, features)
    mod_cut = [unsort_vectors(mod_all[:, s], 6) for s in range(2)]
    grad_mod = [tn(cond_mine, cut) for cut in mod_cut]
    cond_part = nt(mod_cut[0], mod_image) + nt(mod_cut[1], mod_text)
    cond_part = jnp.broadcast_to(cond_part[:, None], (rows_count, cols, width_rows)).reshape(-1, width_rows)
    cond_sum = lax.all_to_all(cond_part, ("row", "col"), 0, 0, tiled=True)
    cond_sum = jnp.sum(cond_sum.reshape(rows_count, cols, width_rows), axis=1)
    _, silu_pull = jax.vjp(jax.nn.silu, cond_float)
    grad_cond = silu_pull(cond_sum.reshape(1, D))[0]

    grad_qkv_w = [
        merge_columns([[attn_grads[d][2 * kind + s] for kind in range(3)] for d in range(LAYERS)], 3)
        for s in range(2)
    ]
    grad_out_w = [merge_columns([[attn_grads[d][6 + s]] for d in range(LAYERS)], 1) for s in range(2)]
    layered = [
        jnp.stack([grads_[d][s].astype(F32) for d in range(LAYERS)]) for grads_ in (up_grads, down_grads) for s in range(2)
    ]
    return (
        image_out,
        text_out,
        grad_image.astype(F32),
        grad_text.astype(F32),
        grad_cond,
        grad_mod[0],
        grad_mod[1],
        grad_qkv_w[0],
        grad_qkv_w[1],
        grad_out_w[0],
        grad_out_w[1],
        layered[0],
        layered[1],
        layered[2],
        layered[3],
    )


def solution(mesh):
    flat = P("row", "col")
    layered = P(None, "row", "col")
    return jax.shard_map(
        functools.partial(on_device, mesh.shape["row"], mesh.shape["col"]),
        mesh=mesh,
        in_specs=(flat, flat, P("row", None)) + (flat,) * 6 + (layered,) * 4 + (flat, flat),
        out_specs=(flat,) * 4 + (P("row", None),) + (flat,) * 6 + (layered,) * 4,
        check_vma=False,
    )
```
